32 devices in a mesh: parts: 2 (over y), dp: 4 (over z), layer: 4 (over x, core).
Axes of the slice: x: 2, y: 2, z: 4, core: 2. Of those that a mesh axis runs over, the one named last changes fastest.
Arguments:
- acts: bfloat16 [4, 2560, 2560], P('layer', ('parts', 'dp')), parts along dimension 1, may hold values from -6 to 6
- grads: bfloat16 [4, 2560, 2560], P('layer', ('parts', 'dp')), parts along dimension 1, may hold values from -6 to 6
- basis_in: bfloat16 [4, 2560, 2560], P('layer', None, 'dp'), may hold values from -0.125 to 0.125
- output_eigen_basis: bfloat16 [4, 2560, 2560], P('layer', None, 'dp'), may hold values from -0.125 to 0.125
- query_in: bfloat16 [4, 2560, 384], P('layer', 'dp'), may hold values from -0.125 to 0.125
- query_out: bfloat16 [4, 2560, 384], P('layer', 'dp'), may hold values from -0.125 to 0.125
- doc_counts: int32 [8, 8], P(('parts', 'dp')), parts along dimension 0, may hold values from 1 to 80, 320 in all within a row
- pair_query: int32 [1024], P(('parts', 'dp')), parts along dimension 0, may hold values from 0 to 11
- pair_device: int32 [1024, 1], P(('parts', 'dp')), parts along dimension 0, may hold values from 0 to 3; in each aligned block of 128 rows (0 to 127, 128 to 255, ...) at most 32 rows name the same one
- pair_doc: int32 [1024], P(('parts', 'dp')), parts along dimension 0, may hold values from 0 to 7
Outputs:
- token_scores: float32 [12, 2560], P(None, ('parts', 'dp')), parts along dimension 1
- pair_scores: float32 [1024], P(('parts', 'dp')), parts along dimension 0
The draws below stay inside these ranges and needn't reach their ends.
There are 2 independent parts, one for each index of `parts`. The reference program is written for one: setup_inputs(seed, part) draws one part's arguments, and reference() takes and returns one part's arrays. A program takes and returns all parts, laid end to end along the dimension named above; an argument that names none is the same for every part. Nothing has to cross between parts.
Inputs may be any that keep to these rules, and one draw needn't show every extreme that they name: `pair_device`: among the 128 pairs of one data device at most 32 name one data device, and some data device is named exactly 32 times. `doc_counts`: each row sums to 320.
All inputs are finite; a program needn't handle non-finite values.
Results may differ from the reference program's by a relative error of at most 0.015.
Values may be sent and summed in bfloat16 or wider, within the bound.
No kernel may reach another device: no remote copies, remote signals or barrier semaphores. Data moves between devices by JAX's collectives and lax.ppermute only.
A program may use at most 64 MiB of HBM per device.

```python
import math
import jax
import jax.numpy as jnp
import numpy as np
from jax import lax

D = 2560
RANK = 32
QUERIES = 12
TOKENS_PER_SHARD = 320
DOC_DEV = 8
PAIR_DEV = 128
EIG_BLK = 640
LAYERS = 4
TOKENS = 1280
PAIRS = 512
PAIR_CAP = 32
DOC_MAX = 80
N_DP = 4


def with_ends(result, own_key, smallest, high):
    spot = [jax.random.randint(jax.random.fold_in(own_key, axis), (), 0, length) for axis, length in enumerate(result.shape)]
    main_axis = result.shape.index(max(result.shape))
    beside = spot[:main_axis] + [(spot[main_axis] + 1) % result.shape[main_axis]] + spot[main_axis + 1:]
    return result.at[tuple(spot)].set(smallest).at[tuple(beside)].set(high)


def level_of(stream_key, shape, cuts, low, top_value):
    loudness, own = 1.0, jax.random.fold_in(stream_key, 6)
    for axis_at, parts in cuts:
        draws = jnp.exp(jax.random.uniform(jax.random.fold_in(own, axis_at), (parts,), jnp.float32, low / len(cuts), top_value / len(cuts)))
        loudness = loudness * jnp.repeat(draws, shape[axis_at] // parts).reshape([-1 if axis == axis_at else 1 for axis in range(len(shape))])
    return loudness


def profile(number_of, total, bound, skew):
    weights = [(1 << 20) // math.isqrt(standing ** skew) + 1 for standing in range(2, number_of + 1)]
    surplus, holding = total - bound - (number_of - 1), [1] * (number_of - 1)
    while surplus > 0:
        movable = [i for i in range(number_of - 1) if holding[i] < bound]
        whole, left = sum([weights[i] for i in movable]), surplus
        for i in movable:
            more = min(bound - holding[i], max(1, left * weights[i] // whole), surplus)
            holding[i] = holding[i] + more
            surplus = surplus - more
    return np.array([bound] + holding)


def uneven_parts(rng, amount, total, bound, slope):
    if amount == 2:
        one = jax.random.randint(rng, (), max(1, total - bound), min(bound, total - 1) + 1)
        return jnp.stack([one, total - one])
    sizes = jnp.asarray(profile(amount, total, bound, slope), jnp.int32)
    twos = (amount - 1) // 2
    giver, receiver = sizes[1:1 + 2 * twos:2], sizes[2:2 + 2 * twos:2]
    slack = jnp.minimum(giver - 1, bound - receiver)
    moved = jax.random.randint(jax.random.fold_in(rng, 1), (twos,), 0, 1 << 20) % (slack + 1)
    sizes = sizes.at[1:1 + 2 * twos:2].set(giver - moved).at[2:2 + 2 * twos:2].set(receiver + moved)
    return sizes[jax.random.permutation(jax.random.fold_in(rng, 2), amount)]


def assign_block(own_key, own, number, rows, count, top, reach, skew):
    ranking = jax.random.permutation(own_key, count)
    crowded, usual = portions_of(count, rows * top, reach, skew, True), portions_of(count, rows * top, reach, skew, False)
    places = jnp.arange(count)

    def named(lengths, rotation):
        used = int((lengths > 0).sum())
        fixed = max(1, used // 4)
        moved = fixed + (places - fixed + rotation * (used - fixed)) % max(1, count - fixed)
        return jnp.zeros((count,), jnp.int32).at[ranking[jnp.where(places < fixed, places, moved)]].set(jnp.asarray(lengths, jnp.int32))

    lengths = jnp.where(number % 4 == 0, named(crowded, number // 4), named(usual, number - number // 4 - 1))
    mixed = jax.random.permutation(jax.random.fold_in(own, 3), count)
    giver, sink = mixed[0:count // 2 * 2:2], mixed[1:count // 2 * 2:2]
    room = jnp.minimum(lengths[giver] - 1, reach - lengths[sink]) // 2
    room = jnp.where((giver == ranking[0]) | (sink == ranking[0]) | (lengths[sink] == 0), 0, jnp.maximum(room, 0))
    moved = jax.random.randint(jax.random.fold_in(own, 4), (count // 2,), 0, 1 << 20) % (room + 1)
    lengths = lengths.at[giver].add(-moved).at[sink].add(moved)
    items = jnp.searchsorted(jnp.cumsum(lengths), jnp.arange(rows * top), side="right").astype(jnp.int32)
    grid = items.reshape(top, rows).T
    grid = grid[jax.random.permutation(jax.random.fold_in(own, 1), rows)]
    rotation = jax.random.randint(jax.random.fold_in(own, 2), (rows, 1), 0, top)
    return jnp.take_along_axis(grid, (jnp.arange(top)[None, :] + rotation) % top, axis=1)


def portions_of(count, total, limit, slope, full):
    portions = [(1 << 20) // math.isqrt(rank ** slope) + 1 for rank in range(1, count + 1)]
    largest = limit if full else min(limit, max(-(-total // count), total * portions[0] // sum(portions)))
    least = 1 if total - largest >= count - 1 else 0
    counts, rest = [largest] + [least] * (count - 1), total - largest - least * (count - 1)
    while rest > 0:
        candidates = [i for i in range(1, count) if counts[i] < largest] or [i for i in range(1, count) if counts[i] < limit]
        pool, left = sum([portions[i] for i in candidates]), rest
        for i in candidates:
            more = min(limit - counts[i], max(1, left * portions[i] // pool), rest)
            counts[i] = counts[i] + more
            rest = rest - more
    return np.array(counts)


def noise(rng, dims, scale, bound, shards=(), kind=jnp.bfloat16):
    array = scale * jax.random.normal(rng, dims, jnp.float32)
    if shards:
        array = array * level_of(rng, dims, shards, -0.22, 0.18)
    return jnp.clip(array, -bound, bound).astype(kind)


def setup_inputs(seed: int = 0, part: int = 0) -> dict:
    key_list = jax.random.split(jax.random.key(seed), 11)
    part_splits = jax.random.split(jax.random.fold_in(key_list[10], part), 11)
    acts = noise(part_splits[0], (LAYERS, TOKENS, D), 1.0, 6.0, ((0, 4), (1, 4)))
    grads = noise(part_splits[1], (LAYERS, TOKENS, D), 1.0, 6.0, ((0, 4), (1, 4)))
    basis_in = noise(key_list[2], (LAYERS, D, D), D ** -0.5, 0.125, ((0, 4), (2, 4)))
    output_eigen_basis = noise(key_list[3], (LAYERS, D, D), D ** -0.5, 0.125, ((0, 4), (2, 4)))
    query_in = noise(key_list[4], (LAYERS, D, QUERIES * RANK), D ** -0.5, 0.125, ((0, 4), (1, 4)))
    query_out = noise(key_list[5], (LAYERS, D, QUERIES * RANK), D ** -0.5, 0.125, ((0, 4), (1, 4)))
    doc_counts = jax.vmap(lambda own: uneven_parts(own, DOC_DEV, TOKENS_PER_SHARD, DOC_MAX, 2))(jax.random.split(part_splits[6], N_DP)).reshape((N_DP, DOC_DEV)).astype(jnp.int32)
    pair_query = with_ends(jax.random.randint(part_splits[7], (PAIRS,), 0, QUERIES), jax.random.fold_in(part_splits[7], 1), 0, QUERIES - 1).astype(jnp.int32)
    pair_device_keys = jax.random.split(jax.random.fold_in(part_splits[8], 1), PAIRS // PAIR_DEV)
    pair_device_turns = jax.random.permutation(jax.random.fold_in(part_splits[8], 3), PAIRS // PAIR_DEV)
    pair_device = jax.vmap(lambda own, number: assign_block(jax.random.fold_in(part_splits[8], 2), own, number, PAIR_DEV, N_DP, 1, PAIR_CAP, 2))(pair_device_keys, pair_device_turns).reshape((PAIRS, 1))
    pair_doc = with_ends(jax.random.randint(part_splits[9], (PAIRS,), 0, DOC_DEV), jax.random.fold_in(part_splits[9], 1), 0, DOC_DEV - 1).astype(jnp.int32)
    return dict(acts=acts, grads=grads, basis_in=basis_in, output_eigen_basis=output_eigen_basis, query_in=query_in, query_out=query_out, doc_counts=doc_counts, pair_query=pair_query, pair_device=pair_device, pair_doc=pair_doc)


def pull_back(basis, factors):
    spread = QUERIES * RANK
    block_list = basis.reshape(D, N_DP, EIG_BLK).transpose(1, 0, 2)
    rows = factors.reshape(N_DP, EIG_BLK, spread)

    def step(total, group_member):
        part = jnp.dot(group_member[0], group_member[1], preferred_element_type=jnp.float32)
        part = lax.optimization_barrier(part.astype(jnp.bfloat16))
        return (total + part.astype(jnp.float32), None)
    total, _ = lax.scan(step, jnp.zeros((D, spread), jnp.float32), (block_list, rows))
    return total.astype(jnp.bfloat16)

def reference(acts, grads, basis_in, output_eigen_basis, query_in, query_out, doc_counts, pair_query, pair_device, pair_doc):
    total = jnp.zeros((QUERIES, TOKENS), jnp.float32)
    for level in range(LAYERS):
        pulled_in = pull_back(basis_in[level], query_in[level])
        pulled_out = pull_back(output_eigen_basis[level], query_out[level])
        proj_in = jnp.dot(acts[level], pulled_in, preferred_element_type=jnp.float32)
        proj_out = jnp.dot(grads[level], pulled_out, preferred_element_type=jnp.float32)
        scores = lax.optimization_barrier(jnp.sum((proj_in * proj_out).reshape(TOKENS, QUERIES, RANK), axis=2)) * RANK ** (-0.5)
        total = total + scores.T
    ends = jnp.cumsum(doc_counts, axis=1).astype(jnp.int32)
    starts = ends - doc_counts
    position = jnp.arange(TOKENS_PER_SHARD, dtype=jnp.int32)
    group_member = ((position[None, None, :] >= starts[:, :, None]) & (position[None, None, :] < ends[:, :, None])).astype(jnp.float32)
    block_list = total.reshape(QUERIES, N_DP, TOKENS_PER_SHARD)
    pooled_scores = jnp.einsum('szx,zkx->zsk', block_list, group_member, precision=lax.Precision.HIGHEST)
    pooled_scores = pooled_scores / jnp.sqrt(doc_counts.astype(jnp.float32))[:, None, :]
    pair_scores = pooled_scores[pair_device[:, 0], pair_query, pair_doc]
    return (total, pair_scores)
```

```python
import functools

import jax
import jax.numpy as jnp
from jax import lax
from jax.experimental import pallas as pl
from jax.experimental.pallas import tpu as pltpu
from jax.sharding import PartitionSpec as P

RANK = 32
NT = (((1,), (1,)), ((), ()))


def pull_kernel(side_ref, basis_in_ref, basis_out_ref, query_in_ref, query_out_ref, out_ref):
    def go(basis_ref, query_ref):
        out_ref[...] = lax.dot_general(
            query_ref[...], basis_ref[...], (((0,), (1,)), ((), ())), preferred_element_type=jnp.float32
        ).astype(out_ref.dtype)

    @pl.when(side_ref[0] == 0)
    def _():
        go(basis_in_ref, query_in_ref)

    @pl.when(side_ref[0] != 0)
    def _():
        go(basis_out_ref, query_out_ref)


def pull(side, basis_in, basis_out, query_in, query_out):
    rows, depth = basis_in.shape
    spread = query_in.shape[1]
    block = 512 if rows % 512 == 0 else rows
    return pl.pallas_call(
        pull_kernel,
        out_shape=jax.ShapeDtypeStruct((spread, rows), jnp.bfloat16),
        grid_spec=pltpu.PrefetchScalarGridSpec(
            num_scalar_prefetch=1,
            grid=(rows // block,),
            in_specs=[
                pl.BlockSpec((block, depth), lambda i, s: (jnp.where(s[0] == 0, i, 0), 0)),
                pl.BlockSpec((block, depth), lambda i, s: (jnp.where(s[0] == 0, 0, i), 0)),
                pl.BlockSpec((depth, spread), lambda i, s: (0, 0)),
                pl.BlockSpec((depth, spread), lambda i, s: (0, 0)),
            ],
            out_specs=pl.BlockSpec((spread, block), lambda i, s: (0, i)),
        ),
        compiler_params=pltpu.CompilerParams(vmem_limit_bytes=24 * 1024 * 1024),
    )(side, basis_in, basis_out, query_in, query_out)


def score_kernel(side_ref, own_ref, other_ref, acts_ref, grads_ref, out_ref):
    def go(factor_in_ref, factor_out_ref):
        proj_in = lax.dot_general(factor_in_ref[...], acts_ref[...], NT, preferred_element_type=jnp.float32)
        proj_out = lax.dot_general(factor_out_ref[...], grads_ref[...], NT, preferred_element_type=jnp.float32)
        product = proj_in * proj_out
        queries = product.shape[0] // RANK
        out_ref[...] = jnp.sum(product.reshape(queries, RANK, product.shape[1]), axis=1) * RANK ** (-0.5)

    @pl.when(side_ref[0] == 0)
    def _():
        go(own_ref, other_ref)

    @pl.when(side_ref[0] != 0)
    def _():
        go(other_ref, own_ref)


def score(side, own, other, acts, grads):
    vmem = pl.BlockSpec(memory_space=pltpu.VMEM)
    return pl.pallas_call(
        score_kernel,
        out_shape=jax.ShapeDtypeStruct((own.shape[0] // RANK, acts.shape[0]), jnp.float32),
        in_specs=[pl.BlockSpec(memory_space=pltpu.SMEM), vmem, vmem, vmem, vmem],
        out_specs=vmem,
        compiler_params=pltpu.CompilerParams(vmem_limit_bytes=24 * 1024 * 1024),
    )(side, own, other, acts, grads)


def choose(at, options):
    picked = options[-1]
    for i in range(len(options) - 2, -1, -1):
        picked = jnp.where(at == i, options[i], picked)
    return picked


def sum_over_layers(value, layers):
    if layers & (layers - 1):
        return lax.psum(value, "layer")
    terms = [value] + [
        lax.ppermute(value, "layer", [(i, i ^ k) for i in range(layers)]) for k in range(1, layers)
    ]
    while len(terms) > 1:
        terms = [terms[i] + terms[i + 1] for i in range(0, len(terms), 2)]
    return terms[0]


def per_device(
    acts,
    grads,
    basis_in,
    output_eigen_basis,
    query_in,
    query_out,
    doc_counts,
    pair_query,
    pair_device,
    pair_doc,
):
    n = lax.axis_size("dp")
    layers = lax.axis_size("layer")
    side = lax.axis_index("parts")
    z = lax.axis_index("dp")
    side_array = side.astype(jnp.int32).reshape(1)
    tokens, features = acts.shape[1:]
    spread = query_in.shape[2]
    queries = spread // RANK
    chunks = queries
    width = spread // chunks

    own = pull(side_array, basis_in[0], output_eigen_basis[0], query_in[0], query_out[0])
    own = own.reshape(chunks, width, features)

    def own_chunk(c):
        return lax.dynamic_index_in_dim(own, jnp.clip(c, 0, chunks - 1), 0, keepdims=False)

    def add(a, b):
        return (a.astype(jnp.float32) + b.astype(jnp.float32)).astype(jnp.bfloat16)

    from_left, from_right, totals, swapped = [], [], [], []
    swap = [(0, 1), (1, 0)]
    group_ends = [4, 8, 11, 12] if chunks == 12 else [chunks]
    pieces, done = [], 0
    for step in range(chunks + n - 2):
        send_right, send_left = own_chunk(step - z), own_chunk(step - (n - 1 - z))
        if step:
            send_right, send_left = add(send_right, from_left[-1]), add(send_left, from_right[-1])
        from_left.append(
            lax.ppermute(send_right, "dp", [(i, i + 1) for i in range(n - 1) if 0 <= step - i < chunks])
        )
        from_right.append(
            lax.ppermute(send_left, "dp", [(n - 1 - i, n - 2 - i) for i in range(n - 1) if 0 <= step - i < chunks])
        )
        c = step - (n - 2)
        if c >= 0:
            zero = jnp.zeros((width, features), jnp.bfloat16)
            before = choose(z, [zero] + from_left[c : c + n - 1])
            after = choose(n - 1 - z, [zero] + from_right[c : c + n - 1])
            total = (
                own[c].astype(jnp.float32) + before.astype(jnp.float32) + after.astype(jnp.float32)
            ).astype(jnp.bfloat16)
            totals.append(total)
            swapped.append(lax.ppermute(total, "parts", swap))
            if c + 1 in group_ends:
                mine = jnp.concatenate(totals[done : c + 1], axis=0)
                theirs = jnp.concatenate(swapped[done : c + 1], axis=0)
                pieces.append(score(side_array, mine, theirs, acts[0], grads[0]))
                done = c + 1

    token_scores = sum_over_layers(jnp.concatenate(pieces, axis=0), layers)

    counts = doc_counts[0]
    ends = jnp.cumsum(counts)
    starts = ends - counts
    position = jnp.arange(tokens, dtype=jnp.int32)
    group_member = (
        (position[None, :] >= starts[:, None]) & (position[None, :] < ends[:, None])
    ).astype(jnp.float32)
    pooled = jnp.dot(token_scores, group_member.T, precision=lax.Precision.HIGHEST)
    pooled = pooled / jnp.sqrt(counts.astype(jnp.float32))[None, :]
    docs = counts.shape[0]
    cells = queries * docs
    flat = pooled.reshape(1, cells)
    target = pair_device[:, 0]
    cell = pair_query * docs + pair_doc
    if n <= 8:
        table = jnp.concatenate(
            [flat]
            + [lax.ppermute(flat, "dp", [(i, (i + k) % n) for i in range(n)]) for k in range(1, n)],
            axis=1,
        )
        column = lax.rem(z - target + n, n) * cells + cell
    else:
        table = lax.all_gather(flat, "dp", axis=1, tiled=True)
        column = target * cells + cell
    hit = column[:, None] == jnp.arange(n * cells, dtype=jnp.int32)[None, :]
    pair_scores = jnp.sum(jnp.where(hit, table, 0.0), axis=1)
    return (token_scores, pair_scores)


def solution(mesh):
    in_specs = (
        P("layer", ("parts", "dp"), None),
        P("layer", ("parts", "dp"), None),
        P("layer", None, "dp"),
        P("layer", None, "dp"),
        P("layer", "dp", None),
        P("layer", "dp", None),
        P(("parts", "dp"), None),
        P(("parts", "dp")),
        P(("parts", "dp"), None),
        P(("parts", "dp")),
    )
    out_specs = (P(None, ("parts", "dp")), P(("parts", "dp")))
    return jax.shard_map(
        per_device, mesh=mesh, in_specs=in_specs, out_specs=out_specs, check_vma=False
    )
```

```python
import functools

import jax
import jax.numpy as jnp
from jax import lax
from jax.experimental import pallas as pl
from jax.experimental.pallas import tpu as pltpu
from jax.sharding import PartitionSpec as P

RANK = 32
PULL_VMEM = 123 * 512 * 1024
NT = (((1,), (1,)), ((), ()))


def pull_kernel(widths, side_ref, basis_in_ref, basis_out_ref, query_in_ref, query_out_ref, *rest):
    outs, (basis, query, turned, sems) = rest[: len(widths)], rest[len(widths) :]
    blocks, block = basis.shape[:2]

    def copies(basis_ref, query_ref):
        return [pltpu.make_async_copy(query_ref, query, sems.at[blocks])] + [
            pltpu.make_async_copy(basis_ref.at[pl.ds(i * block, block)], basis.at[i], sems.at[i])
            for i in range(blocks)
        ]

    @pl.when(side_ref[0] == 0)
    def _():
        for copy in copies(basis_in_ref, query_in_ref):
            copy.start()

    @pl.when(side_ref[0] != 0)
    def _():
        for copy in copies(basis_out_ref, query_out_ref):
            copy.start()

    landed = copies(basis_in_ref, query_in_ref)
    landed[0].wait()
    turned[...] = query[...].T
    for i in range(blocks):
        landed[1 + i].wait()
        pulled = lax.dot_general(turned[...], basis[i], NT, preferred_element_type=jnp.float32).astype(jnp.bfloat16)
        first = 0
        for out, width in zip(outs, widths):
            out[:, i * block : (i + 1) * block] = pulled[first : first + width]
            first += width


def pull(side, basis_in, basis_out, query_in, query_out, widths):
    rows, depth = basis_in.shape
    spread = query_in.shape[1]
    block = 512 if rows % 512 == 0 else rows
    blocks = rows // block
    hbm = pl.BlockSpec(memory_space=pltpu.HBM)
    return pl.pallas_call(
        functools.partial(pull_kernel, widths),
        out_shape=[jax.ShapeDtypeStruct((width, rows), jnp.bfloat16) for width in widths],
        in_specs=[pl.BlockSpec(memory_space=pltpu.SMEM)] + [hbm] * 4,
        out_specs=[pl.BlockSpec(memory_space=pltpu.VMEM)] * len(widths),
        scratch_shapes=[
            pltpu.VMEM((blocks, block, depth), jnp.bfloat16),
            pltpu.VMEM((depth, spread), jnp.bfloat16),
            pltpu.VMEM((spread, depth), jnp.bfloat16),
            pltpu.SemaphoreType.DMA((blocks + 1,)),
        ],
        compiler_params=pltpu.CompilerParams(vmem_limit_bytes=PULL_VMEM),
    )(side, basis_in, basis_out, query_in, query_out)


def total_kernel(mine_ref, came_ref, *rest):
    mine = mine_ref[...].astype(jnp.float32) + came_ref[...].astype(jnp.float32)
    rest[-1][...] = mine.astype(jnp.bfloat16)
    if len(rest) == 4:
        rest[2][...] = rest[1][...]


def total(after, mine, came, later=None):
    extra = [] if later is None else [later]
    vmem = pl.BlockSpec(memory_space=pltpu.VMEM)
    out = pl.pallas_call(
        total_kernel,
        out_shape=[jax.ShapeDtypeStruct(a.shape, a.dtype) for a in extra + [mine]],
        in_specs=[vmem] * 2 + [pl.BlockSpec(memory_space=pl.ANY)] + [vmem] * len(extra),
        out_specs=[vmem] * (1 + len(extra)),
        compiler_params=pltpu.CompilerParams(vmem_limit_bytes=8 * 1024 * 1024),
    )(mine, came, after, *extra)
    return out[-1], (out[0] if extra else None)


def take_kernel(flag_ref, mine_ref, came_ref, after_ref, out_ref):
    @pl.when(flag_ref[0] != 0)
    def _():
        out_ref[...] = came_ref[...]

    @pl.when(flag_ref[0] == 0)
    def _():
        out_ref[...] = mine_ref[...]


def take(after, flag, mine, came):
    vmem = pl.BlockSpec(memory_space=pltpu.VMEM)
    return pl.pallas_call(
        take_kernel,
        out_shape=jax.ShapeDtypeStruct(mine.shape, mine.dtype),
        in_specs=[pl.BlockSpec(memory_space=pltpu.SMEM), vmem, vmem, pl.BlockSpec(memory_space=pl.ANY)],
        out_specs=vmem,
        compiler_params=pltpu.CompilerParams(vmem_limit_bytes=8 * 1024 * 1024),
    )(flag, mine, came, after)


def score_kernel(side_ref, own_ref, other_ref, acts_ref, grads_ref, after_ref, out_ref):
    def go(factor_in_ref, factor_out_ref):
        proj_in = lax.dot_general(factor_in_ref[...], acts_ref[...], NT, preferred_element_type=jnp.float32)
        proj_out = lax.dot_general(factor_out_ref[...], grads_ref[...], NT, preferred_element_type=jnp.float32)
        product = proj_in * proj_out
        queries = product.shape[0] // RANK
        out_ref[...] = jnp.sum(product.reshape(queries, RANK, product.shape[1]), axis=1) * RANK ** (-0.5)

    @pl.when(side_ref[0] == 0)
    def _():
        go(own_ref, other_ref)

    @pl.when(side_ref[0] != 0)
    def _():
        go(other_ref, own_ref)


def score(after, side, own, other, acts, grads):
    vmem = pl.BlockSpec(memory_space=pltpu.VMEM)
    return pl.pallas_call(
        score_kernel,
        out_shape=jax.ShapeDtypeStruct((own.shape[0] // RANK, acts.shape[0]), jnp.float32),
        in_specs=[pl.BlockSpec(memory_space=pltpu.SMEM), vmem, vmem, vmem, vmem, pl.BlockSpec(memory_space=pl.ANY)],
        out_specs=vmem,
        compiler_params=pltpu.CompilerParams(vmem_limit_bytes=24 * 1024 * 1024),
    )(side, own, other, acts, grads, after)


def chunk_queries(queries):
    if queries < 4:
        return [1] * queries
    inner = queries - 2
    return [1] + [2] * (inner // 2) + [1] * (inner % 2) + [1]


def sum_over_layers(value, layers):
    if layers & (layers - 1):
        return lax.psum(value, "layer")
    terms = [value] + [
        lax.ppermute(value, "layer", [(i, i ^ k) for i in range(layers)]) for k in range(1, layers)
    ]
    while len(terms) > 1:
        terms = [terms[i] + terms[i + 1] for i in range(0, len(terms), 2)]
    return terms[0]


def per_device(
    acts,
    grads,
    basis_in,
    output_eigen_basis,
    query_in,
    query_out,
    doc_counts,
    pair_query,
    pair_device,
    pair_doc,
):
    n = lax.axis_size("dp")
    layers = lax.axis_size("layer")
    side = lax.axis_index("parts")
    z = lax.axis_index("dp")
    side_array = side.astype(jnp.int32).reshape(1)
    tokens, features = acts.shape[1:]
    spread = query_in.shape[2]
    queries = spread // RANK
    half = n // 2
    widths = [RANK * k for k in chunk_queries(queries)]
    chunks = len(widths)

    own = pull(side_array, basis_in[0], output_eigen_basis[0], query_in[0], query_out[0], widths)
    depth = jnp.minimum(z, n - 1 - z)
    at_hop = [(depth == hop).astype(jnp.int32).reshape(1) for hop in range(half - 1)]

    stages = [("in", hop) for hop in range(half - 1)] + [("mid", 0)]
    stages += [("out", hop) for hop in range(half - 2, -1, -1)] + [("swap", 0)]

    def transfer(kind, hop, value):
        if kind == "in":
            return lax.ppermute(value, "dp", [(hop, hop + 1), (n - 1 - hop, n - 2 - hop)])
        if kind == "mid":
            return lax.ppermute(value, "dp", [(half - 1, half), (half, half - 1)])
        if kind == "out":
            return lax.ppermute(value, "dp", [(hop + 1, hop), (n - 2 - hop, n - 1 - hop)])
        return lax.ppermute(value, "parts", [(0, 1), (1, 0)])

    part, came = list(own), [None] * chunks
    ahead = min(2, chunks)
    for c in range(ahead):
        came[c] = transfer(*stages[0], part[c])
    after = own[0]
    pieces = []
    for turn in range(chunks + len(stages) - 1):
        for s, (kind, hop) in enumerate(stages):
            c = turn - s
            if not 0 <= c < chunks:
                continue
            if kind == "swap":
                pieces.append(score(after, side_array, part[c], came[c], acts[0], grads[0]))
                after = pieces[-1]
                continue
            if kind == "out":
                part[c] = take(after, at_hop[hop], part[c], came[c])
            else:
                later = c + ahead if s == 0 and c + ahead < chunks else None
                part[c], moved = total(after, part[c], came[c], None if later is None else own[later])
                if later is not None:
                    came[later] = transfer(*stages[0], moved)
            after = part[c]
            came[c] = transfer(*stages[s + 1], part[c])

    token_scores = sum_over_layers(jnp.concatenate(pieces, axis=0), layers)

    counts = doc_counts[0]
    ends = jnp.cumsum(counts)
    starts = ends - counts
    position = jnp.arange(tokens, dtype=jnp.int32)
    group_member = (
        (position[None, :] >= starts[:, None]) & (position[None, :] < ends[:, None])
    ).astype(jnp.float32)
    pooled = jnp.dot(token_scores, group_member.T, precision=lax.Precision.HIGHEST)
    pooled = pooled / jnp.sqrt(counts.astype(jnp.float32))[None, :]
    docs = counts.shape[0]
    cells = queries * docs
    flat = pooled.reshape(1, cells)
    target = pair_device[:, 0]
    cell = pair_query * docs + pair_doc
    if n <= 8:
        table = jnp.concatenate(
            [flat]
            + [lax.ppermute(flat, "dp", [(i, (i + k) % n) for i in range(n)]) for k in range(1, n)],
            axis=1,
        )
        column = lax.rem(z - target + n, n) * cells + cell
    else:
        table = lax.all_gather(flat, "dp", axis=1, tiled=True)
        column = target * cells + cell
    hit = column[:, None] == jnp.arange(n * cells, dtype=jnp.int32)[None, :]
    pair_scores = jnp.sum(jnp.where(hit, table, 0.0), axis=1)
    return (token_scores, pair_scores)


def solution(mesh):
    in_specs = (
        P("layer", ("parts", "dp"), None),
        P("layer", ("parts", "dp"), None),
        P("layer", None, "dp"),
        P("layer", None, "dp"),
        P("layer", "dp", None),
        P("layer", "dp", None),
        P(("parts", "dp"), None),
        P(("parts", "dp")),
        P(("parts", "dp"), None),
        P(("parts", "dp")),
    )
    out_specs = (P(None, ("parts", "dp")), P(("parts", "dp")))
    return jax.shard_map(
        per_device, mesh=mesh, in_specs=in_specs, out_specs=out_specs, check_vma=False
    )
```

```python
import functools

import jax
import jax.numpy as jnp
from jax import lax
from jax.experimental import pallas as pl
from jax.experimental.pallas import tpu as pltpu
from jax.sharding import PartitionSpec as P

RANK = 32
NT = (((1,), (1,)), ((), ()))


def first_pull_kernel(side_ref, basis_in_ref, basis_out_ref, query_in_ref, query_out_ref, out_ref, basis_ref, query_ref, turned_ref, sems):
    rows = out_ref.shape[0]

    def copies(from_basis, from_query):
        return [
            pltpu.make_async_copy(from_query, query_ref, sems.at[0]),
            pltpu.make_async_copy(from_basis, basis_ref, sems.at[1]),
        ]

    @pl.when(side_ref[0] == 0)
    def _():
        for copy in copies(basis_in_ref, query_in_ref):
            copy.start()

    @pl.when(side_ref[0] != 0)
    def _():
        for copy in copies(basis_out_ref, query_out_ref):
            copy.start()

    landed = copies(basis_in_ref, query_in_ref)
    landed[0].wait()
    turned_ref[...] = query_ref[...].T
    landed[1].wait()
    out_ref[...] = lax.dot_general(
        turned_ref[:rows], basis_ref[...], NT, preferred_element_type=jnp.float32
    ).astype(jnp.bfloat16)


def first_pull(side, basis_in, basis_out, query_in, query_out, rows):
    features, depth = basis_in.shape
    spread = query_in.shape[1]
    hbm = [pltpu.with_memory_space_constraint(a, pltpu.HBM) for a in (basis_in, basis_out, query_in, query_out)]
    vmem = pl.BlockSpec(memory_space=pltpu.VMEM)
    bf16 = functools.partial(jax.ShapeDtypeStruct, dtype=jnp.bfloat16)
    out, basis, _, turned = pl.pallas_call(
        first_pull_kernel,
        out_shape=[bf16((rows, features)), bf16((features, depth)), bf16((depth, spread)), bf16((spread, depth))],
        in_specs=[pl.BlockSpec(memory_space=pltpu.SMEM)] + [pl.BlockSpec(memory_space=pltpu.HBM)] * 4,
        out_specs=[vmem] * 4,
        scratch_shapes=[pltpu.SemaphoreType.DMA((2,))],
        compiler_params=pltpu.CompilerParams(vmem_limit_bytes=16 * 1024 * 1024),
    )(side, *hbm)
    return out, basis, turned


def pull_kernel(turned_ref, basis_ref, after_ref, *outs):
    rows, features = outs[0].shape
    block = 512 if features % 512 == 0 else features
    for i in range(features // block):
        pulled = lax.dot_general(
            turned_ref[rows:], basis_ref[i * block : (i + 1) * block], NT, preferred_element_type=jnp.float32
        ).astype(jnp.bfloat16)
        for c, out in enumerate(outs):
            out[:, i * block : (i + 1) * block] = pulled[c * rows : (c + 1) * rows]


def pull(after, turned, basis, rows):
    vmem = pl.BlockSpec(memory_space=pltpu.VMEM)
    chunks = turned.shape[0] // rows - 1
    return pl.pallas_call(
        pull_kernel,
        out_shape=[jax.ShapeDtypeStruct((rows, basis.shape[0]), jnp.bfloat16)] * chunks,
        in_specs=[vmem, vmem, pl.BlockSpec(memory_space=pl.ANY)],
        out_specs=[vmem] * chunks,
        compiler_params=pltpu.CompilerParams(vmem_limit_bytes=16 * 1024 * 1024),
    )(turned, basis, after)


def total_kernel(mine_ref, came_ref, *rest):
    mine = mine_ref[...].astype(jnp.float32) + came_ref[...].astype(jnp.float32)
    rest[-1][...] = mine.astype(jnp.bfloat16)
    if len(rest) == 4:
        rest[2][...] = rest[1][...]


def total(after, mine, came, later=None):
    extra = [] if later is None else [later]
    vmem = pl.BlockSpec(memory_space=pltpu.VMEM)
    out = pl.pallas_call(
        total_kernel,
        out_shape=[jax.ShapeDtypeStruct(a.shape, a.dtype) for a in extra + [mine]],
        in_specs=[vmem] * 2 + [pl.BlockSpec(memory_space=pl.ANY)] + [vmem] * len(extra),
        out_specs=[vmem] * (1 + len(extra)),
        compiler_params=pltpu.CompilerParams(vmem_limit_bytes=8 * 1024 * 1024),
    )(mine, came, after, *extra)
    return out[-1], (out[0] if extra else None)


def take_kernel(flag_ref, mine_ref, came_ref, after_ref, out_ref):
    @pl.when(flag_ref[0] != 0)
    def _():
        out_ref[...] = came_ref[...]

    @pl.when(flag_ref[0] == 0)
    def _():
        out_ref[...] = mine_ref[...]


def take(after, flag, mine, came):
    vmem = pl.BlockSpec(memory_space=pltpu.VMEM)
    return pl.pallas_call(
        take_kernel,
        out_shape=jax.ShapeDtypeStruct(mine.shape, mine.dtype),
        in_specs=[pl.BlockSpec(memory_space=pltpu.SMEM), vmem, vmem, pl.BlockSpec(memory_space=pl.ANY)],
        out_specs=vmem,
        compiler_params=pltpu.CompilerParams(vmem_limit_bytes=8 * 1024 * 1024),
    )(flag, mine, came, after)


def score_kernel(count, side_ref, acts_ref, grads_ref, after_ref, *rest):
    own, other, out_ref = rest[:count], rest[count : 2 * count], rest[-1]

    def go(factors_in, factors_out):
        factor_in = jnp.concatenate([ref[...] for ref in factors_in], axis=0)
        factor_out = jnp.concatenate([ref[...] for ref in factors_out], axis=0)
        proj_in = lax.dot_general(factor_in, acts_ref[...], NT, preferred_element_type=jnp.float32)
        proj_out = lax.dot_general(factor_out, grads_ref[...], NT, preferred_element_type=jnp.float32)
        product = proj_in * proj_out
        queries = product.shape[0] // RANK
        out_ref[...] = jnp.sum(product.reshape(queries, RANK, product.shape[1]), axis=1) * RANK ** (-0.5)

    @pl.when(side_ref[0] == 0)
    def _():
        go(own, other)

    @pl.when(side_ref[0] != 0)
    def _():
        go(other, own)


def score(after, side, own, other, acts, grads):
    vmem = pl.BlockSpec(memory_space=pltpu.VMEM)
    rows = sum(chunk.shape[0] for chunk in own)
    return pl.pallas_call(
        functools.partial(score_kernel, len(own)),
        out_shape=jax.ShapeDtypeStruct((rows // RANK, acts.shape[0]), jnp.float32),
        in_specs=[pl.BlockSpec(memory_space=pltpu.SMEM), vmem, vmem, pl.BlockSpec(memory_space=pl.ANY)]
        + [vmem] * (2 * len(own)),
        out_specs=vmem,
        compiler_params=pltpu.CompilerParams(vmem_limit_bytes=16 * 1024 * 1024),
    )(side, acts, grads, after, *own, *other)


def chunk_rows(spread):
    for chunks, group in ((8, 2), (12, 1)):
        rows = spread // chunks
        if spread % chunks == 0 and rows % 16 == 0 and rows * group % RANK == 0:
            return rows, group
    return RANK, 1


def sum_over_layers(value, layers):
    if layers & (layers - 1):
        return lax.psum(value, "layer")
    terms = [value] + [
        lax.ppermute(value, "layer", [(i, i ^ k) for i in range(layers)]) for k in range(1, layers)
    ]
    while len(terms) > 1:
        terms = [terms[i] + terms[i + 1] for i in range(0, len(terms), 2)]
    return terms[0]


def per_device(
    acts,
    grads,
    basis_in,
    output_eigen_basis,
    query_in,
    query_out,
    doc_counts,
    pair_query,
    pair_device,
    pair_doc,
):
    n = lax.axis_size("dp")
    layers = lax.axis_size("layer")
    side = lax.axis_index("parts")
    z = lax.axis_index("dp")
    side_array = side.astype(jnp.int32).reshape(1)
    tokens, features = acts.shape[1:]
    spread = query_in.shape[2]
    queries = spread // RANK
    half = n // 2
    rows, group = chunk_rows(spread)
    chunks = spread // rows

    first, basis, turned = first_pull(
        side_array, basis_in[0], output_eigen_basis[0], query_in[0], query_out[0], rows
    )
    own = [first] + list(pull(first, turned, basis, rows))
    depth = jnp.minimum(z, n - 1 - z)
    at_hop = [(depth == hop).astype(jnp.int32).reshape(1) for hop in range(half - 1)]

    stages = [("in", hop) for hop in range(half - 1)] + [("mid", 0)]
    stages += [("out", hop) for hop in range(half - 2, -1, -1)] + [("swap", 0)]

    def transfer(kind, hop, value):
        if kind == "in":
            return lax.ppermute(value, "dp", [(hop, hop + 1), (n - 1 - hop, n - 2 - hop)])
        if kind == "mid":
            return lax.ppermute(value, "dp", [(half - 1, half), (half, half - 1)])
        if kind == "out":
            return lax.ppermute(value, "dp", [(hop + 1, hop), (n - 2 - hop, n - 1 - hop)])
        return lax.ppermute(value, "parts", [(0, 1), (1, 0)])

    part, came = list(own), [None] * chunks
    ahead = min(2, chunks)
    for c in range(ahead):
        came[c] = transfer(*stages[0], part[c])
    after = own[0]
    pieces = []
    for turn in range(chunks + len(stages) - 1):
        for s, (kind, hop) in enumerate(stages):
            c = turn - s
            if not 0 <= c < chunks:
                continue
            if kind == "swap":
                if c % group == group - 1:
                    span = slice(c + 1 - group, c + 1)
                    pieces.append(score(after, side_array, part[span], came[span], acts[0], grads[0]))
                    after = pieces[-1]
                continue
            if kind == "out":
                part[c] = take(after, at_hop[hop], part[c], came[c])
            else:
                later = c + ahead if s == 0 and c + ahead < chunks else None
                part[c], moved = total(after, part[c], came[c], None if later is None else own[later])
                if later is not None:
                    came[later] = transfer(*stages[0], moved)
            after = part[c]
            came[c] = transfer(*stages[s + 1], part[c])

    token_scores = sum_over_layers(jnp.concatenate(pieces, axis=0), layers)

    counts = doc_counts[0]
    ends = jnp.cumsum(counts)
    starts = ends - counts
    position = jnp.arange(tokens, dtype=jnp.int32)
    group_member = (
        (position[None, :] >= starts[:, None]) & (position[None, :] < ends[:, None])
    ).astype(jnp.float32)
    pooled = jnp.dot(token_scores, group_member.T, precision=lax.Precision.HIGHEST)
    pooled = pooled / jnp.sqrt(counts.astype(jnp.float32))[None, :]
    docs = counts.shape[0]
    cells = queries * docs
    flat = pooled.reshape(1, cells)
    target = pair_device[:, 0]
    cell = pair_query * docs + pair_doc
    if n <= 8 and n & (n - 1) == 0:
        table = jnp.concatenate(
            [flat] + [lax.ppermute(flat, "dp", [(i, i ^ k) for i in range(n)]) for k in range(1, n)],
            axis=1,
        )
        column = (z ^ target) * cells + cell
    else:
        table = lax.all_gather(flat, "dp", axis=1, tiled=True)
        column = target * cells + cell
    hit = column[:, None] == jnp.arange(n * cells, dtype=jnp.int32)[None, :]
    pair_scores = jnp.sum(jnp.where(hit, table, 0.0), axis=1)
    return (token_scores, pair_scores)


def solution(mesh):
    in_specs = (
        P("layer", ("parts", "dp"), None),
        P("layer", ("parts", "dp"), None),
        P("layer", None, "dp"),
        P("layer", None, "dp"),
        P("layer", "dp", None),
        P("layer", "dp", None),
        P(("parts", "dp"), None),
        P(("parts", "dp")),
        P(("parts", "dp"), None),
        P(("parts", "dp")),
    )
    out_specs = (P(None, ("parts", "dp")), P(("parts", "dp")))
    return jax.shard_map(
        per_device, mesh=mesh, in_specs=in_specs, out_specs=out_specs, check_vma=False
    )
```

```python
import functools

import jax
import jax.numpy as jnp
from jax import lax
from jax.experimental import pallas as pl
from jax.experimental.pallas import tpu as pltpu
from jax.sharding import PartitionSpec as P

RANK = 32
NT = (((1,), (1,)), ((), ()))


def first_pull_kernel(side_ref, basis_in_ref, basis_out_ref, query_in_ref, query_out_ref, out_ref, basis_ref, query_ref, turned_ref, sems):
    rows = out_ref.shape[0]

    def copies(from_basis, from_query):
        return [
            pltpu.make_async_copy(from_query, query_ref, sems.at[0]),
            pltpu.make_async_copy(from_basis, basis_ref, sems.at[1]),
        ]

    @pl.when(side_ref[0] == 0)
    def _():
        for copy in copies(basis_in_ref, query_in_ref):
            copy.start()

    @pl.when(side_ref[0] != 0)
    def _():
        for copy in copies(basis_out_ref, query_out_ref):
            copy.start()

    landed = copies(basis_in_ref, query_in_ref)
    landed[0].wait()
    turned_ref[...] = query_ref[...].T
    landed[1].wait()
    out_ref[...] = lax.dot_general(
        turned_ref[:rows], basis_ref[...], NT, preferred_element_type=jnp.float32
    ).astype(jnp.bfloat16)


def first_pull(side, basis_in, basis_out, query_in, query_out, rows):
    features, depth = basis_in.shape
    spread = query_in.shape[1]
    hbm = [pltpu.with_memory_space_constraint(a, pltpu.HBM) for a in (basis_in, basis_out, query_in, query_out)]
    vmem = pl.BlockSpec(memory_space=pltpu.VMEM)
    bf16 = functools.partial(jax.ShapeDtypeStruct, dtype=jnp.bfloat16)
    out, basis, _, turned = pl.pallas_call(
        first_pull_kernel,
        out_shape=[bf16((rows, features)), bf16((features, depth)), bf16((depth, spread)), bf16((spread, depth))],
        in_specs=[pl.BlockSpec(memory_space=pltpu.SMEM)] + [pl.BlockSpec(memory_space=pltpu.HBM)] * 4,
        out_specs=[vmem] * 4,
        scratch_shapes=[pltpu.SemaphoreType.DMA((2,))],
        compiler_params=pltpu.CompilerParams(vmem_limit_bytes=16 * 1024 * 1024),
    )(side, *hbm)
    return out, basis, turned


def pull_kernel(turned_ref, basis_ref, after_ref, *outs):
    rows, features = outs[0].shape
    block = 512 if features % 512 == 0 else features
    for i in range(features // block):
        pulled = lax.dot_general(
            turned_ref[rows:], basis_ref[i * block : (i + 1) * block], NT, preferred_element_type=jnp.float32
        ).astype(jnp.bfloat16)
        for c, out in enumerate(outs):
            out[:, i * block : (i + 1) * block] = pulled[c * rows : (c + 1) * rows]


def pull(after, turned, basis, rows):
    vmem = pl.BlockSpec(memory_space=pltpu.VMEM)
    chunks = turned.shape[0] // rows - 1
    return pl.pallas_call(
        pull_kernel,
        out_shape=[jax.ShapeDtypeStruct((rows, basis.shape[0]), jnp.bfloat16)] * chunks,
        in_specs=[vmem, vmem, pl.BlockSpec(memory_space=pl.ANY)],
        out_specs=[vmem] * chunks,
        compiler_params=pltpu.CompilerParams(vmem_limit_bytes=16 * 1024 * 1024),
    )(turned, basis, after)


def score_kernel(factors_ref, acts_ref, grads_ref, out_ref):
    spread = factors_ref.shape[0] // 2
    proj_in = lax.dot_general(factors_ref[:spread], acts_ref[...], NT, preferred_element_type=jnp.float32)
    proj_out = lax.dot_general(factors_ref[spread:], grads_ref[...], NT, preferred_element_type=jnp.float32)
    product = proj_in * proj_out
    queries = product.shape[0] // RANK
    out_ref[...] = jnp.sum(product.reshape(queries, RANK, product.shape[1]), axis=1) * RANK ** (-0.5)


def score(factors, acts, grads):
    vmem = pl.BlockSpec(memory_space=pltpu.VMEM)
    return pl.pallas_call(
        score_kernel,
        out_shape=jax.ShapeDtypeStruct((factors.shape[0] // 2 // RANK, acts.shape[0]), jnp.float32),
        in_specs=[vmem] * 3,
        out_specs=vmem,
        compiler_params=pltpu.CompilerParams(vmem_limit_bytes=24 * 1024 * 1024),
    )(factors, acts, grads)


def sum_over_layers(value, layers):
    if layers & (layers - 1):
        return lax.psum(value, "layer")
    terms = [value] + [
        lax.ppermute(value, "layer", [(i, i ^ k) for i in range(layers)]) for k in range(1, layers)
    ]
    while len(terms) > 1:
        terms = [terms[i] + terms[i + 1] for i in range(0, len(terms), 2)]
    return terms[0]


def per_device(
    acts,
    grads,
    basis_in,
    output_eigen_basis,
    query_in,
    query_out,
    doc_counts,
    pair_query,
    pair_device,
    pair_doc,
):
    n = lax.axis_size("dp")
    layers = lax.axis_size("layer")
    side = lax.axis_index("parts")
    z = lax.axis_index("dp")
    side_array = side.astype(jnp.int32).reshape(1)
    tokens, features = acts.shape[1:]
    spread = query_in.shape[2]
    queries = spread // RANK
    rows = spread // n
    first, basis, turned = first_pull(
        side_array, basis_in[0], output_eigen_basis[0], query_in[0], query_out[0], rows
    )
    own = jnp.concatenate([first] + list(pull(first, turned, basis, rows)), axis=0)
    shard = lax.psum_scatter(own, "dp", scatter_dimension=0, tiled=True)
    whole = lax.all_gather(shard, ("parts", "dp"), axis=0, tiled=True)
    scores = score(whole, acts[0], grads[0])

    token_scores = sum_over_layers(scores, layers)

    counts = doc_counts[0]
    ends = jnp.cumsum(counts)
    starts = ends - counts
    position = jnp.arange(tokens, dtype=jnp.int32)
    group_member = (
        (position[None, :] >= starts[:, None]) & (position[None, :] < ends[:, None])
    ).astype(jnp.float32)
    pooled = jnp.dot(token_scores, group_member.T, precision=lax.Precision.HIGHEST)
    pooled = pooled / jnp.sqrt(counts.astype(jnp.float32))[None, :]
    docs = counts.shape[0]
    cells = queries * docs
    flat = pooled.reshape(1, cells)
    target = pair_device[:, 0]
    cell = pair_query * docs + pair_doc
    if n <= 8 and n & (n - 1) == 0:
        table = jnp.concatenate(
            [flat] + [lax.ppermute(flat, "dp", [(i, i ^ k) for i in range(n)]) for k in range(1, n)],
            axis=1,
        )
        column = (z ^ target) * cells + cell
    else:
        table = lax.all_gather(flat, "dp", axis=1, tiled=True)
        column = target * cells + cell
    hit = column[:, None] == jnp.arange(n * cells, dtype=jnp.int32)[None, :]
    pair_scores = jnp.sum(jnp.where(hit, table, 0.0), axis=1)
    return (token_scores, pair_scores)


def solution(mesh):
    in_specs = (
        P("layer", ("parts", "dp"), None),
        P("layer", ("parts", "dp"), None),
        P("layer", None, "dp"),
        P("layer", None, "dp"),
        P("layer", "dp", None),
        P("layer", "dp", None),
        P(("parts", "dp"), None),
        P(("parts", "dp")),
        P(("parts", "dp"), None),
        P(("parts", "dp")),
    )
    out_specs = (P(None, ("parts", "dp")), P(("parts", "dp")))
    return jax.shard_map(
        per_device, mesh=mesh, in_specs=in_specs, out_specs=out_specs, check_vma=False
    )
```

```python
import functools

import jax
import jax.numpy as jnp
from jax import lax
from jax.experimental import pallas as pl
from jax.experimental.pallas import tpu as pltpu
from jax.sharding import PartitionSpec as P

RANK = 32
NT = (((1,), (1,)), ((), ()))


VMEM = pl.BlockSpec(memory_space=pltpu.VMEM)
HBM = pl.BlockSpec(memory_space=pltpu.HBM)
ANY = pl.BlockSpec(memory_space=pl.ANY)
MIB = 1024 * 1024


def in_hbm(*arrays):
    return [pltpu.with_memory_space_constraint(array, pltpu.HBM) for array in arrays]


def bf16(*shape):
    return jax.ShapeDtypeStruct(shape, jnp.bfloat16)


def first_pull_kernel(basis_in_ref, basis_out_ref, query_in_ref, query_out_ref, out_ref, basis_ref, query_ref, turned_ref, sems):
    rows = out_ref.shape[0]
    features = basis_ref.shape[0]
    block = 512 if features % 512 == 0 else features
    spans = [pl.ds(first, block) for first in range(0, features, block)]

    def copies(from_basis, from_query):
        return [pltpu.make_async_copy(from_query, query_ref, sems.at[0])] + [
            pltpu.make_async_copy(from_basis.at[span], basis_ref.at[span], sems.at[1 + i])
            for i, span in enumerate(spans)
        ]

    side = lax.axis_index("parts")

    @pl.when(side == 0)
    def _():
        for copy in copies(basis_in_ref, query_in_ref):
            copy.start()

    @pl.when(side != 0)
    def _():
        for copy in copies(basis_out_ref, query_out_ref):
            copy.start()

    landed = copies(basis_in_ref, query_in_ref)
    landed[0].wait()
    turned_ref[...] = query_ref[...].T
    for copy, span in zip(landed[1:], spans):
        copy.wait()
        out_ref[:, span] = lax.dot_general(
            turned_ref[:rows], basis_ref[span], NT, preferred_element_type=jnp.float32
        ).astype(jnp.bfloat16)


def first_pull(basis_in, basis_out, query_in, query_out, rows):
    features, depth = basis_in.shape
    spread = query_in.shape[1]
    blocks = features // 512 if features % 512 == 0 else 1
    out, basis, _, turned = pl.pallas_call(
        first_pull_kernel,
        out_shape=[bf16(rows, features), bf16(features, depth), bf16(depth, spread), bf16(spread, depth)],
        in_specs=[HBM] * 4,
        out_specs=[VMEM] * 4,
        scratch_shapes=[pltpu.SemaphoreType.DMA((1 + blocks,))],
        compiler_params=pltpu.CompilerParams(vmem_limit_bytes=16 * MIB),
    )(*in_hbm(basis_in, basis_out, query_in, query_out))
    return out, basis, turned


def pull_kernel(turned_ref, basis_ref, after_ref, *outs):
    rows, features = outs[0].shape
    block = 512 if features % 512 == 0 else features
    for i in range(features // block):
        pulled = lax.dot_general(
            turned_ref[rows:], basis_ref[i * block : (i + 1) * block], NT, preferred_element_type=jnp.float32
        ).astype(jnp.bfloat16)
        for c, out in enumerate(outs):
            out[:, i * block : (i + 1) * block] = pulled[c * rows : (c + 1) * rows]


def pull(after, turned, basis, rows):
    chunks = turned.shape[0] // rows - 1
    return pl.pallas_call(
        pull_kernel,
        out_shape=[bf16(rows, basis.shape[0])] * chunks,
        in_specs=[VMEM, VMEM, ANY],
        out_specs=[VMEM] * chunks,
        compiler_params=pltpu.CompilerParams(vmem_limit_bytes=16 * MIB),
    )(turned, basis, after)


def deal_kernel(acts_ref, grads_ref, after_ref, mine_ref, theirs_ref, sems):
    def copies(mine, theirs):
        return [
            pltpu.make_async_copy(mine, mine_ref, sems.at[0]),
            pltpu.make_async_copy(theirs, theirs_ref, sems.at[1]),
        ]

    side = lax.axis_index("parts")

    @pl.when(side == 0)
    def _():
        for copy in copies(acts_ref, grads_ref):
            copy.start()

    @pl.when(side != 0)
    def _():
        for copy in copies(grads_ref, acts_ref):
            copy.start()

    for copy in copies(acts_ref, grads_ref):
        copy.wait()


def deal(after, acts, grads):
    return pl.pallas_call(
        deal_kernel,
        out_shape=[bf16(*acts.shape)] * 2,
        in_specs=[HBM, HBM, ANY],
        out_specs=[VMEM, VMEM],
        scratch_shapes=[pltpu.SemaphoreType.DMA((2,))],
        compiler_params=pltpu.CompilerParams(vmem_limit_bytes=8 * MIB),
    )(*in_hbm(acts, grads), after)


def total_kernel(mine_ref, came_ref, after_ref, *rest):
    mine = mine_ref[...].astype(jnp.float32) + came_ref[...].astype(jnp.float32)
    rest[-1][...] = mine.astype(jnp.bfloat16)
    if len(rest) == 3:
        rest[1][...] = rest[0][...]


def total(after, mine, came, later=None):
    extra = [] if later is None else [later]
    out = pl.pallas_call(
        total_kernel,
        out_shape=[bf16(*a.shape) for a in extra + [mine]],
        in_specs=[VMEM, VMEM, ANY] + [VMEM] * len(extra),
        out_specs=[VMEM] * (1 + len(extra)),
        compiler_params=pltpu.CompilerParams(vmem_limit_bytes=8 * MIB),
    )(mine, came, after, *extra)
    return out[-1], (out[0] if extra else None)


def take_kernel(hop, mine_ref, came_ref, after_ref, out_ref):
    z = lax.axis_index("dp")
    here = jnp.minimum(z, lax.axis_size("dp") - 1 - z) == hop

    @pl.when(here)
    def _():
        out_ref[...] = came_ref[...]

    @pl.when(jnp.logical_not(here))
    def _():
        out_ref[...] = mine_ref[...]


def take(after, hop, mine, came):
    return pl.pallas_call(
        functools.partial(take_kernel, hop),
        out_shape=bf16(*mine.shape),
        in_specs=[VMEM, VMEM, ANY],
        out_specs=VMEM,
        compiler_params=pltpu.CompilerParams(vmem_limit_bytes=8 * MIB),
    )(mine, came, after)


def project_kernel(tokens_ref, others_ref, after_ref, *rest):
    factors = jnp.concatenate([ref[...] for ref in rest[:-2]], axis=0)
    others = lax.dot_general(factors, others_ref[...], NT, preferred_element_type=jnp.float32)
    rest[-1][...] = others.astype(jnp.bfloat16)
    rest[-2][...] = lax.dot_general(factors, tokens_ref[...], NT, preferred_element_type=jnp.float32)


def project(after, factors, tokens, others):
    rows = sum(chunk.shape[0] for chunk in factors)
    return pl.pallas_call(
        project_kernel,
        out_shape=[jax.ShapeDtypeStruct((rows, tokens.shape[0]), jnp.float32), bf16(rows, others.shape[0])],
        in_specs=[VMEM, VMEM, ANY] + [VMEM] * len(factors),
        out_specs=[VMEM, VMEM],
        compiler_params=pltpu.CompilerParams(vmem_limit_bytes=16 * MIB),
    )(tokens, others, after, *factors)


def score_kernel(count, *refs):
    out_ref, first = refs[-1], 0
    for own_ref, other_ref in zip(refs[:count], refs[count : 2 * count]):
        product = own_ref[...] * other_ref[...].astype(jnp.float32)
        queries = product.shape[0] // RANK
        out_ref[first : first + queries] = jnp.sum(
            product.reshape(queries, RANK, product.shape[1]), axis=1
        ) * RANK ** (-0.5)
        first += queries


def score(own, other):
    rows = sum(piece.shape[0] for piece in own)
    return pl.pallas_call(
        functools.partial(score_kernel, len(own)),
        out_shape=jax.ShapeDtypeStruct((rows // RANK, own[0].shape[1]), jnp.float32),
        in_specs=[VMEM] * (2 * len(own)),
        out_specs=VMEM,
        compiler_params=pltpu.CompilerParams(vmem_limit_bytes=8 * MIB),
    )(*own, *other)


def pool_kernel(counts_ref, one_ref, two_ref, scores_ref, pooled_ref):
    scores = one_ref[...] + two_ref[...]
    scores_ref[...] = scores
    position = lax.broadcasted_iota(jnp.int32, scores.shape, 1)
    column = lax.broadcasted_iota(jnp.int32, pooled_ref.shape, 1)
    pooled = jnp.zeros(pooled_ref.shape, jnp.float32)
    start = jnp.int32(0)
    for k in range(counts_ref.shape[1]):
        count = counts_ref[0, k]
        inside = (position >= start) & (position < start + count)
        found = jnp.sum(jnp.where(inside, scores, 0.0), axis=1, keepdims=True)
        root = jnp.sqrt(jnp.full((1, 1), count, jnp.int32).astype(jnp.float32))
        pooled = jnp.where(column == k, found / root, pooled)
        start = start + count
    pooled_ref[...] = pooled


def pool(counts, one, two):
    return pl.pallas_call(
        pool_kernel,
        out_shape=[
            jax.ShapeDtypeStruct(one.shape, jnp.float32),
            jax.ShapeDtypeStruct((one.shape[0], counts.shape[1]), jnp.float32),
        ],
        in_specs=[pl.BlockSpec(memory_space=pltpu.SMEM), VMEM, VMEM],
        out_specs=[VMEM, VMEM],
        compiler_params=pltpu.CompilerParams(vmem_limit_bytes=8 * MIB),
    )(counts, one, two)


def chunk_rows(spread):
    for chunks, group in ((8, 2), (12, 1)):
        rows = spread // chunks
        if spread % chunks == 0 and rows % 16 == 0 and rows * group % RANK == 0:
            return rows, group
    return RANK, 1


def is_power(number):
    return number & (number - 1) == 0


def per_device(
    acts,
    grads,
    basis_in,
    output_eigen_basis,
    query_in,
    query_out,
    doc_counts,
    pair_query,
    pair_device,
    pair_doc,
):
    n = lax.axis_size("dp")
    layers = lax.axis_size("layer")
    z = lax.axis_index("dp")
    spread = query_in.shape[2]
    queries = spread // RANK
    half = n // 2
    rows, group = chunk_rows(spread)
    chunks = spread // rows

    first, basis, turned = first_pull(
        basis_in[0], output_eigen_basis[0], query_in[0], query_out[0], rows
    )
    own = [first] + list(pull(first, turned, basis, rows))
    swap = [(0, 1), (1, 0)]

    stages = [("in", hop) for hop in range(half - 1)] + [("mid", 0)]
    stages += [("out", hop) for hop in range(half - 2, -1, -1)]

    def transfer(kind, hop, value):
        if kind == "in":
            return lax.ppermute(value, "dp", [(hop, hop + 1), (n - 1 - hop, n - 2 - hop)])
        if kind == "mid":
            return lax.ppermute(value, "dp", [(half - 1, half), (half, half - 1)])
        return lax.ppermute(value, "dp", [(hop + 1, hop), (n - 2 - hop, n - 1 - hop)])

    part, came = list(own), [None] * chunks
    ahead = min(2, chunks)
    for c in range(ahead):
        came[c] = transfer(*stages[0], part[c])
    after = own[-1]
    tokens, theirs = deal(own[-1], acts[0], grads[0])
    others = lax.ppermute(theirs, "parts", swap)
    waiting, mine, back = [], [], []
    for turn in range(chunks + len(stages) - 1):
        for s, (kind, hop) in enumerate(stages):
            c = turn - s
            if not 0 <= c < chunks:
                continue
            if kind == "out":
                part[c] = take(after, hop, part[c], came[c])
            else:
                later = c + ahead if s == 0 and c + ahead < chunks else None
                part[c], moved = total(after, part[c], came[c], None if later is None else own[later])
                if later is not None:
                    came[later] = transfer(*stages[0], moved)
            after = part[c]
            if s + 1 < len(stages):
                came[c] = transfer(*stages[s + 1], part[c])
            elif c % group == group - 1:
                waiting.append(part[c + 1 - group : c + 1])
        while turn >= chunks - 1 and waiting:
            projected, away = project(after, waiting.pop(0), tokens, others)
            mine.append(projected)
            back.append(lax.ppermute(away, "parts", swap))
            after = projected

    scores = score(mine, back)
    if is_power(layers):
        step = 1
        while 2 * step < layers:
            scores = scores + lax.ppermute(scores, "layer", [(i, i ^ step) for i in range(layers)])
            step *= 2
        one, two = scores, lax.ppermute(scores, "layer", [(i, i ^ step) for i in range(layers)])
    else:
        one = lax.psum(scores, "layer")
        two = jnp.zeros_like(one)
    token_scores, pooled = pool(doc_counts, one, two)

    docs = doc_counts.shape[1]
    cells = queries * docs
    target = pair_device[:, 0]
    cell = pair_query * docs + pair_doc
    if n <= 8 and is_power(n):
        table, step = pooled[None], 1
        while step < n:
            table = jnp.concatenate(
                [table, lax.ppermute(table, "dp", [(i, i ^ step) for i in range(n)])], axis=0
            )
            step *= 2
        table = table.reshape(1, n * cells)
        column = (z ^ target) * cells + cell
    else:
        table = lax.all_gather(pooled.reshape(1, cells), "dp", axis=1, tiled=True)
        column = target * cells + cell
    hit = column[:, None] == jnp.arange(n * cells, dtype=jnp.int32)[None, :]
    pair_scores = jnp.sum(jnp.where(hit, table, 0.0), axis=1)
    return (token_scores, pair_scores)


def solution(mesh):
    in_specs = (
        P("layer", ("parts", "dp"), None),
        P("layer", ("parts", "dp"), None),
        P("layer", None, "dp"),
        P("layer", None, "dp"),
        P("layer", "dp", None),
        P("layer", "dp", None),
        P(("parts", "dp"), None),
        P(("parts", "dp")),
        P(("parts", "dp"), None),
        P(("parts", "dp")),
    )
    out_specs = (P(None, ("parts", "dp")), P(("parts", "dp")))
    return jax.shard_map(
        per_device, mesh=mesh, in_specs=in_specs, out_specs=out_specs, check_vma=False
    )
```

```python
import functools

import jax
import jax.numpy as jnp
from jax import lax
from jax.experimental import pallas as pl
from jax.experimental.pallas import tpu as pltpu
from jax.sharding import PartitionSpec as P

RANK = 32
NT = (((1,), (1,)), ((), ()))


VMEM = pl.BlockSpec(memory_space=pltpu.VMEM)
HBM = pl.BlockSpec(memory_space=pltpu.HBM)
ANY = pl.BlockSpec(memory_space=pl.ANY)
MIB = 1024 * 1024
LANES = 128


def in_hbm(*arrays):
    return [pltpu.with_memory_space_constraint(array, pltpu.HBM) for array in arrays]


def bf16(*shape):
    return jax.ShapeDtypeStruct(shape, jnp.bfloat16)


def pull_kernel(chunks, acts_ref, grads_ref, basis_in_ref, basis_out_ref, query_in_ref, query_out_ref, *rest):
    outs, (tokens_ref, theirs_ref, basis, query, turned, sems) = rest[:chunks], rest[chunks:]
    rows = outs[0].shape[0]
    features = basis.shape[0]
    block = 512 if features % 512 == 0 else features
    spans = [pl.ds(first, block) for first in range(0, features, block)]

    def copies(mine, theirs, from_basis, from_query):
        pairs = [(from_query, query)]
        pairs += [(from_basis.at[span], basis.at[span]) for span in spans]
        pairs += [(mine, tokens_ref), (theirs, theirs_ref)]
        return [pltpu.make_async_copy(source, target, sems.at[i]) for i, (source, target) in enumerate(pairs)]

    side = lax.axis_index("parts")

    @pl.when(side == 0)
    def _():
        for copy in copies(acts_ref, grads_ref, basis_in_ref, query_in_ref):
            copy.start()

    @pl.when(side != 0)
    def _():
        for copy in copies(grads_ref, acts_ref, basis_out_ref, query_out_ref):
            copy.start()

    landed = copies(acts_ref, grads_ref, basis_in_ref, query_in_ref)
    landed[0].wait()
    turned[...] = query[...].T
    for copy, span in zip(landed[1:], spans):
        copy.wait()
        pulled = lax.dot_general(turned[...], basis[span], NT, preferred_element_type=jnp.float32)
        pulled = pulled.astype(jnp.bfloat16)
        for c, out in enumerate(outs):
            out[:, span] = pulled[c * rows : (c + 1) * rows]
    for copy in landed[1 + len(spans) :]:
        copy.wait()


def pull(acts, grads, basis_in, basis_out, query_in, query_out, rows):
    features, depth = basis_in.shape
    spread = query_in.shape[1]
    chunks = spread // rows
    blocks = features // 512 if features % 512 == 0 else 1
    out = pl.pallas_call(
        functools.partial(pull_kernel, chunks),
        out_shape=[bf16(rows, features)] * chunks + [bf16(*acts.shape)] * 2,
        in_specs=[HBM] * 6,
        out_specs=[VMEM] * (chunks + 2),
        scratch_shapes=[
            pltpu.VMEM((features, depth), jnp.bfloat16),
            pltpu.VMEM((depth, spread), jnp.bfloat16),
            pltpu.VMEM((spread, depth), jnp.bfloat16),
            pltpu.SemaphoreType.DMA((blocks + 3,)),
        ],
        compiler_params=pltpu.CompilerParams(vmem_limit_bytes=24 * MIB),
    )(*in_hbm(acts, grads, basis_in, basis_out, query_in, query_out))
    return list(out[:chunks]), out[-2], out[-1]


def at_depth(hop):
    z = lax.axis_index("dp")
    return jnp.minimum(z, lax.axis_size("dp") - 1 - z) == hop


def write_send(later_ref, value_ref, send_ref):
    @pl.when(at_depth(0))
    def _():
        send_ref[...] = later_ref[...]

    @pl.when(jnp.logical_not(at_depth(0)))
    def _():
        send_ref[...] = value_ref[...]


def total_kernel(shared, mine_ref, came_ref, after_ref, *rest):
    mine = mine_ref[...].astype(jnp.float32) + came_ref[...].astype(jnp.float32)
    rest[-1][...] = mine.astype(jnp.bfloat16)
    if shared:
        write_send(rest[0], rest[2], rest[1])
    elif len(rest) == 3:
        rest[1][...] = rest[0][...]


def total(after, mine, came, later=None, shared=False):
    extra = [] if later is None else [later]
    out = pl.pallas_call(
        functools.partial(total_kernel, shared),
        out_shape=[bf16(*a.shape) for a in extra + [mine]],
        in_specs=[VMEM, VMEM, ANY] + [VMEM] * len(extra),
        out_specs=[VMEM] * (1 + len(extra)),
        compiler_params=pltpu.CompilerParams(vmem_limit_bytes=8 * MIB),
    )(mine, came, after, *extra)
    return out[-1], (out[0] if extra else None)


def take_kernel(hop, shared, mine_ref, came_ref, after_ref, *rest):
    @pl.when(at_depth(hop))
    def _():
        rest[-1][...] = came_ref[...]

    @pl.when(jnp.logical_not(at_depth(hop)))
    def _():
        rest[-1][...] = mine_ref[...]

    if shared:
        write_send(rest[0], rest[2], rest[1])


def take(after, hop, mine, came, later=None):
    extra = [] if later is None else [later]
    out = pl.pallas_call(
        functools.partial(take_kernel, hop, later is not None),
        out_shape=[bf16(*a.shape) for a in extra + [mine]],
        in_specs=[VMEM, VMEM, ANY] + [VMEM] * len(extra),
        out_specs=[VMEM] * (1 + len(extra)),
        compiler_params=pltpu.CompilerParams(vmem_limit_bytes=8 * MIB),
    )(mine, came, after, *extra)
    return out[-1], (out[0] if extra else None)


def project_kernel(tokens_ref, after_ref, *rest):
    factors = jnp.concatenate([ref[...] for ref in rest[:-1]], axis=0)
    projected = lax.dot_general(factors, tokens_ref[...], NT, preferred_element_type=jnp.float32)
    rest[-1][...] = projected.astype(rest[-1].dtype)


def project(after, factors, tokens, dtype):
    rows = sum(chunk.shape[0] for chunk in factors)
    return pl.pallas_call(
        project_kernel,
        out_shape=jax.ShapeDtypeStruct((rows, tokens.shape[0]), dtype),
        in_specs=[VMEM, ANY] + [VMEM] * len(factors),
        out_specs=VMEM,
        compiler_params=pltpu.CompilerParams(vmem_limit_bytes=16 * MIB),
    )(tokens, after, *factors)


def score_kernel(count, counts_ref, *refs):
    out_ref = refs[-1]
    own = jnp.concatenate([ref[...] for ref in refs[:count]], axis=0)
    other = jnp.concatenate([ref[...] for ref in refs[count : 2 * count]], axis=0)
    product = own * other.astype(jnp.float32)
    queries, tokens = product.shape[0] // RANK, product.shape[1]
    scores = jnp.sum(product.reshape(queries, RANK, tokens), axis=1) * RANK ** (-0.5)
    out_ref[:, :tokens] = scores
    position = lax.broadcasted_iota(jnp.int32, scores.shape, 1)
    column = lax.broadcasted_iota(jnp.int32, (queries, LANES), 1)
    pooled = jnp.zeros((queries, LANES), jnp.float32)
    start = jnp.int32(0)
    for k in range(counts_ref.shape[1]):
        count = counts_ref[0, k]
        inside = (position >= start) & (position < start + count)
        found = jnp.sum(jnp.where(inside, scores, 0.0), axis=1, keepdims=True)
        root = jnp.sqrt(jnp.full((1, 1), count, jnp.int32).astype(jnp.float32))
        pooled = jnp.where(column == k, found / root, pooled)
        start = start + count
    out_ref[:, out_ref.shape[1] - LANES :] = pooled


def score(counts, own, other):
    rows = sum(piece.shape[0] for piece in own)
    tokens = own[0].shape[1]
    width = (tokens + LANES - 1) // LANES * LANES + LANES
    return pl.pallas_call(
        functools.partial(score_kernel, len(own)),
        out_shape=jax.ShapeDtypeStruct((rows // RANK, width), jnp.float32),
        in_specs=[pl.BlockSpec(memory_space=pltpu.SMEM)] + [VMEM] * (2 * len(own)),
        out_specs=VMEM,
        compiler_params=pltpu.CompilerParams(vmem_limit_bytes=16 * MIB),
    )(counts, *own, *other)


def chunk_rows(spread):
    return spread // 8 if spread % 128 == 0 else RANK


def is_power(number):
    return number & (number - 1) == 0


def per_device(
    acts,
    grads,
    basis_in,
    output_eigen_basis,
    query_in,
    query_out,
    doc_counts,
    pair_query,
    pair_device,
    pair_doc,
):
    n = lax.axis_size("dp")
    layers = lax.axis_size("layer")
    z = lax.axis_index("dp")
    spread = query_in.shape[2]
    queries = spread // RANK
    half = n // 2
    rows = chunk_rows(spread)
    chunks = spread // rows

    own, tokens, theirs = pull(
        acts[0], grads[0], basis_in[0], output_eigen_basis[0], query_in[0], query_out[0], rows
    )
    swap = [(0, 1), (1, 0)]

    stages = [("in", hop) for hop in range(half - 1)] + [("mid", 0)]
    stages += [("out", hop) for hop in range(half - 2, -1, -1)]
    last = len(stages) - 1

    def transfer(kinds, hop, value):
        pairs = []
        if "in" in kinds:
            pairs += [(hop, hop + 1), (n - 1 - hop, n - 2 - hop)]
        if "mid" in kinds:
            pairs += [(half - 1, half), (half, half - 1)]
        if "out" in kinds:
            pairs += [(hop + 1, hop), (n - 2 - hop, n - 1 - hop)]
        return lax.ppermute(value, "dp", pairs)

    part, came = list(own), [None] * chunks
    ahead = min(2, chunks)
    for c in range(ahead):
        came[c] = transfer(stages[0][:1], stages[0][1], part[c])
    others = lax.ppermute(theirs, "parts", swap)
    after = own[0]
    waiting, mine, back = [], [], []

    def project_waiting(after):
        away = project(after, waiting, others, jnp.bfloat16)
        back.append(lax.ppermute(away, "parts", swap))
        mine.append(project(away, waiting, tokens, jnp.float32))
        waiting.clear()
        return mine[-1]

    for turn in range(chunks + last):
        for s, (kind, hop) in enumerate(stages):
            c = turn - s
            if not 0 <= c < chunks:
                continue
            later = turn + ahead if turn + ahead < chunks else None
            if turn >= last - 1:
                use = later if s == last - 1 else None
            else:
                use = later if s == 0 else None
            shared = use is not None and turn >= last - 1
            chunk = None if use is None else own[use]
            if kind == "out":
                part[c], send = take(after, hop, part[c], came[c], chunk)
            else:
                part[c], send = total(after, part[c], came[c], chunk, shared)
            after = part[c]
            if shared:
                came[c] = came[use] = transfer(("in", "out"), 0, send)
                continue
            if use is not None:
                came[use] = transfer(stages[0][:1], stages[0][1], send)
            if s < last:
                came[c] = transfer(stages[s + 1][:1], stages[s + 1][1], part[c])
            else:
                waiting.append(part[c])
        if turn >= chunks - 1 and waiting:
            after = project_waiting(after)

    scores = score(doc_counts, mine, back)
    if not is_power(layers):
        scores = lax.psum(scores, "layer")
    steps = [1 << k for k in range(layers.bit_length() - 1)] if is_power(layers) else []

    def add_other(value, step):
        return value + lax.ppermute(value, "layer", [(i, i ^ step) for i in range(layers)])

    if steps:
        scores = add_other(scores, steps[0])
    token_scores, pooled = scores[:, : acts.shape[1]], scores[:, -LANES:]
    for step in steps[1:]:
        token_scores = add_other(token_scores, step)

    docs = doc_counts.shape[1]
    cells = queries * docs
    flat = pooled[:, :docs].reshape(1, cells)
    target = pair_device[:, 0]
    cell = pair_query * docs + pair_doc
    if n <= 8 and is_power(n):
        table = jnp.concatenate(
            [flat] + [lax.ppermute(flat, "dp", [(i, i ^ k) for i in range(n)]) for k in range(1, n)], axis=1
        )
        column = (z ^ target) * cells + cell
    else:
        table = lax.all_gather(flat, "dp", axis=1, tiled=True)
        column = target * cells + cell
    for step in steps[1:]:
        table = add_other(table, step)
    hit = column[:, None] == jnp.arange(n * cells, dtype=jnp.int32)[None, :]
    pair_scores = jnp.sum(jnp.where(hit, table, 0.0), axis=1)
    return (token_scores, pair_scores)


def solution(mesh):
    in_specs = (
        P("layer", ("parts", "dp"), None),
        P("layer", ("parts", "dp"), None),
        P("layer", None, "dp"),
        P("layer", None, "dp"),
        P("layer", "dp", None),
        P("layer", "dp", None),
        P(("parts", "dp"), None),
        P(("parts", "dp")),
        P(("parts", "dp"), None),
        P(("parts", "dp")),
    )
    out_specs = (P(None, ("parts", "dp")), P(("parts", "dp")))
    return jax.shard_map(
        per_device, mesh=mesh, in_specs=in_specs, out_specs=out_specs, check_vma=False
    )
```

```python
import functools

import jax
import jax.numpy as jnp
from jax import lax
from jax.experimental import pallas as pl
from jax.experimental.pallas import tpu as pltpu
from jax.sharding import PartitionSpec as P

RANK = 32
NT = (((1,), (1,)), ((), ()))


VMEM = pl.BlockSpec(memory_space=pltpu.VMEM)
HBM = pl.BlockSpec(memory_space=pltpu.HBM)
ANY = pl.BlockSpec(memory_space=pl.ANY)
MIB = 1024 * 1024
LANES = 128


def in_hbm(*arrays):
    return [pltpu.with_memory_space_constraint(array, pltpu.HBM) for array in arrays]


def bf16(*shape):
    return jax.ShapeDtypeStruct(shape, jnp.bfloat16)


def first_pull_kernel(basis_in_ref, basis_out_ref, query_in_ref, query_out_ref, out_ref, basis_ref, query_ref, turned_ref, sems):
    rows = out_ref.shape[0]
    features = basis_ref.shape[0]
    block = 512 if features % 512 == 0 else features
    spans = [pl.ds(first, block) for first in range(0, features, block)]

    def copies(from_basis, from_query):
        return [pltpu.make_async_copy(from_query, query_ref, sems.at[0])] + [
            pltpu.make_async_copy(from_basis.at[span], basis_ref.at[span], sems.at[1 + i])
            for i, span in enumerate(spans)
        ]

    side = lax.axis_index("parts")

    @pl.when(side == 0)
    def _():
        for copy in copies(basis_in_ref, query_in_ref):
            copy.start()

    @pl.when(side != 0)
    def _():
        for copy in copies(basis_out_ref, query_out_ref):
            copy.start()

    landed = copies(basis_in_ref, query_in_ref)
    landed[0].wait()
    turned_ref[...] = query_ref[...].T
    for copy, span in zip(landed[1:], spans):
        copy.wait()
        out_ref[:, span] = lax.dot_general(
            turned_ref[:rows], basis_ref[span], NT, preferred_element_type=jnp.float32
        ).astype(jnp.bfloat16)


def first_pull(basis_in, basis_out, query_in, query_out, rows):
    features, depth = basis_in.shape
    spread = query_in.shape[1]
    blocks = features // 512 if features % 512 == 0 else 1
    out, basis, _, turned = pl.pallas_call(
        first_pull_kernel,
        out_shape=[bf16(rows, features), bf16(features, depth), bf16(depth, spread), bf16(spread, depth)],
        in_specs=[HBM] * 4,
        out_specs=[VMEM] * 4,
        scratch_shapes=[pltpu.SemaphoreType.DMA((1 + blocks,))],
        compiler_params=pltpu.CompilerParams(vmem_limit_bytes=16 * MIB),
    )(*in_hbm(basis_in, basis_out, query_in, query_out))
    return out, basis, turned


def pull_kernel(acts_ref, grads_ref, turned_ref, basis_ref, after_ref, *rest):
    outs, (tokens_ref, theirs_ref, sems) = rest[:-3], rest[-3:]

    def copies(mine, theirs):
        return [
            pltpu.make_async_copy(mine, tokens_ref, sems.at[0]),
            pltpu.make_async_copy(theirs, theirs_ref, sems.at[1]),
        ]

    side = lax.axis_index("parts")

    @pl.when(side == 0)
    def _():
        for copy in copies(acts_ref, grads_ref):
            copy.start()

    @pl.when(side != 0)
    def _():
        for copy in copies(grads_ref, acts_ref):
            copy.start()

    rows, features = outs[0].shape
    block = 512 if features % 512 == 0 else features
    for i in range(features // block):
        pulled = lax.dot_general(
            turned_ref[rows:], basis_ref[i * block : (i + 1) * block], NT, preferred_element_type=jnp.float32
        ).astype(jnp.bfloat16)
        for c, out in enumerate(outs):
            out[:, i * block : (i + 1) * block] = pulled[c * rows : (c + 1) * rows]
    for copy in copies(acts_ref, grads_ref):
        copy.wait()


def pull(after, turned, basis, acts, grads, rows):
    chunks = turned.shape[0] // rows - 1
    out = pl.pallas_call(
        pull_kernel,
        out_shape=[bf16(rows, basis.shape[0])] * chunks + [bf16(*acts.shape)] * 2,
        in_specs=[HBM, HBM, VMEM, VMEM, ANY],
        out_specs=[VMEM] * (chunks + 2),
        scratch_shapes=[pltpu.SemaphoreType.DMA((2,))],
        compiler_params=pltpu.CompilerParams(vmem_limit_bytes=24 * MIB),
    )(*in_hbm(acts, grads), turned, basis, after)
    return list(out[:chunks]), out[-2], out[-1]


def at_depth(hop):
    z = lax.axis_index("dp")
    return jnp.minimum(z, lax.axis_size("dp") - 1 - z) == hop


def write_send(later_ref, value_ref, send_ref):
    @pl.when(at_depth(0))
    def _():
        send_ref[...] = later_ref[...]

    @pl.when(jnp.logical_not(at_depth(0)))
    def _():
        send_ref[...] = value_ref[...]


def total_kernel(shared, mine_ref, came_ref, after_ref, *rest):
    mine = mine_ref[...].astype(jnp.float32) + came_ref[...].astype(jnp.float32)
    rest[-1][...] = mine.astype(jnp.bfloat16)
    if shared:
        write_send(rest[0], rest[2], rest[1])
    elif len(rest) == 3:
        rest[1][...] = rest[0][...]


def total(after, mine, came, later=None, shared=False):
    extra = [] if later is None else [later]
    out = pl.pallas_call(
        functools.partial(total_kernel, shared),
        out_shape=[bf16(*a.shape) for a in extra + [mine]],
        in_specs=[VMEM, VMEM, ANY] + [VMEM] * len(extra),
        out_specs=[VMEM] * (1 + len(extra)),
        compiler_params=pltpu.CompilerParams(vmem_limit_bytes=8 * MIB),
    )(mine, came, after, *extra)
    return out[-1], (out[0] if extra else None)


def take_kernel(hop, shared, mine_ref, came_ref, after_ref, *rest):
    @pl.when(at_depth(hop))
    def _():
        rest[-1][...] = came_ref[...]

    @pl.when(jnp.logical_not(at_depth(hop)))
    def _():
        rest[-1][...] = mine_ref[...]

    if shared:
        write_send(rest[0], rest[2], rest[1])


def take(after, hop, mine, came, later=None):
    extra = [] if later is None else [later]
    out = pl.pallas_call(
        functools.partial(take_kernel, hop, later is not None),
        out_shape=[bf16(*a.shape) for a in extra + [mine]],
        in_specs=[VMEM, VMEM, ANY] + [VMEM] * len(extra),
        out_specs=[VMEM] * (1 + len(extra)),
        compiler_params=pltpu.CompilerParams(vmem_limit_bytes=8 * MIB),
    )(mine, came, after, *extra)
    return out[-1], (out[0] if extra else None)


def project_kernel(tokens_ref, after_ref, *rest):
    factors = jnp.concatenate([ref[...] for ref in rest[:-1]], axis=0)
    projected = lax.dot_general(factors, tokens_ref[...], NT, preferred_element_type=jnp.float32)
    rest[-1][...] = projected.astype(rest[-1].dtype)


def project(after, factors, tokens, dtype):
    rows = sum(chunk.shape[0] for chunk in factors)
    return pl.pallas_call(
        project_kernel,
        out_shape=jax.ShapeDtypeStruct((rows, tokens.shape[0]), dtype),
        in_specs=[VMEM, ANY] + [VMEM] * len(factors),
        out_specs=VMEM,
        compiler_params=pltpu.CompilerParams(vmem_limit_bytes=16 * MIB),
    )(tokens, after, *factors)


def score_kernel(count, counts_ref, *refs):
    out_ref = refs[-1]
    own = jnp.concatenate([ref[...] for ref in refs[:count]], axis=0)
    other = jnp.concatenate([ref[...] for ref in refs[count : 2 * count]], axis=0)
    product = own * other.astype(jnp.float32)
    queries, tokens = product.shape[0] // RANK, product.shape[1]
    scores = jnp.sum(product.reshape(queries, RANK, tokens), axis=1) * RANK ** (-0.5)
    out_ref[:, :tokens] = scores
    position = lax.broadcasted_iota(jnp.int32, scores.shape, 1)
    column = lax.broadcasted_iota(jnp.int32, (queries, LANES), 1)
    pooled = jnp.zeros((queries, LANES), jnp.float32)
    start = jnp.int32(0)
    for k in range(counts_ref.shape[1]):
        count = counts_ref[0, k]
        inside = (position >= start) & (position < start + count)
        found = jnp.sum(jnp.where(inside, scores, 0.0), axis=1, keepdims=True)
        root = jnp.sqrt(jnp.full((1, 1), count, jnp.int32).astype(jnp.float32))
        pooled = jnp.where(column == k, found / root, pooled)
        start = start + count
    out_ref[:, out_ref.shape[1] - LANES :] = pooled


def score(counts, own, other):
    rows = sum(piece.shape[0] for piece in own)
    tokens = own[0].shape[1]
    width = (tokens + LANES - 1) // LANES * LANES + LANES
    return pl.pallas_call(
        functools.partial(score_kernel, len(own)),
        out_shape=jax.ShapeDtypeStruct((rows // RANK, width), jnp.float32),
        in_specs=[pl.BlockSpec(memory_space=pltpu.SMEM)] + [VMEM] * (2 * len(own)),
        out_specs=VMEM,
        compiler_params=pltpu.CompilerParams(vmem_limit_bytes=16 * MIB),
    )(counts, *own, *other)


def chunk_rows(spread):
    return spread // 8 if spread % 128 == 0 else RANK


def is_power(number):
    return number & (number - 1) == 0


def per_device(
    acts,
    grads,
    basis_in,
    output_eigen_basis,
    query_in,
    query_out,
    doc_counts,
    pair_query,
    pair_device,
    pair_doc,
):
    n = lax.axis_size("dp")
    layers = lax.axis_size("layer")
    z = lax.axis_index("dp")
    spread = query_in.shape[2]
    queries = spread // RANK
    half = n // 2
    rows = chunk_rows(spread)
    chunks = spread // rows

    first, basis, turned = first_pull(
        basis_in[0], output_eigen_basis[0], query_in[0], query_out[0], rows
    )
    own, tokens, theirs = pull(first, turned, basis, acts[0], grads[0], rows)
    own = [first] + own
    swap = [(0, 1), (1, 0)]

    stages = [("in", hop) for hop in range(half - 1)] + [("mid", 0)]
    stages += [("out", hop) for hop in range(half - 2, -1, -1)]
    last = len(stages) - 1

    def transfer(kinds, hop, value):
        pairs = []
        if "in" in kinds:
            pairs += [(hop, hop + 1), (n - 1 - hop, n - 2 - hop)]
        if "mid" in kinds:
            pairs += [(half - 1, half), (half, half - 1)]
        if "out" in kinds:
            pairs += [(hop + 1, hop), (n - 2 - hop, n - 1 - hop)]
        return lax.ppermute(value, "dp", pairs)

    part, came = list(own), [None] * chunks
    ahead = min(2, chunks)
    for c in range(ahead):
        came[c] = transfer(stages[0][:1], stages[0][1], part[c])
    others = lax.ppermute(theirs, "parts", swap)
    after = own[0]
    waiting, mine, back = [], [], []

    def project_waiting(after):
        away = project(after, waiting, others, jnp.bfloat16)
        back.append(lax.ppermute(away, "parts", swap))
        mine.append(project(away, waiting, tokens, jnp.float32))
        waiting.clear()
        return mine[-1]

    swapped = set()
    for turn in range(chunks + last):
        steps = [(s, turn - s) for s in range(last) if 0 <= turn - s < chunks]
        due = [c for c in range(chunks) if c + last + (c in swapped) == turn]
        for s, c in steps + [(last, c) for c in due]:
            kind, hop = stages[s]
            later = turn + ahead if turn + ahead < chunks else None
            if turn >= last - 1:
                use = later if s == last - 1 else None
            else:
                use = later if s == 0 else None
            shared = use is not None and turn >= last - 1
            chunk = None if use is None else own[use]
            if kind == "out":
                part[c], send = take(after, hop, part[c], came[c], chunk)
            else:
                part[c], send = total(after, part[c], came[c], chunk, shared)
            after = part[c]
            if shared:
                came[c] = came[use] = transfer(("in", "out"), 0, send)
                swapped.add(c)
                continue
            if use is not None:
                came[use] = transfer(stages[0][:1], stages[0][1], send)
            if s < last:
                came[c] = transfer(stages[s + 1][:1], stages[s + 1][1], part[c])
            else:
                waiting.append(part[c])
        if turn >= chunks - 1 and waiting:
            after = project_waiting(after)

    scores = score(doc_counts, mine, back)
    if not is_power(layers):
        scores = lax.psum(scores, "layer")
    else:
        for step in [1 << k for k in range(layers.bit_length() - 1)]:
            scores = scores + lax.ppermute(scores, "layer", [(i, i ^ step) for i in range(layers)])
    token_scores, pooled = scores[:, : acts.shape[1]], scores[:, -LANES:]

    docs = doc_counts.shape[1]
    cells = queries * docs
    flat = pooled[:, :docs].reshape(1, cells)
    target = pair_device[:, 0]
    cell = pair_query * docs + pair_doc
    if n <= 8 and is_power(n):
        table = jnp.concatenate(
            [flat] + [lax.ppermute(flat, "dp", [(i, i ^ k) for i in range(n)]) for k in range(1, n)], axis=1
        )
        column = (z ^ target) * cells + cell
    else:
        table = lax.all_gather(flat, "dp", axis=1, tiled=True)
        column = target * cells + cell
    hit = column[:, None] == jnp.arange(n * cells, dtype=jnp.int32)[None, :]
    pair_scores = jnp.sum(jnp.where(hit, table, 0.0), axis=1)
    return (token_scores, pair_scores)


def solution(mesh):
    in_specs = (
        P("layer", ("parts", "dp"), None),
        P("layer", ("parts", "dp"), None),
        P("layer", None, "dp"),
        P("layer", None, "dp"),
        P("layer", "dp", None),
        P("layer", "dp", None),
        P(("parts", "dp"), None),
        P(("parts", "dp")),
        P(("parts", "dp"), None),
        P(("parts", "dp")),
    )
    out_specs = (P(None, ("parts", "dp")), P(("parts", "dp")))
    return jax.shard_map(
        per_device, mesh=mesh, in_specs=in_specs, out_specs=out_specs, check_vma=False
    )
```

```python
import functools

import jax
import jax.numpy as jnp
from jax import lax
from jax.experimental import pallas as pl
from jax.experimental.pallas import tpu as pltpu
from jax.sharding import PartitionSpec as P

RANK = 32
NT = (((1,), (1,)), ((), ()))


VMEM = pl.BlockSpec(memory_space=pltpu.VMEM)
HBM = pl.BlockSpec(memory_space=pltpu.HBM)
ANY = pl.BlockSpec(memory_space=pl.ANY)
MIB = 1024 * 1024
LANES = 128


def in_hbm(*arrays):
    return [pltpu.with_memory_space_constraint(array, pltpu.HBM) for array in arrays]


def bf16(*shape):
    return jax.ShapeDtypeStruct(shape, jnp.bfloat16)


def first_pull_kernel(basis_in_ref, basis_out_ref, query_in_ref, query_out_ref, out_ref, basis_ref, query_ref, turned_ref, sems):
    rows = out_ref.shape[0]
    features = basis_ref.shape[0]
    block = 512 if features % 512 == 0 else features
    spans = [pl.ds(first, block) for first in range(0, features, block)]

    def copies(from_basis, from_query):
        return [pltpu.make_async_copy(from_query, query_ref, sems.at[0])] + [
            pltpu.make_async_copy(from_basis.at[span], basis_ref.at[span], sems.at[1 + i])
            for i, span in enumerate(spans)
        ]

    side = lax.axis_index("parts")

    @pl.when(side == 0)
    def _():
        for copy in copies(basis_in_ref, query_in_ref):
            copy.start()

    @pl.when(side != 0)
    def _():
        for copy in copies(basis_out_ref, query_out_ref):
            copy.start()

    landed = copies(basis_in_ref, query_in_ref)
    landed[0].wait()
    turned_ref[...] = query_ref[...].T
    for copy, span in zip(landed[1:], spans):
        copy.wait()
        out_ref[:, span] = lax.dot_general(
            turned_ref[:rows], basis_ref[span], NT, preferred_element_type=jnp.float32
        ).astype(jnp.bfloat16)


def first_pull(basis_in, basis_out, query_in, query_out, rows):
    features, depth = basis_in.shape
    spread = query_in.shape[1]
    blocks = features // 512 if features % 512 == 0 else 1
    out, basis, _, turned = pl.pallas_call(
        first_pull_kernel,
        out_shape=[bf16(rows, features), bf16(features, depth), bf16(depth, spread), bf16(spread, depth)],
        in_specs=[HBM] * 4,
        out_specs=[VMEM] * 4,
        scratch_shapes=[pltpu.SemaphoreType.DMA((1 + blocks,))],
        compiler_params=pltpu.CompilerParams(vmem_limit_bytes=16 * MIB),
    )(*in_hbm(basis_in, basis_out, query_in, query_out))
    return out, basis, turned


def pull_kernel(turned_ref, basis_ref, after_ref, *outs):
    rows, features = outs[0].shape
    block = 512 if features % 512 == 0 else features
    for i in range(features // block):
        pulled = lax.dot_general(
            turned_ref[rows:], basis_ref[i * block : (i + 1) * block], NT, preferred_element_type=jnp.float32
        ).astype(jnp.bfloat16)
        for c, out in enumerate(outs):
            out[:, i * block : (i + 1) * block] = pulled[c * rows : (c + 1) * rows]


def pull(after, turned, basis, rows):
    chunks = turned.shape[0] // rows - 1
    return pl.pallas_call(
        pull_kernel,
        out_shape=[bf16(rows, basis.shape[0])] * chunks,
        in_specs=[VMEM, VMEM, ANY],
        out_specs=[VMEM] * chunks,
        compiler_params=pltpu.CompilerParams(vmem_limit_bytes=16 * MIB),
    )(turned, basis, after)


def deal_kernel(acts_ref, grads_ref, after_ref, mine_ref, theirs_ref, sems):
    def copies(mine, theirs):
        return [
            pltpu.make_async_copy(mine, mine_ref, sems.at[0]),
            pltpu.make_async_copy(theirs, theirs_ref, sems.at[1]),
        ]

    side = lax.axis_index("parts")

    @pl.when(side == 0)
    def _():
        for copy in copies(acts_ref, grads_ref):
            copy.start()

    @pl.when(side != 0)
    def _():
        for copy in copies(grads_ref, acts_ref):
            copy.start()

    for copy in copies(acts_ref, grads_ref):
        copy.wait()


def deal(after, acts, grads):
    return pl.pallas_call(
        deal_kernel,
        out_shape=[bf16(*acts.shape)] * 2,
        in_specs=[HBM, HBM, ANY],
        out_specs=[VMEM, VMEM],
        scratch_shapes=[pltpu.SemaphoreType.DMA((2,))],
        compiler_params=pltpu.CompilerParams(vmem_limit_bytes=8 * MIB),
    )(*in_hbm(acts, grads), after)


def at_depth(hop):
    z = lax.axis_index("dp")
    return jnp.minimum(z, lax.axis_size("dp") - 1 - z) == hop


def write_send(later_ref, value_ref, send_ref):
    @pl.when(at_depth(0))
    def _():
        send_ref[...] = later_ref[...]

    @pl.when(jnp.logical_not(at_depth(0)))
    def _():
        send_ref[...] = value_ref[...]


def total_kernel(shared, mine_ref, came_ref, after_ref, *rest):
    mine = mine_ref[...].astype(jnp.float32) + came_ref[...].astype(jnp.float32)
    rest[-1][...] = mine.astype(jnp.bfloat16)
    if shared:
        write_send(rest[0], rest[2], rest[1])
    elif len(rest) == 3:
        rest[1][...] = rest[0][...]


def total(after, mine, came, later=None, shared=False):
    extra = [] if later is None else [later]
    out = pl.pallas_call(
        functools.partial(total_kernel, shared),
        out_shape=[bf16(*a.shape) for a in extra + [mine]],
        in_specs=[VMEM, VMEM, ANY] + [VMEM] * len(extra),
        out_specs=[VMEM] * (1 + len(extra)),
        compiler_params=pltpu.CompilerParams(vmem_limit_bytes=8 * MIB),
    )(mine, came, after, *extra)
    return out[-1], (out[0] if extra else None)


def take_kernel(hop, shared, mine_ref, came_ref, after_ref, *rest):
    @pl.when(at_depth(hop))
    def _():
        rest[-1][...] = came_ref[...]

    @pl.when(jnp.logical_not(at_depth(hop)))
    def _():
        rest[-1][...] = mine_ref[...]

    if shared:
        write_send(rest[0], rest[2], rest[1])


def take(after, hop, mine, came, later=None):
    extra = [] if later is None else [later]
    out = pl.pallas_call(
        functools.partial(take_kernel, hop, later is not None),
        out_shape=[bf16(*a.shape) for a in extra + [mine]],
        in_specs=[VMEM, VMEM, ANY] + [VMEM] * len(extra),
        out_specs=[VMEM] * (1 + len(extra)),
        compiler_params=pltpu.CompilerParams(vmem_limit_bytes=8 * MIB),
    )(mine, came, after, *extra)
    return out[-1], (out[0] if extra else None)


def project_kernel(tokens_ref, after_ref, *rest):
    factors = jnp.concatenate([ref[...] for ref in rest[:-1]], axis=0)
    projected = lax.dot_general(factors, tokens_ref[...], NT, preferred_element_type=jnp.float32)
    rest[-1][...] = projected.astype(rest[-1].dtype)


def project(after, factors, tokens, dtype):
    rows = sum(chunk.shape[0] for chunk in factors)
    return pl.pallas_call(
        project_kernel,
        out_shape=jax.ShapeDtypeStruct((rows, tokens.shape[0]), dtype),
        in_specs=[VMEM, ANY] + [VMEM] * len(factors),
        out_specs=VMEM,
        compiler_params=pltpu.CompilerParams(vmem_limit_bytes=16 * MIB),
    )(tokens, after, *factors)


def score_kernel(count, counts_ref, *refs):
    out_ref = refs[-1]
    own = jnp.concatenate([ref[...] for ref in refs[:count]], axis=0)
    other = jnp.concatenate([ref[...] for ref in refs[count : 2 * count]], axis=0)
    product = own * other.astype(jnp.float32)
    queries, tokens = product.shape[0] // RANK, product.shape[1]
    scores = jnp.sum(product.reshape(queries, RANK, tokens), axis=1) * RANK ** (-0.5)
    out_ref[...] = jnp.zeros(out_ref.shape, jnp.float32)
    out_ref[:, :tokens] = scores
    position = lax.broadcasted_iota(jnp.int32, scores.shape, 1)
    docs = counts_ref.shape[1]
    column = lax.broadcasted_iota(jnp.int32, (queries, docs), 1)
    pooled = jnp.zeros((queries, docs), jnp.float32)
    start = jnp.int32(0)
    for k in range(docs):
        count = counts_ref[0, k]
        inside = (position >= start) & (position < start + count)
        found = jnp.sum(jnp.where(inside, scores, 0.0), axis=1, keepdims=True)
        root = jnp.sqrt(jnp.full((1, 1), count, jnp.int32).astype(jnp.float32))
        pooled = jnp.where(column == k, found / root, pooled)
        start = start + count
    out_ref[:, tokens : tokens + pooled.shape[1]] = pooled


def score(counts, own, other):
    rows = sum(piece.shape[0] for piece in own)
    width = (own[0].shape[1] + counts.shape[1] + LANES - 1) // LANES * LANES
    return pl.pallas_call(
        functools.partial(score_kernel, len(own)),
        out_shape=jax.ShapeDtypeStruct((rows // RANK, width), jnp.float32),
        in_specs=[pl.BlockSpec(memory_space=pltpu.SMEM)] + [VMEM] * (2 * len(own)),
        out_specs=VMEM,
        compiler_params=pltpu.CompilerParams(vmem_limit_bytes=16 * MIB),
    )(counts, *own, *other)


def chunk_rows(spread):
    return spread // 8 if spread % 128 == 0 else RANK


def is_power(number):
    return number & (number - 1) == 0


def per_device(
    acts,
    grads,
    basis_in,
    output_eigen_basis,
    query_in,
    query_out,
    doc_counts,
    pair_query,
    pair_device,
    pair_doc,
):
    n = lax.axis_size("dp")
    layers = lax.axis_size("layer")
    z = lax.axis_index("dp")
    spread = query_in.shape[2]
    queries = spread // RANK
    half = n // 2
    rows = chunk_rows(spread)
    chunks = spread // rows

    first, basis, turned = first_pull(
        basis_in[0], output_eigen_basis[0], query_in[0], query_out[0], rows
    )
    own = [first] + list(pull(first, turned, basis, rows))
    tokens, theirs = deal(own[-1], acts[0], grads[0])
    swap = [(0, 1), (1, 0)]

    stages = [("in", hop) for hop in range(half - 1)] + [("mid", 0)]
    stages += [("out", hop) for hop in range(half - 2, -1, -1)]
    last = len(stages) - 1

    def transfer(kinds, hop, value):
        pairs = []
        if "in" in kinds:
            pairs += [(hop, hop + 1), (n - 1 - hop, n - 2 - hop)]
        if "mid" in kinds:
            pairs += [(half - 1, half), (half, half - 1)]
        if "out" in kinds:
            pairs += [(hop + 1, hop), (n - 2 - hop, n - 1 - hop)]
        return lax.ppermute(value, "dp", pairs)

    part, came = list(own), [None] * chunks
    ahead = min(2, chunks)
    for c in range(ahead):
        came[c] = transfer(stages[0][:1], stages[0][1], part[c])
    others = lax.ppermute(theirs, "parts", swap)
    after = own[0]
    waiting, mine, back = [], [], []

    def project_waiting(after):
        away = project(after, waiting, others, jnp.bfloat16)
        back.append(lax.ppermute(away, "parts", swap))
        mine.append(project(away, waiting, tokens, jnp.float32))
        waiting.clear()
        return mine[-1]

    swapped = set()
    for turn in range(chunks + last):
        steps = [(s, turn - s) for s in range(last) if 0 <= turn - s < chunks]
        due = [c for c in range(chunks) if c + last + (c in swapped) == turn]
        for s, c in steps + [(last, c) for c in due]:
            kind, hop = stages[s]
            later = turn + ahead if turn + ahead < chunks else None
            if turn >= last - 1:
                use = later if s == last - 1 else None
            else:
                use = later if s == 0 else None
            shared = use is not None and turn >= last - 1
            chunk = None if use is None else own[use]
            if kind == "out":
                part[c], send = take(after, hop, part[c], came[c], chunk)
            else:
                part[c], send = total(after, part[c], came[c], chunk, shared)
            after = part[c]
            if shared:
                came[c] = came[use] = transfer(("in", "out"), 0, send)
                swapped.add(c)
                continue
            if use is not None:
                came[use] = transfer(stages[0][:1], stages[0][1], send)
            if s < last:
                came[c] = transfer(stages[s + 1][:1], stages[s + 1][1], part[c])
            else:
                waiting.append(part[c])
        if turn >= chunks + last - 2 and waiting:
            after = project_waiting(after)

    scores = score(doc_counts, mine, back)
    if not is_power(layers):
        scores = lax.psum(scores, "layer")
    else:
        for step in [1 << k for k in range(layers.bit_length() - 1)]:
            scores = scores + lax.ppermute(scores, "layer", [(i, i ^ step) for i in range(layers)])
    tokens_here, docs = acts.shape[1], doc_counts.shape[1]
    token_scores, pooled = scores[:, :tokens_here], scores[:, tokens_here : tokens_here + docs]

    cells = queries * docs
    flat = pooled.reshape(1, cells)
    target = pair_device[:, 0]
    cell = pair_query * docs + pair_doc
    if n <= 8 and is_power(n):
        table = jnp.concatenate(
            [flat] + [lax.ppermute(flat, "dp", [(i, i ^ k) for i in range(n)]) for k in range(1, n)], axis=1
        )
        column = (z ^ target) * cells + cell
    else:
        table = lax.all_gather(flat, "dp", axis=1, tiled=True)
        column = target * cells + cell
    hit = column[:, None] == jnp.arange(n * cells, dtype=jnp.int32)[None, :]
    pair_scores = jnp.sum(jnp.where(hit, table, 0.0), axis=1)
    return (token_scores, pair_scores)


def solution(mesh):
    in_specs = (
        P("layer", ("parts", "dp"), None),
        P("layer", ("parts", "dp"), None),
        P("layer", None, "dp"),
        P("layer", None, "dp"),
        P("layer", "dp", None),
        P("layer", "dp", None),
        P(("parts", "dp"), None),
        P(("parts", "dp")),
        P(("parts", "dp"), None),
        P(("parts", "dp")),
    )
    out_specs = (P(None, ("parts", "dp")), P(("parts", "dp")))
    return jax.shard_map(
        per_device, mesh=mesh, in_specs=in_specs, out_specs=out_specs, check_vma=False
    )
```

```python
import functools

import jax
import jax.numpy as jnp
from jax import lax
from jax.experimental import pallas as pl
from jax.experimental.pallas import tpu as pltpu
from jax.sharding import PartitionSpec as P

RANK = 32
NT = (((1,), (1,)), ((), ()))


VMEM = pl.BlockSpec(memory_space=pltpu.VMEM)
HBM = pl.BlockSpec(memory_space=pltpu.HBM)
ANY = pl.BlockSpec(memory_space=pl.ANY)
MIB = 1024 * 1024
LANES = 128


def in_hbm(*arrays):
    return [pltpu.with_memory_space_constraint(array, pltpu.HBM) for array in arrays]


def bf16(*shape):
    return jax.ShapeDtypeStruct(shape, jnp.bfloat16)


def at_depth(hop):
    z = lax.axis_index("dp")
    return jnp.minimum(z, lax.axis_size("dp") - 1 - z) == hop


def first_pull_kernel(
    basis_in_ref, basis_out_ref, query_in_ref, query_out_ref, out_ref, send_ref, basis_ref, query_ref, turned_ref, sems
):
    rows = out_ref.shape[0]
    features = basis_ref.shape[0]
    block = 512 if features % 512 == 0 else features
    spans = [pl.ds(first, block) for first in range(0, features, block)]

    def copies(from_basis, from_query):
        return [pltpu.make_async_copy(from_query, query_ref, sems.at[0])] + [
            pltpu.make_async_copy(from_basis.at[span], basis_ref.at[span], sems.at[1 + i])
            for i, span in enumerate(spans)
        ]

    side = lax.axis_index("parts")

    @pl.when(side == 0)
    def _():
        for copy in copies(basis_in_ref, query_in_ref):
            copy.start()

    @pl.when(side != 0)
    def _():
        for copy in copies(basis_out_ref, query_out_ref):
            copy.start()

    landed = copies(basis_in_ref, query_in_ref)
    landed[0].wait()
    turned_ref[...] = query_ref[...].T
    first = pl.multiple_of(jnp.where(at_depth(0), 0, turned_ref.shape[0] - rows), rows)
    factors = jnp.concatenate([turned_ref[:rows], turned_ref[pl.ds(first, rows)]], axis=0)
    for copy, span in zip(landed[1:], spans):
        copy.wait()
        pulled = lax.dot_general(factors, basis_ref[span], NT, preferred_element_type=jnp.float32)
        pulled = pulled.astype(jnp.bfloat16)
        out_ref[:, span] = pulled[:rows]
        send_ref[:, span] = pulled[rows:]


def first_pull(basis_in, basis_out, query_in, query_out, rows):
    features, depth = basis_in.shape
    spread = query_in.shape[1]
    blocks = features // 512 if features % 512 == 0 else 1
    out, send, basis, _, turned = pl.pallas_call(
        first_pull_kernel,
        out_shape=[bf16(rows, features)] * 2 + [bf16(features, depth), bf16(depth, spread), bf16(spread, depth)],
        in_specs=[HBM] * 4,
        out_specs=[VMEM] * 5,
        scratch_shapes=[pltpu.SemaphoreType.DMA((1 + blocks,))],
        compiler_params=pltpu.CompilerParams(vmem_limit_bytes=16 * MIB),
    )(*in_hbm(basis_in, basis_out, query_in, query_out))
    return out, send, basis, turned


def pull_kernel(turned_ref, basis_ref, after_ref, *outs):
    rows, features = outs[0].shape
    block = 512 if features % 512 == 0 else features
    for i in range(features // block):
        pulled = lax.dot_general(
            turned_ref[rows:], basis_ref[i * block : (i + 1) * block], NT, preferred_element_type=jnp.float32
        ).astype(jnp.bfloat16)
        for c, out in enumerate(outs):
            out[:, i * block : (i + 1) * block] = pulled[c * rows : (c + 1) * rows]


def pull(after, turned, basis, rows):
    chunks = turned.shape[0] // rows - 1
    return pl.pallas_call(
        pull_kernel,
        out_shape=[bf16(rows, basis.shape[0])] * chunks,
        in_specs=[VMEM, VMEM, ANY],
        out_specs=[VMEM] * chunks,
        compiler_params=pltpu.CompilerParams(vmem_limit_bytes=16 * MIB),
    )(turned, basis, after)


def deal_kernel(acts_ref, grads_ref, after_ref, *rest):
    outs, sems = rest[:-1], rest[-1]

    def copies(mine, theirs):
        pairs, first = [(mine, outs[0])], 0
        for out in outs[1:]:
            pairs.append((theirs.at[:, pl.ds(first, out.shape[1])], out))
            first += out.shape[1]
        return [pltpu.make_async_copy(source, target, sems.at[i]) for i, (source, target) in enumerate(pairs)]

    side = lax.axis_index("parts")

    @pl.when(side == 0)
    def _():
        for copy in copies(acts_ref, grads_ref):
            copy.start()

    @pl.when(side != 0)
    def _():
        for copy in copies(grads_ref, acts_ref):
            copy.start()

    for copy in copies(acts_ref, grads_ref):
        copy.wait()


def deal(after, acts, grads):
    tokens, features = acts.shape
    larger = features * 3 // 4
    widths = [larger, features - larger] if larger % LANES == 0 else [features]
    out = pl.pallas_call(
        deal_kernel,
        out_shape=[bf16(tokens, features)] + [bf16(tokens, width) for width in widths],
        in_specs=[HBM, HBM, ANY],
        out_specs=[VMEM] * (1 + len(widths)),
        scratch_shapes=[pltpu.SemaphoreType.DMA((1 + len(widths),))],
        compiler_params=pltpu.CompilerParams(vmem_limit_bytes=8 * MIB),
    )(*in_hbm(acts, grads), after)
    return out[0], out[1:]


def write_send(later_ref, value_ref, send_ref):
    @pl.when(at_depth(0))
    def _():
        send_ref[...] = later_ref[...]

    @pl.when(jnp.logical_not(at_depth(0)))
    def _():
        send_ref[...] = value_ref[...]


def pair_kernel(mine_ref, came_ref, early_ref, after_ref, out_ref):
    @pl.when(at_depth(0))
    def _():
        out_ref[...] = (mine_ref[...].astype(jnp.float32) + early_ref[...].astype(jnp.float32)).astype(jnp.bfloat16)

    @pl.when(jnp.logical_not(at_depth(0)))
    def _():
        out_ref[...] = (mine_ref[...].astype(jnp.float32) + came_ref[...].astype(jnp.float32)).astype(jnp.bfloat16)


def pair(after, mine, came, early):
    return pl.pallas_call(
        pair_kernel,
        out_shape=bf16(*mine.shape),
        in_specs=[VMEM, VMEM, VMEM, ANY],
        out_specs=VMEM,
        compiler_params=pltpu.CompilerParams(vmem_limit_bytes=8 * MIB),
    )(mine, came, early, after)


def total_kernel(shared, mine_ref, came_ref, after_ref, *rest):
    mine = mine_ref[...].astype(jnp.float32) + came_ref[...].astype(jnp.float32)
    rest[-1][...] = mine.astype(jnp.bfloat16)
    if shared:
        write_send(rest[0], rest[2], rest[1])
    elif len(rest) == 3:
        rest[1][...] = rest[0][...]


def total(after, mine, came, later=None, shared=False):
    extra = [] if later is None else [later]
    out = pl.pallas_call(
        functools.partial(total_kernel, shared),
        out_shape=[bf16(*a.shape) for a in extra + [mine]],
        in_specs=[VMEM, VMEM, ANY] + [VMEM] * len(extra),
        out_specs=[VMEM] * (1 + len(extra)),
        compiler_params=pltpu.CompilerParams(vmem_limit_bytes=8 * MIB),
    )(mine, came, after, *extra)
    return out[-1], (out[0] if extra else None)


def take_kernel(hop, shared, mine_ref, came_ref, after_ref, *rest):
    @pl.when(at_depth(hop))
    def _():
        rest[-1][...] = came_ref[...]

    @pl.when(jnp.logical_not(at_depth(hop)))
    def _():
        rest[-1][...] = mine_ref[...]

    if shared:
        write_send(rest[0], rest[2], rest[1])


def take(after, hop, mine, came, later=None):
    extra = [] if later is None else [later]
    out = pl.pallas_call(
        functools.partial(take_kernel, hop, later is not None),
        out_shape=[bf16(*a.shape) for a in extra + [mine]],
        in_specs=[VMEM, VMEM, ANY] + [VMEM] * len(extra),
        out_specs=[VMEM] * (1 + len(extra)),
        compiler_params=pltpu.CompilerParams(vmem_limit_bytes=8 * MIB),
    )(mine, came, after, *extra)
    return out[-1], (out[0] if extra else None)


def project_kernel(parts, after_ref, *rest):
    factors = jnp.concatenate([ref[...] for ref in rest[parts:-1]], axis=0)
    projected, first = 0.0, 0
    for ref in rest[:parts]:
        width = ref.shape[1]
        projected += lax.dot_general(
            factors[:, first : first + width], ref[...], NT, preferred_element_type=jnp.float32
        )
        first += width
    rest[-1][...] = projected.astype(rest[-1].dtype)


def project(after, factors, tokens, dtype):
    rows = sum(chunk.shape[0] for chunk in factors)
    return pl.pallas_call(
        functools.partial(project_kernel, len(tokens)),
        out_shape=jax.ShapeDtypeStruct((rows, tokens[0].shape[0]), dtype),
        in_specs=[ANY] + [VMEM] * (len(tokens) + len(factors)),
        out_specs=VMEM,
        compiler_params=pltpu.CompilerParams(vmem_limit_bytes=16 * MIB),
    )(after, *tokens, *factors)


def score_kernel(count, counts_ref, *refs):
    out_ref = refs[-1]
    own = jnp.concatenate([ref[...] for ref in refs[:count]], axis=0)
    other = jnp.concatenate([ref[...] for ref in refs[count : 2 * count]], axis=0)
    product = own * other.astype(jnp.float32)
    queries, tokens = product.shape[0] // RANK, product.shape[1]
    scores = jnp.sum(product.reshape(queries, RANK, tokens), axis=1) * RANK ** (-0.5)
    out_ref[...] = jnp.zeros(out_ref.shape, jnp.float32)
    out_ref[:, :tokens] = scores
    position = lax.broadcasted_iota(jnp.int32, scores.shape, 1)
    docs = counts_ref.shape[1]
    column = lax.broadcasted_iota(jnp.int32, (queries, docs), 1)
    pooled = jnp.zeros((queries, docs), jnp.float32)
    start = jnp.int32(0)
    for k in range(docs):
        count = counts_ref[0, k]
        inside = (position >= start) & (position < start + count)
        found = jnp.sum(jnp.where(inside, scores, 0.0), axis=1, keepdims=True)
        root = jnp.sqrt(jnp.full((1, 1), count, jnp.int32).astype(jnp.float32))
        pooled = jnp.where(column == k, found / root, pooled)
        start = start + count
    out_ref[:, tokens : tokens + pooled.shape[1]] = pooled


def score(counts, own, other):
    rows = sum(piece.shape[0] for piece in own)
    width = (own[0].shape[1] + counts.shape[1] + LANES - 1) // LANES * LANES
    return pl.pallas_call(
        functools.partial(score_kernel, len(own)),
        out_shape=jax.ShapeDtypeStruct((rows // RANK, width), jnp.float32),
        in_specs=[pl.BlockSpec(memory_space=pltpu.SMEM)] + [VMEM] * (2 * len(own)),
        out_specs=VMEM,
        compiler_params=pltpu.CompilerParams(vmem_limit_bytes=16 * MIB),
    )(counts, *own, *other)


def chunk_rows(spread):
    return spread // 8 if spread % 128 == 0 else RANK


def is_power(number):
    return number & (number - 1) == 0


def per_device(
    acts,
    grads,
    basis_in,
    output_eigen_basis,
    query_in,
    query_out,
    doc_counts,
    pair_query,
    pair_device,
    pair_doc,
):
    n = lax.axis_size("dp")
    layers = lax.axis_size("layer")
    z = lax.axis_index("dp")
    spread = query_in.shape[2]
    queries = spread // RANK
    half = n // 2
    rows = chunk_rows(spread)
    chunks = spread // rows

    first, send, basis, turned = first_pull(
        basis_in[0], output_eigen_basis[0], query_in[0], query_out[0], rows
    )
    own = [first] + list(pull(first, turned, basis, rows))
    tokens, theirs = deal(own[-1], acts[0], grads[0])
    swap = [(0, 1), (1, 0)]

    stages = [("in", hop) for hop in range(half - 1)] + [("mid", 0)]
    stages += [("out", hop) for hop in range(half - 2, -1, -1)]
    last = len(stages) - 1

    def transfer(kinds, hop, value):
        pairs = []
        if "in" in kinds:
            pairs += [(hop, hop + 1), (n - 1 - hop, n - 2 - hop)]
        if "mid" in kinds:
            pairs += [(half - 1, half), (half, half - 1)]
        if "out" in kinds:
            pairs += [(hop + 1, hop), (n - 2 - hop, n - 1 - hop)]
        return lax.ppermute(value, "dp", pairs)

    short = n == 4
    part, came = list(own), [None] * chunks
    ahead = min(2, chunks)
    early = came[0] = transfer(("in", "out") if short else ("in",), 0, send)
    for c in range(1, ahead):
        came[c] = transfer(("in",), 0, part[c])
    others = [lax.ppermute(piece, "parts", swap) for piece in theirs]
    after = own[0]
    waiting, mine, back = [], [], []

    def project_waiting(after):
        factors = [factor for _, factor in sorted(waiting, key=lambda entry: entry[0])]
        away = project(after, factors, others, jnp.bfloat16)
        back.append(lax.ppermute(away, "parts", swap))
        mine.append(project(away, factors, [tokens], jnp.float32))
        waiting.clear()
        return mine[-1]

    swapped = set()
    turns = chunks + last - short
    for turn in range(turns):
        steps = [(s, turn - s) for s in range(last) if 0 <= turn - s < chunks]
        due = [c for c in range(chunks) if c + last + (c in swapped) == turn]
        for s, c in steps + [(last, c) for c in due]:
            kind, hop = stages[s]
            if short and c == chunks - 1:
                if s == 0:
                    after = part[c] = pair(after, own[c], came[c], early)
                    came[c] = lax.ppermute(part[c], "dp", [(i, i ^ 2) for i in range(n)])
                elif s == 1:
                    part[c], _ = total(after, part[c], came[c])
                    after = part[c]
                    waiting.append((c, part[c]))
                continue
            later = turn + ahead if turn + ahead < chunks else None
            if turn >= last - 1:
                use = later if s == last - 1 else None
            else:
                use = later if s == 0 else None
            shared = use is not None and turn >= last - 1
            chunk = None if use is None else own[use]
            if kind == "out":
                part[c], send = take(after, hop, part[c], came[c], chunk)
            else:
                part[c], send = total(after, part[c], came[c], chunk, shared)
            after = part[c]
            if shared:
                came[c] = came[use] = transfer(("in", "out"), 0, send)
                swapped.add(c)
                continue
            if use is not None:
                came[use] = transfer(stages[0][:1], stages[0][1], send)
            if s < last:
                came[c] = transfer(stages[s + 1][:1], stages[s + 1][1], part[c])
            else:
                waiting.append((c, part[c]))
        if turn >= turns - 2 and waiting:
            after = project_waiting(after)

    scores = score(doc_counts, mine, back)
    if not is_power(layers):
        scores = lax.psum(scores, "layer")
    else:
        for step in [1 << k for k in range(layers.bit_length() - 1)]:
            scores = scores + lax.ppermute(scores, "layer", [(i, i ^ step) for i in range(layers)])
    tokens_here, docs = acts.shape[1], doc_counts.shape[1]
    token_scores, pooled = scores[:, :tokens_here], scores[:, tokens_here : tokens_here + docs]

    cells = queries * docs
    flat = pooled.reshape(1, cells)
    target = pair_device[:, 0]
    cell = pair_query * docs + pair_doc
    if n <= 8 and is_power(n):
        table = jnp.concatenate(
            [flat] + [lax.ppermute(flat, "dp", [(i, i ^ k) for i in range(n)]) for k in range(1, n)], axis=1
        )
        column = (z ^ target) * cells + cell
    else:
        table = lax.all_gather(flat, "dp", axis=1, tiled=True)
        column = target * cells + cell
    hit = column[:, None] == jnp.arange(n * cells, dtype=jnp.int32)[None, :]
    pair_scores = jnp.sum(jnp.where(hit, table, 0.0), axis=1)
    return (token_scores, pair_scores)


def solution(mesh):
    in_specs = (
        P("layer", ("parts", "dp"), None),
        P("layer", ("parts", "dp"), None),
        P("layer", None, "dp"),
        P("layer", None, "dp"),
        P("layer", "dp", None),
        P("layer", "dp", None),
        P(("parts", "dp"), None),
        P(("parts", "dp")),
        P(("parts", "dp"), None),
        P(("parts", "dp")),
    )
    out_specs = (P(None, ("parts", "dp")), P(("parts", "dp")))
    return jax.shard_map(
        per_device, mesh=mesh, in_specs=in_specs, out_specs=out_specs, check_vma=False
    )
```

```python
import functools

import jax
import jax.numpy as jnp
from jax import lax
from jax.experimental import pallas as pl
from jax.experimental.pallas import tpu as pltpu
from jax.sharding import PartitionSpec as P

RANK = 32
NT = (((1,), (1,)), ((), ()))


VMEM = pl.BlockSpec(memory_space=pltpu.VMEM)
HBM = pl.BlockSpec(memory_space=pltpu.HBM)
ANY = pl.BlockSpec(memory_space=pl.ANY)
MIB = 1024 * 1024
LANES = 128


def in_hbm(*arrays):
    return [pltpu.with_memory_space_constraint(array, pltpu.HBM) for array in arrays]


def bf16(*shape):
    return jax.ShapeDtypeStruct(shape, jnp.bfloat16)


def at_depth(hop):
    z = lax.axis_index("dp")
    return jnp.minimum(z, lax.axis_size("dp") - 1 - z) == hop


def first_pull_kernel(
    basis_in_ref, basis_out_ref, query_in_ref, query_out_ref, out_ref, send_ref, basis_ref, query_ref, turned_ref, sems
):
    rows = out_ref.shape[0]
    features = basis_ref.shape[0]
    block = 512 if features % 512 == 0 else features
    spans = [pl.ds(first, block) for first in range(0, features, block)]

    def copies(from_basis, from_query):
        return [pltpu.make_async_copy(from_query, query_ref, sems.at[0])] + [
            pltpu.make_async_copy(from_basis.at[span], basis_ref.at[span], sems.at[1 + i])
            for i, span in enumerate(spans)
        ]

    side = lax.axis_index("parts")

    @pl.when(side == 0)
    def _():
        for copy in copies(basis_in_ref, query_in_ref):
            copy.start()

    @pl.when(side != 0)
    def _():
        for copy in copies(basis_out_ref, query_out_ref):
            copy.start()

    landed = copies(basis_in_ref, query_in_ref)
    landed[0].wait()
    turned_ref[...] = query_ref[...].T
    first = pl.multiple_of(jnp.where(at_depth(0), 0, turned_ref.shape[0] - rows), rows)
    factors = jnp.concatenate([turned_ref[:rows], turned_ref[pl.ds(first, rows)]], axis=0)
    for copy, span in zip(landed[1:], spans):
        copy.wait()
        pulled = lax.dot_general(factors, basis_ref[span], NT, preferred_element_type=jnp.float32)
        pulled = pulled.astype(jnp.bfloat16)
        out_ref[:, span] = pulled[:rows]
        send_ref[:, span] = pulled[rows:]


def first_pull(basis_in, basis_out, query_in, query_out, rows):
    features, depth = basis_in.shape
    spread = query_in.shape[1]
    blocks = features // 512 if features % 512 == 0 else 1
    out, send, basis, _, turned = pl.pallas_call(
        first_pull_kernel,
        out_shape=[bf16(rows, features)] * 2 + [bf16(features, depth), bf16(depth, spread), bf16(spread, depth)],
        in_specs=[HBM] * 4,
        out_specs=[VMEM] * 5,
        scratch_shapes=[pltpu.SemaphoreType.DMA((1 + blocks,))],
        compiler_params=pltpu.CompilerParams(vmem_limit_bytes=16 * MIB),
    )(*in_hbm(basis_in, basis_out, query_in, query_out))
    return out, send, basis, turned


def pull_kernel(turned_ref, basis_ref, after_ref, *outs):
    rows, features = outs[0].shape
    block = 512 if features % 512 == 0 else features
    for i in range(features // block):
        pulled = lax.dot_general(
            turned_ref[rows:], basis_ref[i * block : (i + 1) * block], NT, preferred_element_type=jnp.float32
        ).astype(jnp.bfloat16)
        for c, out in enumerate(outs):
            out[:, i * block : (i + 1) * block] = pulled[c * rows : (c + 1) * rows]


def pull(after, turned, basis, rows):
    chunks = turned.shape[0] // rows - 1
    return pl.pallas_call(
        pull_kernel,
        out_shape=[bf16(rows, basis.shape[0])] * chunks,
        in_specs=[VMEM, VMEM, ANY],
        out_specs=[VMEM] * chunks,
        compiler_params=pltpu.CompilerParams(vmem_limit_bytes=16 * MIB),
    )(turned, basis, after)


def deal_kernel(acts_ref, grads_ref, after_ref, *rest):
    outs, sems = rest[:-1], rest[-1]

    def copies(mine, theirs):
        pairs, first = [(mine, outs[0])], 0
        for out in outs[1:]:
            pairs.append((theirs.at[:, pl.ds(first, out.shape[1])], out))
            first += out.shape[1]
        return [pltpu.make_async_copy(source, target, sems.at[i]) for i, (source, target) in enumerate(pairs)]

    side = lax.axis_index("parts")

    @pl.when(side == 0)
    def _():
        for copy in copies(acts_ref, grads_ref):
            copy.start()

    @pl.when(side != 0)
    def _():
        for copy in copies(grads_ref, acts_ref):
            copy.start()

    for copy in copies(acts_ref, grads_ref):
        copy.wait()


def deal(after, acts, grads):
    tokens, features = acts.shape
    larger = features * 3 // 4
    widths = [larger, features - larger] if larger % LANES == 0 else [features]
    out = pl.pallas_call(
        deal_kernel,
        out_shape=[bf16(tokens, features)] + [bf16(tokens, width) for width in widths],
        in_specs=[HBM, HBM, ANY],
        out_specs=[VMEM] * (1 + len(widths)),
        scratch_shapes=[pltpu.SemaphoreType.DMA((1 + len(widths),))],
        compiler_params=pltpu.CompilerParams(vmem_limit_bytes=8 * MIB),
    )(*in_hbm(acts, grads), after)
    return out[0], out[1:]


def write_send(later_ref, value_ref, send_ref):
    @pl.when(at_depth(0))
    def _():
        send_ref[...] = later_ref[...]

    @pl.when(jnp.logical_not(at_depth(0)))
    def _():
        send_ref[...] = value_ref[...]


def pair_kernel(mine_ref, came_ref, early_ref, after_ref, out_ref):
    @pl.when(at_depth(0))
    def _():
        out_ref[...] = (mine_ref[...].astype(jnp.float32) + early_ref[...].astype(jnp.float32)).astype(jnp.bfloat16)

    @pl.when(jnp.logical_not(at_depth(0)))
    def _():
        out_ref[...] = (mine_ref[...].astype(jnp.float32) + came_ref[...].astype(jnp.float32)).astype(jnp.bfloat16)


def pair(after, mine, came, early):
    return pl.pallas_call(
        pair_kernel,
        out_shape=bf16(*mine.shape),
        in_specs=[VMEM, VMEM, VMEM, ANY],
        out_specs=VMEM,
        compiler_params=pltpu.CompilerParams(vmem_limit_bytes=8 * MIB),
    )(mine, came, early, after)


def total_kernel(shared, mine_ref, came_ref, after_ref, *rest):
    mine = mine_ref[...].astype(jnp.float32) + came_ref[...].astype(jnp.float32)
    rest[-1][...] = mine.astype(jnp.bfloat16)
    if shared:
        write_send(rest[0], rest[2], rest[1])
    else:
        count = len(rest) // 2
        for later_ref, send_ref in zip(rest[:count], rest[count:]):
            send_ref[...] = later_ref[...]


def total(after, mine, came, extra=(), shared=False):
    extra = list(extra)
    out = pl.pallas_call(
        functools.partial(total_kernel, shared),
        out_shape=[bf16(*a.shape) for a in extra + [mine]],
        in_specs=[VMEM, VMEM, ANY] + [VMEM] * len(extra),
        out_specs=[VMEM] * (1 + len(extra)),
        compiler_params=pltpu.CompilerParams(vmem_limit_bytes=8 * MIB),
    )(mine, came, after, *extra)
    return out[-1], out[:-1]


def take_kernel(hop, shared, mine_ref, came_ref, after_ref, *rest):
    @pl.when(at_depth(hop))
    def _():
        rest[-1][...] = came_ref[...]

    @pl.when(jnp.logical_not(at_depth(hop)))
    def _():
        rest[-1][...] = mine_ref[...]

    if shared:
        write_send(rest[0], rest[2], rest[1])


def take(after, hop, mine, came, extra=()):
    extra = list(extra)
    out = pl.pallas_call(
        functools.partial(take_kernel, hop, len(extra) > 0),
        out_shape=[bf16(*a.shape) for a in extra + [mine]],
        in_specs=[VMEM, VMEM, ANY] + [VMEM] * len(extra),
        out_specs=[VMEM] * (1 + len(extra)),
        compiler_params=pltpu.CompilerParams(vmem_limit_bytes=8 * MIB),
    )(mine, came, after, *extra)
    return out[-1], out[:-1]


def project_kernel(parts, after_ref, *rest):
    factors = jnp.concatenate([ref[...] for ref in rest[parts:-1]], axis=0)
    projected, first = 0.0, 0
    for ref in rest[:parts]:
        width = ref.shape[1]
        projected += lax.dot_general(
            factors[:, first : first + width], ref[...], NT, preferred_element_type=jnp.float32
        )
        first += width
    rest[-1][...] = projected.astype(rest[-1].dtype)


def project(after, factors, tokens, dtype):
    rows = sum(chunk.shape[0] for chunk in factors)
    return pl.pallas_call(
        functools.partial(project_kernel, len(tokens)),
        out_shape=jax.ShapeDtypeStruct((rows, tokens[0].shape[0]), dtype),
        in_specs=[ANY] + [VMEM] * (len(tokens) + len(factors)),
        out_specs=VMEM,
        compiler_params=pltpu.CompilerParams(vmem_limit_bytes=16 * MIB),
    )(after, *tokens, *factors)


def score_kernel(count, counts_ref, *refs):
    out_ref = refs[-1]
    own = jnp.concatenate([ref[...] for ref in refs[:count]], axis=0)
    other = jnp.concatenate([ref[...] for ref in refs[count : 2 * count]], axis=0)
    product = own * other.astype(jnp.float32)
    queries, tokens = product.shape[0] // RANK, product.shape[1]
    scores = jnp.sum(product.reshape(queries, RANK, tokens), axis=1) * RANK ** (-0.5)
    out_ref[...] = jnp.zeros(out_ref.shape, jnp.float32)
    out_ref[:, :tokens] = scores
    position = lax.broadcasted_iota(jnp.int32, scores.shape, 1)
    docs = counts_ref.shape[1]
    column = lax.broadcasted_iota(jnp.int32, (queries, docs), 1)
    pooled = jnp.zeros((queries, docs), jnp.float32)
    start = jnp.int32(0)
    for k in range(docs):
        count = counts_ref[0, k]
        inside = (position >= start) & (position < start + count)
        found = jnp.sum(jnp.where(inside, scores, 0.0), axis=1, keepdims=True)
        root = jnp.sqrt(jnp.full((1, 1), count, jnp.int32).astype(jnp.float32))
        pooled = jnp.where(column == k, found / root, pooled)
        start = start + count
    out_ref[:, tokens : tokens + pooled.shape[1]] = pooled


def score(counts, own, other):
    rows = sum(piece.shape[0] for piece in own)
    width = (own[0].shape[1] + counts.shape[1] + LANES - 1) // LANES * LANES
    return pl.pallas_call(
        functools.partial(score_kernel, len(own)),
        out_shape=jax.ShapeDtypeStruct((rows // RANK, width), jnp.float32),
        in_specs=[pl.BlockSpec(memory_space=pltpu.SMEM)] + [VMEM] * (2 * len(own)),
        out_specs=VMEM,
        compiler_params=pltpu.CompilerParams(vmem_limit_bytes=16 * MIB),
    )(counts, *own, *other)


def chunk_rows(spread):
    return spread // 8 if spread % 128 == 0 else RANK


def is_power(number):
    return number & (number - 1) == 0


def per_device(
    acts,
    grads,
    basis_in,
    output_eigen_basis,
    query_in,
    query_out,
    doc_counts,
    pair_query,
    pair_device,
    pair_doc,
):
    n = lax.axis_size("dp")
    layers = lax.axis_size("layer")
    z = lax.axis_index("dp")
    spread = query_in.shape[2]
    queries = spread // RANK
    half = n // 2
    rows = chunk_rows(spread)
    chunks = spread // rows

    first, send, basis, turned = first_pull(
        basis_in[0], output_eigen_basis[0], query_in[0], query_out[0], rows
    )
    own = [first] + list(pull(first, turned, basis, rows))
    tokens, theirs = deal(own[-1], acts[0], grads[0])
    swap = [(0, 1), (1, 0)]

    stages = [("in", hop) for hop in range(half - 1)] + [("mid", 0)]
    stages += [("out", hop) for hop in range(half - 2, -1, -1)]
    last = len(stages) - 1

    def transfer(kinds, hop, value):
        pairs = []
        if "in" in kinds:
            pairs += [(hop, hop + 1), (n - 1 - hop, n - 2 - hop)]
        if "mid" in kinds:
            pairs += [(half - 1, half), (half, half - 1)]
        if "out" in kinds:
            pairs += [(hop + 1, hop), (n - 2 - hop, n - 1 - hop)]
        return lax.ppermute(value, "dp", pairs)

    short = n == 4
    part, came = list(own), [None] * chunks
    ahead, flying = min(2, chunks), 3
    early = came[0] = transfer(("in", "out") if short else ("in",), 0, send)
    for c in range(1, ahead):
        came[c] = transfer(("in",), 0, part[c])
    others = [lax.ppermute(piece, "parts", swap) for piece in theirs]
    after = own[0]
    waiting, mine, back = [], [], []

    def project_waiting(after):
        factors = [factor for _, factor in sorted(waiting, key=lambda entry: entry[0])]
        away = project(after, factors, others, jnp.bfloat16)
        back.append(lax.ppermute(away, "parts", swap))
        mine.append(project(away, factors, [tokens], jnp.float32))
        waiting.clear()
        return mine[-1]

    swapped = set()
    turns = chunks + last - short
    for turn in range(turns):
        steps = [(s, turn - s) for s in range(last) if 0 <= turn - s < chunks]
        due = [c for c in range(chunks) if c + last + (flying - 1) * (c in swapped) == turn]
        for s, c in steps + [(last, c) for c in due]:
            kind, hop = stages[s]
            if short and c == chunks - 1:
                if s == 0:
                    after = part[c] = pair(after, own[c], came[c], early)
                    came[c] = lax.ppermute(part[c], "dp", [(i, i ^ 2) for i in range(n)])
                elif s == 1:
                    part[c], _ = total(after, part[c], came[c])
                    after = part[c]
                    waiting.append((c, part[c]))
                continue
            later = range(ahead, min(flying + 1, chunks)) if turn == 0 else range(turn + flying, min(turn + flying + 1, chunks))
            shared = turn >= last - 1 and turn > 0 and s == last - 1 and len(later) == 1
            use = later if shared or (s == 0 and (turn < last - 1 or turn == 0)) else ()
            extra = [own[i] for i in use]
            if kind == "out":
                part[c], sends = take(after, hop, part[c], came[c], extra)
            else:
                part[c], sends = total(after, part[c], came[c], extra, shared)
            after = part[c]
            if shared:
                came[c] = came[use[0]] = transfer(("in", "out"), 0, sends[0])
                swapped.add(c)
                continue
            for i, send in zip(use, sends):
                came[i] = transfer(stages[0][:1], stages[0][1], send)
            if s < last:
                came[c] = transfer(stages[s + 1][:1], stages[s + 1][1], part[c])
            else:
                waiting.append((c, part[c]))
        if turn >= turns - 2 and waiting:
            after = project_waiting(after)

    scores = score(doc_counts, mine, back)
    if not is_power(layers):
        scores = lax.psum(scores, "layer")
    else:
        for step in [1 << k for k in range(layers.bit_length() - 1)]:
            scores = scores + lax.ppermute(scores, "layer", [(i, i ^ step) for i in range(layers)])
    tokens_here, docs = acts.shape[1], doc_counts.shape[1]
    token_scores, pooled = scores[:, :tokens_here], scores[:, tokens_here : tokens_here + docs]

    cells = queries * docs
    flat = pooled.reshape(1, cells)
    target = pair_device[:, 0]
    cell = pair_query * docs + pair_doc
    if n <= 8 and is_power(n):
        table = jnp.concatenate(
            [flat] + [lax.ppermute(flat, "dp", [(i, i ^ k) for i in range(n)]) for k in range(1, n)], axis=1
        )
        column = (z ^ target) * cells + cell
    else:
        table = lax.all_gather(flat, "dp", axis=1, tiled=True)
        column = target * cells + cell
    hit = column[:, None] == jnp.arange(n * cells, dtype=jnp.int32)[None, :]
    pair_scores = jnp.sum(jnp.where(hit, table, 0.0), axis=1)
    return (token_scores, pair_scores)


def solution(mesh):
    in_specs = (
        P("layer", ("parts", "dp"), None),
        P("layer", ("parts", "dp"), None),
        P("layer", None, "dp"),
        P("layer", None, "dp"),
        P("layer", "dp", None),
        P("layer", "dp", None),
        P(("parts", "dp"), None),
        P(("parts", "dp")),
        P(("parts", "dp"), None),
        P(("parts", "dp")),
    )
    out_specs = (P(None, ("parts", "dp")), P(("parts", "dp")))
    return jax.shard_map(
        per_device, mesh=mesh, in_specs=in_specs, out_specs=out_specs, check_vma=False
    )
```

```python
import functools

import jax
import jax.numpy as jnp
from jax import lax
from jax.experimental import pallas as pl
from jax.experimental.pallas import tpu as pltpu
from jax.sharding import PartitionSpec as P

RANK = 32
NT = (((1,), (1,)), ((), ()))


VMEM = pl.BlockSpec(memory_space=pltpu.VMEM)
HBM = pl.BlockSpec(memory_space=pltpu.HBM)
ANY = pl.BlockSpec(memory_space=pl.ANY)
MIB = 1024 * 1024
LANES = 128
BEFORE = 3


def in_hbm(*arrays):
    return [pltpu.with_memory_space_constraint(array, pltpu.HBM) for array in arrays]


def bf16(*shape):
    return jax.ShapeDtypeStruct(shape, jnp.bfloat16)


def at_depth(hop):
    z = lax.axis_index("dp")
    return jnp.minimum(z, lax.axis_size("dp") - 1 - z) == hop


def first_pull_kernel(
    basis_in_ref, basis_out_ref, query_in_ref, query_out_ref, out_ref, send_ref, basis_ref, query_ref, turned_ref, sems
):
    rows = out_ref.shape[0]
    features = basis_ref.shape[0]
    block = 512 if features % 512 == 0 else features
    spans = [pl.ds(first, block) for first in range(0, features, block)]

    def copies(from_basis, from_query):
        return [pltpu.make_async_copy(from_query, query_ref, sems.at[0])] + [
            pltpu.make_async_copy(from_basis.at[span], basis_ref.at[span], sems.at[1 + i])
            for i, span in enumerate(spans)
        ]

    side = lax.axis_index("parts")

    def start(which):
        @pl.when(side == 0)
        def _():
            for copy in copies(basis_in_ref, query_in_ref)[which]:
                copy.start()

        @pl.when(side != 0)
        def _():
            for copy in copies(basis_out_ref, query_out_ref)[which]:
                copy.start()

    start(slice(0, 1 + BEFORE))
    landed = copies(basis_in_ref, query_in_ref)
    landed[0].wait()
    turned_ref[...] = query_ref[...].T
    first = pl.multiple_of(jnp.where(at_depth(0), 0, turned_ref.shape[0] - rows), rows)
    factors = jnp.concatenate([turned_ref[:rows], turned_ref[pl.ds(first, rows)]], axis=0)
    for i, (copy, span) in enumerate(zip(landed[1:], spans)):
        copy.wait()
        start(slice(1 + BEFORE + i, 2 + BEFORE + i))
        pulled = lax.dot_general(factors, basis_ref[span], NT, preferred_element_type=jnp.float32)
        pulled = pulled.astype(jnp.bfloat16)
        out_ref[:, span] = pulled[:rows]
        send_ref[:, span] = pulled[rows:]


def first_pull(basis_in, basis_out, query_in, query_out, rows):
    features, depth = basis_in.shape
    spread = query_in.shape[1]
    blocks = features // 512 if features % 512 == 0 else 1
    out, send, basis, _, turned = pl.pallas_call(
        first_pull_kernel,
        out_shape=[bf16(rows, features)] * 2 + [bf16(features, depth), bf16(depth, spread), bf16(spread, depth)],
        in_specs=[HBM] * 4,
        out_specs=[VMEM] * 5,
        scratch_shapes=[pltpu.SemaphoreType.DMA((1 + blocks,))],
        compiler_params=pltpu.CompilerParams(vmem_limit_bytes=16 * MIB),
    )(*in_hbm(basis_in, basis_out, query_in, query_out))
    return out, send, basis, turned


def pull_kernel(turned_ref, basis_ref, after_ref, *outs):
    rows, features = outs[0].shape
    block = 512 if features % 512 == 0 else features
    for i in range(features // block):
        pulled = lax.dot_general(
            turned_ref[rows:], basis_ref[i * block : (i + 1) * block], NT, preferred_element_type=jnp.float32
        ).astype(jnp.bfloat16)
        for c, out in enumerate(outs):
            out[:, i * block : (i + 1) * block] = pulled[c * rows : (c + 1) * rows]


def pull(after, turned, basis, rows):
    chunks = turned.shape[0] // rows - 1
    return pl.pallas_call(
        pull_kernel,
        out_shape=[bf16(rows, basis.shape[0])] * chunks,
        in_specs=[VMEM, VMEM, ANY],
        out_specs=[VMEM] * chunks,
        compiler_params=pltpu.CompilerParams(vmem_limit_bytes=16 * MIB),
    )(turned, basis, after)


def deal_kernel(acts_ref, grads_ref, after_ref, *rest):
    outs, sems = rest[:-1], rest[-1]

    def copies(mine, theirs):
        pairs, first = [(mine, outs[0])], 0
        for out in outs[1:]:
            pairs.append((theirs.at[:, pl.ds(first, out.shape[1])], out))
            first += out.shape[1]
        return [pltpu.make_async_copy(source, target, sems.at[i]) for i, (source, target) in enumerate(pairs)]

    side = lax.axis_index("parts")

    @pl.when(side == 0)
    def _():
        for copy in copies(acts_ref, grads_ref):
            copy.start()

    @pl.when(side != 0)
    def _():
        for copy in copies(grads_ref, acts_ref):
            copy.start()

    for copy in copies(acts_ref, grads_ref):
        copy.wait()


def deal(after, acts, grads):
    tokens, features = acts.shape
    larger = features * 17 // 20
    widths = [larger, features - larger] if larger % LANES == 0 else [features]
    out = pl.pallas_call(
        deal_kernel,
        out_shape=[bf16(tokens, features)] + [bf16(tokens, width) for width in widths],
        in_specs=[HBM, HBM, ANY],
        out_specs=[VMEM] * (1 + len(widths)),
        scratch_shapes=[pltpu.SemaphoreType.DMA((1 + len(widths),))],
        compiler_params=pltpu.CompilerParams(vmem_limit_bytes=8 * MIB),
    )(*in_hbm(acts, grads), after)
    return out[0], out[1:]


def write_send(later_ref, value_ref, send_ref):
    @pl.when(at_depth(0))
    def _():
        send_ref[...] = later_ref[...]

    @pl.when(jnp.logical_not(at_depth(0)))
    def _():
        send_ref[...] = value_ref[...]


def pair_kernel(mine_ref, came_ref, early_ref, after_ref, out_ref):
    @pl.when(at_depth(0))
    def _():
        out_ref[...] = (mine_ref[...].astype(jnp.float32) + early_ref[...].astype(jnp.float32)).astype(jnp.bfloat16)

    @pl.when(jnp.logical_not(at_depth(0)))
    def _():
        out_ref[...] = (mine_ref[...].astype(jnp.float32) + came_ref[...].astype(jnp.float32)).astype(jnp.bfloat16)


def pair(after, mine, came, early):
    return pl.pallas_call(
        pair_kernel,
        out_shape=bf16(*mine.shape),
        in_specs=[VMEM, VMEM, VMEM, ANY],
        out_specs=VMEM,
        compiler_params=pltpu.CompilerParams(vmem_limit_bytes=8 * MIB),
    )(mine, came, early, after)


def total_kernel(shared, mine_ref, came_ref, after_ref, *rest):
    mine = mine_ref[...].astype(jnp.float32) + came_ref[...].astype(jnp.float32)
    rest[-1][...] = mine.astype(jnp.bfloat16)
    if shared:
        write_send(rest[0], rest[2], rest[1])
    elif len(rest) == 3:
        rest[1][...] = rest[0][...]


def total(after, mine, came, later=None, shared=False):
    extra = [] if later is None else [later]
    out = pl.pallas_call(
        functools.partial(total_kernel, shared),
        out_shape=[bf16(*a.shape) for a in extra + [mine]],
        in_specs=[VMEM, VMEM, ANY] + [VMEM] * len(extra),
        out_specs=[VMEM] * (1 + len(extra)),
        compiler_params=pltpu.CompilerParams(vmem_limit_bytes=8 * MIB),
    )(mine, came, after, *extra)
    return out[-1], (out[0] if extra else None)


def take_kernel(hop, shared, mine_ref, came_ref, after_ref, *rest):
    @pl.when(at_depth(hop))
    def _():
        rest[-1][...] = came_ref[...]

    @pl.when(jnp.logical_not(at_depth(hop)))
    def _():
        rest[-1][...] = mine_ref[...]

    if shared:
        write_send(rest[0], rest[2], rest[1])


def take(after, hop, mine, came, later=None):
    extra = [] if later is None else [later]
    out = pl.pallas_call(
        functools.partial(take_kernel, hop, later is not None),
        out_shape=[bf16(*a.shape) for a in extra + [mine]],
        in_specs=[VMEM, VMEM, ANY] + [VMEM] * len(extra),
        out_specs=[VMEM] * (1 + len(extra)),
        compiler_params=pltpu.CompilerParams(vmem_limit_bytes=8 * MIB),
    )(mine, came, after, *extra)
    return out[-1], (out[0] if extra else None)


def project_kernel(parts, after_ref, *rest):
    factors = jnp.concatenate([ref[...] for ref in rest[parts:-1]], axis=0)
    projected, first = 0.0, 0
    for ref in rest[:parts]:
        width = ref.shape[1]
        projected += lax.dot_general(
            factors[:, first : first + width], ref[...], NT, preferred_element_type=jnp.float32
        )
        first += width
    rest[-1][...] = projected.astype(rest[-1].dtype)


def project(after, factors, tokens, dtype):
    rows = sum(chunk.shape[0] for chunk in factors)
    return pl.pallas_call(
        functools.partial(project_kernel, len(tokens)),
        out_shape=jax.ShapeDtypeStruct((rows, tokens[0].shape[0]), dtype),
        in_specs=[ANY] + [VMEM] * (len(tokens) + len(factors)),
        out_specs=VMEM,
        compiler_params=pltpu.CompilerParams(vmem_limit_bytes=16 * MIB),
    )(after, *tokens, *factors)


def score_kernel(counts_ref, own_ref, other_ref, *rest):
    done, out_ref = rest[:-1], rest[-1]
    product = own_ref[...] * other_ref[...].astype(jnp.float32)
    queries, tokens = product.shape[0] // RANK, product.shape[1]
    scores = jnp.sum(product.reshape(queries, RANK, tokens), axis=1) * RANK ** (-0.5)
    position = lax.broadcasted_iota(jnp.int32, scores.shape, 1)
    docs = counts_ref.shape[1]
    column = lax.broadcasted_iota(jnp.int32, (queries, docs), 1)
    pooled = jnp.zeros((queries, docs), jnp.float32)
    start = jnp.int32(0)
    for k in range(docs):
        count = counts_ref[0, k]
        inside = (position >= start) & (position < start + count)
        found = jnp.sum(jnp.where(inside, scores, 0.0), axis=1, keepdims=True)
        root = jnp.sqrt(jnp.full((1, 1), count, jnp.int32).astype(jnp.float32))
        pooled = jnp.where(column == k, found / root, pooled)
        start = start + count
    first = 0
    for ref in done:
        out_ref[: ref.shape[0]] = ref[...]
        first = ref.shape[0]
    out_ref[first:] = jnp.zeros((queries, out_ref.shape[1]), jnp.float32)
    out_ref[first:, :tokens] = scores
    out_ref[first:, tokens : tokens + docs] = pooled


def score(counts, own, other, done=()):
    queries = own.shape[0] // RANK + sum(ref.shape[0] for ref in done)
    width = (own.shape[1] + counts.shape[1] + LANES - 1) // LANES * LANES
    return pl.pallas_call(
        score_kernel,
        out_shape=jax.ShapeDtypeStruct((queries, width), jnp.float32),
        in_specs=[pl.BlockSpec(memory_space=pltpu.SMEM)] + [VMEM] * (2 + len(done)),
        out_specs=VMEM,
        compiler_params=pltpu.CompilerParams(vmem_limit_bytes=16 * MIB),
    )(counts, own, other, *done)


def chunk_rows(spread):
    return spread // 8 if spread % 128 == 0 else RANK


def is_power(number):
    return number & (number - 1) == 0


def per_device(
    acts,
    grads,
    basis_in,
    output_eigen_basis,
    query_in,
    query_out,
    doc_counts,
    pair_query,
    pair_device,
    pair_doc,
):
    n = lax.axis_size("dp")
    layers = lax.axis_size("layer")
    z = lax.axis_index("dp")
    spread = query_in.shape[2]
    queries = spread // RANK
    half = n // 2
    rows = chunk_rows(spread)
    chunks = spread // rows

    first, send, basis, turned = first_pull(
        basis_in[0], output_eigen_basis[0], query_in[0], query_out[0], rows
    )
    own = [first] + list(pull(first, turned, basis, rows))
    tokens, theirs = deal(own[-1], acts[0], grads[0])
    swap = [(0, 1), (1, 0)]

    stages = [("in", hop) for hop in range(half - 1)] + [("mid", 0)]
    stages += [("out", hop) for hop in range(half - 2, -1, -1)]
    last = len(stages) - 1

    def transfer(kinds, hop, value):
        pairs = []
        if "in" in kinds:
            pairs += [(hop, hop + 1), (n - 1 - hop, n - 2 - hop)]
        if "mid" in kinds:
            pairs += [(half - 1, half), (half, half - 1)]
        if "out" in kinds:
            pairs += [(hop + 1, hop), (n - 2 - hop, n - 1 - hop)]
        return lax.ppermute(value, "dp", pairs)

    short = n == 4
    part, came = list(own), [None] * chunks
    ahead = min(2, chunks)
    early = came[0] = transfer(("in", "out") if short else ("in",), 0, send)
    for c in range(1, ahead):
        came[c] = transfer(("in",), 0, part[c])
    others = [lax.ppermute(piece, "parts", swap) for piece in theirs]
    after = own[0]
    waiting, mine, back = [], [], []

    def project_waiting(after):
        factors = [factor for _, factor in sorted(waiting, key=lambda entry: entry[0])]
        away = project(after, factors, others, jnp.bfloat16)
        back.append(lax.ppermute(away, "parts", swap))
        mine.append(project(away, factors, [tokens], jnp.float32))
        waiting.clear()
        return mine[-1]

    swapped = set()
    turns = chunks + last - short
    for turn in range(turns):
        steps = [(s, turn - s) for s in range(last) if 0 <= turn - s < chunks]
        due = [c for c in range(chunks) if c + last + (c in swapped) == turn]
        for s, c in steps + [(last, c) for c in due]:
            kind, hop = stages[s]
            if short and c == chunks - 1:
                if s == 0:
                    after = part[c] = pair(after, own[c], came[c], early)
                    came[c] = lax.ppermute(part[c], "dp", [(i, i ^ 2) for i in range(n)])
                elif s == 1:
                    part[c], _ = total(after, part[c], came[c])
                    after = part[c]
                    waiting.append((c, part[c]))
                continue
            later = turn + ahead if turn + ahead < chunks else None
            if turn >= last - 1:
                use = later if s == last - 1 else None
            else:
                use = later if s == 0 else None
            shared = use is not None and turn >= last - 1
            chunk = None if use is None else own[use]
            if kind == "out":
                part[c], send = take(after, hop, part[c], came[c], chunk)
            else:
                part[c], send = total(after, part[c], came[c], chunk, shared)
            after = part[c]
            if shared:
                came[c] = came[use] = transfer(("in", "out"), 0, send)
                swapped.add(c)
                continue
            if use is not None:
                came[use] = transfer(stages[0][:1], stages[0][1], send)
            if s < last:
                came[c] = transfer(stages[s + 1][:1], stages[s + 1][1], part[c])
            else:
                waiting.append((c, part[c]))
        if turn >= turns - 2 and waiting:
            after = project_waiting(after)

    if any(piece.shape[0] % RANK for piece in mine):
        mine, back = [jnp.concatenate(mine, axis=0)], [jnp.concatenate(back, axis=0)]
    done = ()
    for piece, other in zip(mine, back):
        done = (score(doc_counts, piece, other, done),)
    scores = done[0]
    if not is_power(layers):
        scores = lax.psum(scores, "layer")
    else:
        for step in [1 << k for k in range(layers.bit_length() - 1)]:
            scores = scores + lax.ppermute(scores, "layer", [(i, i ^ step) for i in range(layers)])
    tokens_here, docs = acts.shape[1], doc_counts.shape[1]
    token_scores, pooled = scores[:, :tokens_here], scores[:, tokens_here : tokens_here + docs]

    cells = queries * docs
    flat = pooled.reshape(1, cells)
    target = pair_device[:, 0]
    cell = pair_query * docs + pair_doc
    if n <= 8 and is_power(n):
        table = jnp.concatenate(
            [flat] + [lax.ppermute(flat, "dp", [(i, i ^ k) for i in range(n)]) for k in range(1, n)], axis=1
        )
        column = (z ^ target) * cells + cell
    else:
        table = lax.all_gather(flat, "dp", axis=1, tiled=True)
        column = target * cells + cell
    hit = column[:, None] == jnp.arange(n * cells, dtype=jnp.int32)[None, :]
    pair_scores = jnp.sum(jnp.where(hit, table, 0.0), axis=1)
    return (token_scores, pair_scores)


def solution(mesh):
    in_specs = (
        P("layer", ("parts", "dp"), None),
        P("layer", ("parts", "dp"), None),
        P("layer", None, "dp"),
        P("layer", None, "dp"),
        P("layer", "dp", None),
        P("layer", "dp", None),
        P(("parts", "dp"), None),
        P(("parts", "dp")),
        P(("parts", "dp"), None),
        P(("parts", "dp")),
    )
    out_specs = (P(None, ("parts", "dp")), P(("parts", "dp")))
    return jax.shard_map(
        per_device, mesh=mesh, in_specs=in_specs, out_specs=out_specs, check_vma=False
    )
```

```python
import functools

import jax
import jax.numpy as jnp
from jax import lax
from jax.experimental import pallas as pl
from jax.experimental.pallas import tpu as pltpu
from jax.sharding import PartitionSpec as P

RANK = 32
NT = (((1,), (1,)), ((), ()))


VMEM = pl.BlockSpec(memory_space=pltpu.VMEM)
HBM = pl.BlockSpec(memory_space=pltpu.HBM)
ANY = pl.BlockSpec(memory_space=pl.ANY)
MIB = 1024 * 1024
LANES = 128


def in_hbm(*arrays):
    return [pltpu.with_memory_space_constraint(array, pltpu.HBM) for array in arrays]


def bf16(*shape):
    return jax.ShapeDtypeStruct(shape, jnp.bfloat16)


def at_depth(hop):
    z = lax.axis_index("dp")
    return jnp.minimum(z, lax.axis_size("dp") - 1 - z) == hop


def first_pull_kernel(
    basis_in_ref, basis_out_ref, query_in_ref, query_out_ref, out_ref, send_ref, basis_ref, query_ref, turned_ref, sems
):
    rows = out_ref.shape[0]
    features = basis_ref.shape[0]
    block = 512 if features % 512 == 0 else features
    spans = [pl.ds(first, block) for first in range(0, features, block)]

    def copies(from_basis, from_query):
        return [pltpu.make_async_copy(from_query, query_ref, sems.at[0])] + [
            pltpu.make_async_copy(from_basis.at[span], basis_ref.at[span], sems.at[1 + i])
            for i, span in enumerate(spans)
        ]

    side = lax.axis_index("parts")

    @pl.when(side == 0)
    def _():
        for copy in copies(basis_in_ref, query_in_ref):
            copy.start()

    @pl.when(side != 0)
    def _():
        for copy in copies(basis_out_ref, query_out_ref):
            copy.start()

    landed = copies(basis_in_ref, query_in_ref)
    landed[0].wait()
    turned_ref[...] = query_ref[...].T
    first = pl.multiple_of(jnp.where(at_depth(0), 0, turned_ref.shape[0] - rows), rows)
    factors = jnp.concatenate([turned_ref[:rows], turned_ref[pl.ds(first, rows)]], axis=0)
    for copy, span in zip(landed[1:], spans):
        copy.wait()
        pulled = lax.dot_general(factors, basis_ref[span], NT, preferred_element_type=jnp.float32)
        pulled = pulled.astype(jnp.bfloat16)
        out_ref[:, span] = pulled[:rows]
        send_ref[:, span] = pulled[rows:]


def first_pull(basis_in, basis_out, query_in, query_out, rows):
    features, depth = basis_in.shape
    spread = query_in.shape[1]
    blocks = features // 512 if features % 512 == 0 else 1
    out, send, basis, _, turned = pl.pallas_call(
        first_pull_kernel,
        out_shape=[bf16(rows, features)] * 2 + [bf16(features, depth), bf16(depth, spread), bf16(spread, depth)],
        in_specs=[HBM] * 4,
        out_specs=[VMEM] * 5,
        scratch_shapes=[pltpu.SemaphoreType.DMA((1 + blocks,))],
        compiler_params=pltpu.CompilerParams(vmem_limit_bytes=16 * MIB),
    )(*in_hbm(basis_in, basis_out, query_in, query_out))
    return out, send, basis, turned


def pull_kernel(turned_ref, basis_ref, after_ref, *outs):
    rows, features = outs[0].shape
    block = 512 if features % 512 == 0 else features
    for i in range(features // block):
        pulled = lax.dot_general(
            turned_ref[rows:], basis_ref[i * block : (i + 1) * block], NT, preferred_element_type=jnp.float32
        ).astype(jnp.bfloat16)
        for c, out in enumerate(outs):
            out[:, i * block : (i + 1) * block] = pulled[c * rows : (c + 1) * rows]


def pull(after, turned, basis, rows):
    chunks = turned.shape[0] // rows - 1
    return pl.pallas_call(
        pull_kernel,
        out_shape=[bf16(rows, basis.shape[0])] * chunks,
        in_specs=[VMEM, VMEM, ANY],
        out_specs=[VMEM] * chunks,
        compiler_params=pltpu.CompilerParams(vmem_limit_bytes=16 * MIB),
    )(turned, basis, after)


def deal_kernel(acts_ref, grads_ref, after_ref, *rest):
    outs, sems = rest[:-1], rest[-1]

    def copies(mine, theirs):
        pairs, first = [(mine, outs[0])], 0
        for out in outs[1:]:
            pairs.append((theirs.at[:, pl.ds(first, out.shape[1])], out))
            first += out.shape[1]
        return [pltpu.make_async_copy(source, target, sems.at[i]) for i, (source, target) in enumerate(pairs)]

    side = lax.axis_index("parts")

    @pl.when(side == 0)
    def _():
        for copy in copies(acts_ref, grads_ref):
            copy.start()

    @pl.when(side != 0)
    def _():
        for copy in copies(grads_ref, acts_ref):
            copy.start()

    for copy in copies(acts_ref, grads_ref):
        copy.wait()


def deal(after, acts, grads):
    tokens, features = acts.shape
    larger = features * 3 // 4
    widths = [larger, features - larger] if larger % LANES == 0 else [features]
    out = pl.pallas_call(
        deal_kernel,
        out_shape=[bf16(tokens, features)] + [bf16(tokens, width) for width in widths],
        in_specs=[HBM, HBM, ANY],
        out_specs=[VMEM] * (1 + len(widths)),
        scratch_shapes=[pltpu.SemaphoreType.DMA((1 + len(widths),))],
        compiler_params=pltpu.CompilerParams(vmem_limit_bytes=8 * MIB),
    )(*in_hbm(acts, grads), after)
    return out[0], out[1:]


def write_send(later_ref, value_ref, send_ref):
    @pl.when(at_depth(0))
    def _():
        send_ref[...] = later_ref[...]

    @pl.when(jnp.logical_not(at_depth(0)))
    def _():
        send_ref[...] = value_ref[...]


def pair_kernel(mine_ref, came_ref, early_ref, after_ref, out_ref):
    @pl.when(at_depth(0))
    def _():
        out_ref[...] = (mine_ref[...].astype(jnp.float32) + early_ref[...].astype(jnp.float32)).astype(jnp.bfloat16)

    @pl.when(jnp.logical_not(at_depth(0)))
    def _():
        out_ref[...] = (mine_ref[...].astype(jnp.float32) + came_ref[...].astype(jnp.float32)).astype(jnp.bfloat16)


def pair(after, mine, came, early):
    return pl.pallas_call(
        pair_kernel,
        out_shape=bf16(*mine.shape),
        in_specs=[VMEM, VMEM, VMEM, ANY],
        out_specs=VMEM,
        compiler_params=pltpu.CompilerParams(vmem_limit_bytes=8 * MIB),
    )(mine, came, early, after)


def total_kernel(shared, mine_ref, came_ref, after_ref, *rest):
    mine = mine_ref[...].astype(jnp.float32) + came_ref[...].astype(jnp.float32)
    rest[-1][...] = mine.astype(jnp.bfloat16)
    if shared:
        write_send(rest[0], rest[2], rest[1])
    elif len(rest) == 3:
        rest[1][...] = rest[0][...]


def total(after, mine, came, later=None, shared=False):
    extra = [] if later is None else [later]
    out = pl.pallas_call(
        functools.partial(total_kernel, shared),
        out_shape=[bf16(*a.shape) for a in extra + [mine]],
        in_specs=[VMEM, VMEM, ANY] + [VMEM] * len(extra),
        out_specs=[VMEM] * (1 + len(extra)),
        compiler_params=pltpu.CompilerParams(vmem_limit_bytes=8 * MIB),
    )(mine, came, after, *extra)
    return out[-1], (out[0] if extra else None)


def take_kernel(hop, shared, mine_ref, came_ref, after_ref, *rest):
    @pl.when(at_depth(hop))
    def _():
        rest[-1][...] = came_ref[...]

    @pl.when(jnp.logical_not(at_depth(hop)))
    def _():
        rest[-1][...] = mine_ref[...]

    if shared:
        write_send(rest[0], rest[2], rest[1])


def take(after, hop, mine, came, later=None):
    extra = [] if later is None else [later]
    out = pl.pallas_call(
        functools.partial(take_kernel, hop, later is not None),
        out_shape=[bf16(*a.shape) for a in extra + [mine]],
        in_specs=[VMEM, VMEM, ANY] + [VMEM] * len(extra),
        out_specs=[VMEM] * (1 + len(extra)),
        compiler_params=pltpu.CompilerParams(vmem_limit_bytes=8 * MIB),
    )(mine, came, after, *extra)
    return out[-1], (out[0] if extra else None)


def project_kernel(parts, after_ref, *rest):
    factors = jnp.concatenate([ref[...] for ref in rest[parts:-1]], axis=0)
    projected, first = 0.0, 0
    for ref in rest[:parts]:
        width = ref.shape[1]
        projected += lax.dot_general(
            factors[:, first : first + width], ref[...], NT, preferred_element_type=jnp.float32
        )
        first += width
    rest[-1][...] = projected.astype(rest[-1].dtype)


def project(after, factors, tokens, dtype):
    rows = sum(chunk.shape[0] for chunk in factors)
    return pl.pallas_call(
        functools.partial(project_kernel, len(tokens)),
        out_shape=jax.ShapeDtypeStruct((rows, tokens[0].shape[0]), dtype),
        in_specs=[ANY] + [VMEM] * (len(tokens) + len(factors)),
        out_specs=VMEM,
        compiler_params=pltpu.CompilerParams(vmem_limit_bytes=16 * MIB),
    )(after, *tokens, *factors)


def score_kernel(count, counts_ref, *refs):
    out_ref = refs[-1]
    own = jnp.concatenate([ref[...] for ref in refs[:count]], axis=0)
    other = jnp.concatenate([ref[...] for ref in refs[count : 2 * count]], axis=0)
    product = own * other.astype(jnp.float32)
    queries, tokens = product.shape[0] // RANK, product.shape[1]
    scores = jnp.sum(product.reshape(queries, RANK, tokens), axis=1) * RANK ** (-0.5)
    out_ref[...] = jnp.zeros(out_ref.shape, jnp.float32)
    out_ref[:, :tokens] = scores
    position = lax.broadcasted_iota(jnp.int32, scores.shape, 1)
    docs = counts_ref.shape[1]
    column = lax.broadcasted_iota(jnp.int32, (queries, docs), 1)
    pooled = jnp.zeros((queries, docs), jnp.float32)
    start = jnp.int32(0)
    for k in range(docs):
        count = counts_ref[0, k]
        inside = (position >= start) & (position < start + count)
        found = jnp.sum(jnp.where(inside, scores, 0.0), axis=1, keepdims=True)
        root = jnp.sqrt(jnp.full((1, 1), count, jnp.int32).astype(jnp.float32))
        pooled = jnp.where(column == k, found / root, pooled)
        start = start + count
    out_ref[:, tokens : tokens + pooled.shape[1]] = pooled


def score(counts, own, other):
    rows = sum(piece.shape[0] for piece in own)
    width = (own[0].shape[1] + counts.shape[1] + LANES - 1) // LANES * LANES
    return pl.pallas_call(
        functools.partial(score_kernel, len(own)),
        out_shape=jax.ShapeDtypeStruct((rows // RANK, width), jnp.float32),
        in_specs=[pl.BlockSpec(memory_space=pltpu.SMEM)] + [VMEM] * (2 * len(own)),
        out_specs=VMEM,
        compiler_params=pltpu.CompilerParams(vmem_limit_bytes=16 * MIB),
    )(counts, *own, *other)


def chunk_rows(spread):
    return spread // 6 if spread % 192 == 0 else RANK


def is_power(number):
    return number & (number - 1) == 0


def per_device(
    acts,
    grads,
    basis_in,
    output_eigen_basis,
    query_in,
    query_out,
    doc_counts,
    pair_query,
    pair_device,
    pair_doc,
):
    n = lax.axis_size("dp")
    layers = lax.axis_size("layer")
    z = lax.axis_index("dp")
    spread = query_in.shape[2]
    queries = spread // RANK
    half = n // 2
    rows = chunk_rows(spread)
    chunks = spread // rows

    first, send, basis, turned = first_pull(
        basis_in[0], output_eigen_basis[0], query_in[0], query_out[0], rows
    )
    own = [first] + list(pull(first, turned, basis, rows))
    tokens, theirs = deal(own[-1], acts[0], grads[0])
    swap = [(0, 1), (1, 0)]

    stages = [("in", hop) for hop in range(half - 1)] + [("mid", 0)]
    stages += [("out", hop) for hop in range(half - 2, -1, -1)]
    last = len(stages) - 1

    def transfer(kinds, hop, value):
        pairs = []
        if "in" in kinds:
            pairs += [(hop, hop + 1), (n - 1 - hop, n - 2 - hop)]
        if "mid" in kinds:
            pairs += [(half - 1, half), (half, half - 1)]
        if "out" in kinds:
            pairs += [(hop + 1, hop), (n - 2 - hop, n - 1 - hop)]
        return lax.ppermute(value, "dp", pairs)

    short = n == 4
    part, came = list(own), [None] * chunks
    ahead = min(2, chunks)
    early = came[0] = transfer(("in", "out") if short else ("in",), 0, send)
    for c in range(1, ahead):
        came[c] = transfer(("in",), 0, part[c])
    others = [lax.ppermute(piece, "parts", swap) for piece in theirs]
    after = own[0]
    waiting, mine, back = [], [], []

    def project_waiting(after):
        factors = [factor for _, factor in sorted(waiting, key=lambda entry: entry[0])]
        away = project(after, factors, others, jnp.bfloat16)
        back.append(lax.ppermute(away, "parts", swap))
        mine.append(project(away, factors, [tokens], jnp.float32))
        waiting.clear()
        return mine[-1]

    swapped = set()
    turns = chunks + last - short
    for turn in range(turns):
        steps = [(s, turn - s) for s in range(last) if 0 <= turn - s < chunks]
        due = [c for c in range(chunks) if c + last + (c in swapped) == turn]
        for s, c in steps + [(last, c) for c in due]:
            kind, hop = stages[s]
            if short and c == chunks - 1:
                if s == 0:
                    after = part[c] = pair(after, own[c], came[c], early)
                    came[c] = lax.ppermute(part[c], "dp", [(i, i ^ 2) for i in range(n)])
                elif s == 1:
                    part[c], _ = total(after, part[c], came[c])
                    after = part[c]
                    waiting.append((c, part[c]))
                continue
            later = turn + ahead if turn + ahead < chunks else None
            if turn >= last - 1:
                use = later if s == last - 1 else None
            else:
                use = later if s == 0 else None
            shared = use is not None and turn >= last - 1
            chunk = None if use is None else own[use]
            if kind == "out":
                part[c], send = take(after, hop, part[c], came[c], chunk)
            else:
                part[c], send = total(after, part[c], came[c], chunk, shared)
            after = part[c]
            if shared:
                came[c] = came[use] = transfer(("in", "out"), 0, send)
                swapped.add(c)
                continue
            if use is not None:
                came[use] = transfer(stages[0][:1], stages[0][1], send)
            if s < last:
                came[c] = transfer(stages[s + 1][:1], stages[s + 1][1], part[c])
            else:
                waiting.append((c, part[c]))
        if turn >= turns - 2 and waiting:
            after = project_waiting(after)

    scores = score(doc_counts, mine, back)
    if not is_power(layers):
        scores = lax.psum(scores, "layer")
    else:
        for step in [1 << k for k in range(layers.bit_length() - 1)]:
            scores = scores + lax.ppermute(scores, "layer", [(i, i ^ step) for i in range(layers)])
    tokens_here, docs = acts.shape[1], doc_counts.shape[1]
    token_scores, pooled = scores[:, :tokens_here], scores[:, tokens_here : tokens_here + docs]

    cells = queries * docs
    flat = pooled.reshape(1, cells)
    target = pair_device[:, 0]
    cell = pair_query * docs + pair_doc
    if n <= 8 and is_power(n):
        table = jnp.concatenate(
            [flat] + [lax.ppermute(flat, "dp", [(i, i ^ k) for i in range(n)]) for k in range(1, n)], axis=1
        )
        column = (z ^ target) * cells + cell
    else:
        table = lax.all_gather(flat, "dp", axis=1, tiled=True)
        column = target * cells + cell
    hit = column[:, None] == jnp.arange(n * cells, dtype=jnp.int32)[None, :]
    pair_scores = jnp.sum(jnp.where(hit, table, 0.0), axis=1)
    return (token_scores, pair_scores)


def solution(mesh):
    in_specs = (
        P("layer", ("parts", "dp"), None),
        P("layer", ("parts", "dp"), None),
        P("layer", None, "dp"),
        P("layer", None, "dp"),
        P("layer", "dp", None),
        P("layer", "dp", None),
        P(("parts", "dp"), None),
        P(("parts", "dp")),
        P(("parts", "dp"), None),
        P(("parts", "dp")),
    )
    out_specs = (P(None, ("parts", "dp")), P(("parts", "dp")))
    return jax.shard_map(
        per_device, mesh=mesh, in_specs=in_specs, out_specs=out_specs, check_vma=False
    )
```

```python
import functools

import jax
import jax.numpy as jnp
from jax import lax
from jax.experimental import pallas as pl
from jax.experimental.pallas import tpu as pltpu
from jax.sharding import PartitionSpec as P

RANK = 32
NT = (((1,), (1,)), ((), ()))


VMEM = pl.BlockSpec(memory_space=pltpu.VMEM)
HBM = pl.BlockSpec(memory_space=pltpu.HBM)
ANY = pl.BlockSpec(memory_space=pl.ANY)
MIB = 1024 * 1024
LANES = 128


def in_hbm(*arrays):
    return [pltpu.with_memory_space_constraint(array, pltpu.HBM) for array in arrays]


def bf16(*shape):
    return jax.ShapeDtypeStruct(shape, jnp.bfloat16)


def at_depth(hop):
    z = lax.axis_index("dp")
    return jnp.minimum(z, lax.axis_size("dp") - 1 - z) == hop


def first_pull_kernel(
    basis_in_ref, basis_out_ref, query_in_ref, query_out_ref, out_ref, send_ref, basis_ref, query_ref, turned_ref, sems
):
    rows = out_ref.shape[0]
    features = basis_ref.shape[0]
    block = 512 if features % 512 == 0 else features
    spans = [pl.ds(first, block) for first in range(0, features, block)]

    def copies(from_basis, from_query):
        return [pltpu.make_async_copy(from_query, query_ref, sems.at[0])] + [
            pltpu.make_async_copy(from_basis.at[span], basis_ref.at[span], sems.at[1 + i])
            for i, span in enumerate(spans)
        ]

    side = lax.axis_index("parts")

    @pl.when(side == 0)
    def _():
        for copy in copies(basis_in_ref, query_in_ref):
            copy.start()

    @pl.when(side != 0)
    def _():
        for copy in copies(basis_out_ref, query_out_ref):
            copy.start()

    landed = copies(basis_in_ref, query_in_ref)
    landed[0].wait()
    turned_ref[...] = query_ref[...].T
    first = pl.multiple_of(jnp.where(at_depth(0), 0, turned_ref.shape[0] - rows), rows)
    factors = jnp.concatenate([turned_ref[:rows], turned_ref[pl.ds(first, rows)]], axis=0)
    for copy, span in zip(landed[1:], spans):
        copy.wait()
        pulled = lax.dot_general(factors, basis_ref[span], NT, preferred_element_type=jnp.float32)
        pulled = pulled.astype(jnp.bfloat16)
        out_ref[:, span] = pulled[:rows]
        send_ref[:, span] = pulled[rows:]


def first_pull(basis_in, basis_out, query_in, query_out, rows):
    features, depth = basis_in.shape
    spread = query_in.shape[1]
    blocks = features // 512 if features % 512 == 0 else 1
    out, send, basis, _, turned = pl.pallas_call(
        first_pull_kernel,
        out_shape=[bf16(rows, features)] * 2 + [bf16(features, depth), bf16(depth, spread), bf16(spread, depth)],
        in_specs=[HBM] * 4,
        out_specs=[VMEM] * 5,
        scratch_shapes=[pltpu.SemaphoreType.DMA((1 + blocks,))],
        compiler_params=pltpu.CompilerParams(vmem_limit_bytes=16 * MIB),
    )(*in_hbm(basis_in, basis_out, query_in, query_out))
    return out, send, basis, turned


def pull_kernel(turned_ref, basis_ref, after_ref, *outs):
    rows, features = outs[0].shape
    block = 512 if features % 512 == 0 else features
    for i in range(features // block):
        pulled = lax.dot_general(
            turned_ref[rows:], basis_ref[i * block : (i + 1) * block], NT, preferred_element_type=jnp.float32
        ).astype(jnp.bfloat16)
        for c, out in enumerate(outs):
            out[:, i * block : (i + 1) * block] = pulled[c * rows : (c + 1) * rows]


def pull(after, turned, basis, rows):
    chunks = turned.shape[0] // rows - 1
    return pl.pallas_call(
        pull_kernel,
        out_shape=[bf16(rows, basis.shape[0])] * chunks,
        in_specs=[VMEM, VMEM, ANY],
        out_specs=[VMEM] * chunks,
        compiler_params=pltpu.CompilerParams(vmem_limit_bytes=16 * MIB),
    )(turned, basis, after)


def deal_kernel(acts_ref, grads_ref, after_ref, *rest):
    outs, sems = rest[:-1], rest[-1]

    def copies(mine, theirs):
        pairs, first = [(mine, outs[0])], 0
        for out in outs[1:]:
            pairs.append((theirs.at[:, pl.ds(first, out.shape[1])], out))
            first += out.shape[1]
        return [pltpu.make_async_copy(source, target, sems.at[i]) for i, (source, target) in enumerate(pairs)]

    side = lax.axis_index("parts")

    @pl.when(side == 0)
    def _():
        for copy in copies(acts_ref, grads_ref):
            copy.start()

    @pl.when(side != 0)
    def _():
        for copy in copies(grads_ref, acts_ref):
            copy.start()

    for copy in copies(acts_ref, grads_ref):
        copy.wait()


def deal(after, acts, grads):
    tokens, features = acts.shape
    larger = features * 3 // 4
    widths = [larger, features - larger] if larger % LANES == 0 else [features]
    out = pl.pallas_call(
        deal_kernel,
        out_shape=[bf16(tokens, features)] + [bf16(tokens, width) for width in widths],
        in_specs=[HBM, HBM, ANY],
        out_specs=[VMEM] * (1 + len(widths)),
        scratch_shapes=[pltpu.SemaphoreType.DMA((1 + len(widths),))],
        compiler_params=pltpu.CompilerParams(vmem_limit_bytes=8 * MIB),
    )(*in_hbm(acts, grads), after)
    return out[0], out[1:]


def write_send(later_ref, value_ref, send_ref):
    @pl.when(at_depth(0))
    def _():
        send_ref[...] = later_ref[...]

    @pl.when(jnp.logical_not(at_depth(0)))
    def _():
        send_ref[...] = value_ref[...]


def pair_kernel(mine_ref, came_ref, early_ref, after_ref, out_ref):
    @pl.when(at_depth(0))
    def _():
        out_ref[...] = (mine_ref[...].astype(jnp.float32) + early_ref[...].astype(jnp.float32)).astype(jnp.bfloat16)

    @pl.when(jnp.logical_not(at_depth(0)))
    def _():
        out_ref[...] = (mine_ref[...].astype(jnp.float32) + came_ref[...].astype(jnp.float32)).astype(jnp.bfloat16)


def pair(after, mine, came, early):
    return pl.pallas_call(
        pair_kernel,
        out_shape=bf16(*mine.shape),
        in_specs=[VMEM, VMEM, VMEM, ANY],
        out_specs=VMEM,
        compiler_params=pltpu.CompilerParams(vmem_limit_bytes=8 * MIB),
    )(mine, came, early, after)


def total_kernel(shared, mine_ref, came_ref, after_ref, *rest):
    mine = mine_ref[...].astype(jnp.float32) + came_ref[...].astype(jnp.float32)
    rest[-1][...] = mine.astype(jnp.bfloat16)
    if shared:
        write_send(rest[0], rest[2], rest[1])
    elif len(rest) == 3:
        rest[1][...] = rest[0][...]


def total(after, mine, came, later=None, shared=False):
    extra = [] if later is None else [later]
    out = pl.pallas_call(
        functools.partial(total_kernel, shared),
        out_shape=[bf16(*a.shape) for a in extra + [mine]],
        in_specs=[VMEM, VMEM, ANY] + [VMEM] * len(extra),
        out_specs=[VMEM] * (1 + len(extra)),
        compiler_params=pltpu.CompilerParams(vmem_limit_bytes=8 * MIB),
    )(mine, came, after, *extra)
    return out[-1], (out[0] if extra else None)


def take_kernel(hop, shared, mine_ref, came_ref, after_ref, *rest):
    @pl.when(at_depth(hop))
    def _():
        rest[-1][...] = came_ref[...]

    @pl.when(jnp.logical_not(at_depth(hop)))
    def _():
        rest[-1][...] = mine_ref[...]

    if shared:
        write_send(rest[0], rest[2], rest[1])


def take(after, hop, mine, came, later=None):
    extra = [] if later is None else [later]
    out = pl.pallas_call(
        functools.partial(take_kernel, hop, later is not None),
        out_shape=[bf16(*a.shape) for a in extra + [mine]],
        in_specs=[VMEM, VMEM, ANY] + [VMEM] * len(extra),
        out_specs=[VMEM] * (1 + len(extra)),
        compiler_params=pltpu.CompilerParams(vmem_limit_bytes=8 * MIB),
    )(mine, came, after, *extra)
    return out[-1], (out[0] if extra else None)


def project_kernel(parts, after_ref, *rest):
    factors = jnp.concatenate([ref[...] for ref in rest[parts:-1]], axis=0)
    projected, first = 0.0, 0
    for ref in rest[:parts]:
        width = ref.shape[1]
        projected += lax.dot_general(
            factors[:, first : first + width], ref[...], NT, preferred_element_type=jnp.float32
        )
        first += width
    rest[-1][...] = projected.astype(rest[-1].dtype)


def project(after, factors, tokens, dtype):
    rows = sum(chunk.shape[0] for chunk in factors)
    return pl.pallas_call(
        functools.partial(project_kernel, len(tokens)),
        out_shape=jax.ShapeDtypeStruct((rows, tokens[0].shape[0]), dtype),
        in_specs=[ANY] + [VMEM] * (len(tokens) + len(factors)),
        out_specs=VMEM,
        compiler_params=pltpu.CompilerParams(vmem_limit_bytes=16 * MIB),
    )(after, *tokens, *factors)


def score_kernel(count, counts_ref, *refs):
    out_ref = refs[-1]
    own = jnp.concatenate([ref[...] for ref in refs[:count]], axis=0)
    other = jnp.concatenate([ref[...] for ref in refs[count : 2 * count]], axis=0)
    product = own * other.astype(jnp.float32)
    queries, tokens = product.shape[0] // RANK, product.shape[1]
    scores = jnp.sum(product.reshape(queries, RANK, tokens), axis=1) * RANK ** (-0.5)
    out_ref[...] = jnp.zeros(out_ref.shape, jnp.float32)
    out_ref[:, :tokens] = scores
    position = lax.broadcasted_iota(jnp.int32, scores.shape, 1)
    docs = counts_ref.shape[1]
    column = lax.broadcasted_iota(jnp.int32, (queries, docs), 1)
    pooled = jnp.zeros((queries, docs), jnp.float32)
    start = jnp.int32(0)
    for k in range(docs):
        count = counts_ref[0, k]
        inside = (position >= start) & (position < start + count)
        found = jnp.sum(jnp.where(inside, scores, 0.0), axis=1, keepdims=True)
        root = jnp.sqrt(jnp.full((1, 1), count, jnp.int32).astype(jnp.float32))
        pooled = jnp.where(column == k, found / root, pooled)
        start = start + count
    out_ref[:, tokens : tokens + pooled.shape[1]] = pooled


def score(counts, own, other):
    rows = sum(piece.shape[0] for piece in own)
    width = (own[0].shape[1] + counts.shape[1] + LANES - 1) // LANES * LANES
    return pl.pallas_call(
        functools.partial(score_kernel, len(own)),
        out_shape=jax.ShapeDtypeStruct((rows // RANK, width), jnp.float32),
        in_specs=[pl.BlockSpec(memory_space=pltpu.SMEM)] + [VMEM] * (2 * len(own)),
        out_specs=VMEM,
        compiler_params=pltpu.CompilerParams(vmem_limit_bytes=16 * MIB),
    )(counts, *own, *other)


def chunk_rows(spread):
    return spread // 8 if spread % 128 == 0 else RANK


def is_power(number):
    return number & (number - 1) == 0


def per_device(
    acts,
    grads,
    basis_in,
    output_eigen_basis,
    query_in,
    query_out,
    doc_counts,
    pair_query,
    pair_device,
    pair_doc,
):
    n = lax.axis_size("dp")
    layers = lax.axis_size("layer")
    z = lax.axis_index("dp")
    spread = query_in.shape[2]
    queries = spread // RANK
    half = n // 2
    rows = chunk_rows(spread)
    chunks = spread // rows

    first, send, basis, turned = first_pull(
        basis_in[0], output_eigen_basis[0], query_in[0], query_out[0], rows
    )
    own = [first] + list(pull(first, turned, basis, rows))
    tokens, theirs = deal(own[-1], acts[0], grads[0])
    swap = [(0, 1), (1, 0)]

    stages = [("in", hop) for hop in range(half - 1)] + [("mid", 0)]
    stages += [("out", hop) for hop in range(half - 2, -1, -1)]
    last = len(stages) - 1

    def transfer(kinds, hop, value):
        pairs = []
        if "in" in kinds:
            pairs += [(hop, hop + 1), (n - 1 - hop, n - 2 - hop)]
        if "mid" in kinds:
            pairs += [(half - 1, half), (half, half - 1)]
        if "out" in kinds:
            pairs += [(hop + 1, hop), (n - 2 - hop, n - 1 - hop)]
        return lax.ppermute(value, "dp", pairs)

    short = n == 4
    part, came = list(own), [None] * chunks
    ahead = min(2, chunks)
    early = came[0] = transfer(("in", "out") if short else ("in",), 0, send)
    for c in range(1, ahead):
        came[c] = transfer(("in",), 0, part[c])
    others = [lax.ppermute(piece, "parts", swap) for piece in theirs]
    after = own[0]
    waiting, mine, back = [], [], []

    def project_waiting(after):
        factors = [factor for _, factor in sorted(waiting, key=lambda entry: entry[0])]
        away = project(after, factors, others, jnp.bfloat16)
        back.append(lax.ppermute(away, "parts", swap))
        mine.append(project(away, factors, [tokens], jnp.float32))
        waiting.clear()
        return mine[-1]

    swapped = set()
    turns = chunks + last - short
    for turn in range(turns):
        steps = [(s, turn - s) for s in range(last) if 0 <= turn - s < chunks]
        due = [c for c in range(chunks) if c + last + (c in swapped) == turn]
        for s, c in steps + [(last, c) for c in due]:
            kind, hop = stages[s]
            if short and c == chunks - 1:
                if s == 0:
                    after = part[c] = pair(after, own[c], came[c], early)
                    came[c] = lax.ppermute(part[c], "dp", [(i, i ^ 2) for i in range(n)])
                elif s == 1:
                    part[c], _ = total(after, part[c], came[c])
                    after = part[c]
                    waiting.append((c, part[c]))
                continue
            later = turn + ahead if turn + ahead < chunks else None
            if turn >= last - 1:
                use = later if s == last - 1 else None
            else:
                use = later if s == 0 else None
            shared = use is not None and turn >= last - 1
            chunk = None if use is None else own[use]
            if kind == "out":
                part[c], send = take(after, hop, part[c], came[c], chunk)
            else:
                part[c], send = total(after, part[c], came[c], chunk, shared)
            after = part[c]
            if shared:
                came[c] = came[use] = transfer(("in", "out"), 0, send)
                swapped.add(c)
                continue
            if use is not None:
                came[use] = transfer(stages[0][:1], stages[0][1], send)
            if s < last:
                came[c] = transfer(stages[s + 1][:1], stages[s + 1][1], part[c])
            else:
                waiting.append((c, part[c]))
        if turn >= turns - 2 and waiting:
            after = project_waiting(after)

    scores = score(doc_counts, mine, back)
    if not is_power(layers):
        scores = lax.psum(scores, "layer")
    else:
        for step in [1 << k for k in range(layers.bit_length() - 1)]:
            scores = scores + lax.ppermute(scores, "layer", [(i, i ^ step) for i in range(layers)])
    tokens_here, docs = acts.shape[1], doc_counts.shape[1]
    token_scores, pooled = scores[:, :tokens_here], scores[:, tokens_here : tokens_here + docs]

    cells = queries * docs
    flat = pooled.reshape(1, cells)
    target = pair_device[:, 0]
    cell = pair_query * docs + pair_doc
    if n <= 8 and is_power(n):
        away = [0] + list(range(n - 1, 0, -1))
        table = jnp.concatenate(
            [flat] + [lax.ppermute(flat, "dp", [(i, i ^ k) for i in range(n)]) for k in away[1:]], axis=1
        )
        column = lax.rem(n - (z ^ target), n) * cells + cell
    else:
        table = lax.all_gather(flat, "dp", axis=1, tiled=True)
        column = target * cells + cell
    hit = column[:, None] == jnp.arange(n * cells, dtype=jnp.int32)[None, :]
    pair_scores = jnp.sum(jnp.where(hit, table, 0.0), axis=1)
    return (token_scores, pair_scores)


def solution(mesh):
    in_specs = (
        P("layer", ("parts", "dp"), None),
        P("layer", ("parts", "dp"), None),
        P("layer", None, "dp"),
        P("layer", None, "dp"),
        P("layer", "dp", None),
        P("layer", "dp", None),
        P(("parts", "dp"), None),
        P(("parts", "dp")),
        P(("parts", "dp"), None),
        P(("parts", "dp")),
    )
    out_specs = (P(None, ("parts", "dp")), P(("parts", "dp")))
    return jax.shard_map(
        per_device, mesh=mesh, in_specs=in_specs, out_specs=out_specs, check_vma=False
    )
```

```python
import functools

import jax
import jax.numpy as jnp
from jax import lax
from jax.experimental import pallas as pl
from jax.experimental.pallas import tpu as pltpu
from jax.sharding import PartitionSpec as P

RANK = 32
NT = (((1,), (1,)), ((), ()))


VMEM = pl.BlockSpec(memory_space=pltpu.VMEM)
HBM = pl.BlockSpec(memory_space=pltpu.HBM)
ANY = pl.BlockSpec(memory_space=pl.ANY)
MIB = 1024 * 1024
LANES = 128


def in_hbm(*arrays):
    return [pltpu.with_memory_space_constraint(array, pltpu.HBM) for array in arrays]


def bf16(*shape):
    return jax.ShapeDtypeStruct(shape, jnp.bfloat16)


def at_depth(hop):
    z = lax.axis_index("dp")
    return jnp.minimum(z, lax.axis_size("dp") - 1 - z) == hop


def first_pull_kernel(
    basis_in_ref, basis_out_ref, query_in_ref, query_out_ref, out_ref, send_ref, basis_ref, query_ref, turned_ref, sems
):
    rows = out_ref.shape[0]
    features = basis_ref.shape[0]
    block = 512 if features % 512 == 0 else features
    spans = [pl.ds(first, block) for first in range(0, features, block)]

    def copies(from_basis, from_query):
        return [pltpu.make_async_copy(from_query, query_ref, sems.at[0])] + [
            pltpu.make_async_copy(from_basis.at[span], basis_ref.at[span], sems.at[1 + i])
            for i, span in enumerate(spans)
        ]

    side = lax.axis_index("parts")

    @pl.when(side == 0)
    def _():
        for copy in copies(basis_in_ref, query_in_ref):
            copy.start()

    @pl.when(side != 0)
    def _():
        for copy in copies(basis_out_ref, query_out_ref):
            copy.start()

    landed = copies(basis_in_ref, query_in_ref)
    landed[0].wait()
    turned_ref[...] = query_ref[...].T
    first = pl.multiple_of(jnp.where(at_depth(0), 0, turned_ref.shape[0] - rows), rows)
    factors = jnp.concatenate([turned_ref[:rows], turned_ref[pl.ds(first, rows)]], axis=0)
    for copy, span in zip(landed[1:], spans):
        copy.wait()
        pulled = lax.dot_general(factors, basis_ref[span], NT, preferred_element_type=jnp.float32)
        pulled = pulled.astype(jnp.bfloat16)
        out_ref[:, span] = pulled[:rows]
        send_ref[:, span] = pulled[rows:]


def first_pull(basis_in, basis_out, query_in, query_out, rows):
    features, depth = basis_in.shape
    spread = query_in.shape[1]
    blocks = features // 512 if features % 512 == 0 else 1
    out, send, basis, _, turned = pl.pallas_call(
        first_pull_kernel,
        out_shape=[bf16(rows, features)] * 2 + [bf16(features, depth), bf16(depth, spread), bf16(spread, depth)],
        in_specs=[HBM] * 4,
        out_specs=[VMEM] * 5,
        scratch_shapes=[pltpu.SemaphoreType.DMA((1 + blocks,))],
        compiler_params=pltpu.CompilerParams(vmem_limit_bytes=16 * MIB),
    )(*in_hbm(basis_in, basis_out, query_in, query_out))
    return out, send, basis, turned


def pull_kernel(turned_ref, basis_ref, after_ref, *outs):
    rows, features = outs[0].shape
    block = 512 if features % 512 == 0 else features
    for i in range(features // block):
        pulled = lax.dot_general(
            turned_ref[rows:], basis_ref[i * block : (i + 1) * block], NT, preferred_element_type=jnp.float32
        ).astype(jnp.bfloat16)
        for c, out in enumerate(outs):
            out[:, i * block : (i + 1) * block] = pulled[c * rows : (c + 1) * rows]


def pull(after, turned, basis, rows):
    chunks = turned.shape[0] // rows - 1
    return pl.pallas_call(
        pull_kernel,
        out_shape=[bf16(rows, basis.shape[0])] * chunks,
        in_specs=[VMEM, VMEM, ANY],
        out_specs=[VMEM] * chunks,
        compiler_params=pltpu.CompilerParams(vmem_limit_bytes=16 * MIB),
    )(turned, basis, after)


def deal_kernel(acts_ref, grads_ref, after_ref, *rest):
    outs, sems = rest[:-1], rest[-1]

    def copies(mine, theirs):
        pairs, first = [(mine, outs[0])], 0
        for out in outs[1:]:
            pairs.append((theirs.at[:, pl.ds(first, out.shape[1])], out))
            first += out.shape[1]
        return [pltpu.make_async_copy(source, target, sems.at[i]) for i, (source, target) in enumerate(pairs)]

    side = lax.axis_index("parts")

    @pl.when(side == 0)
    def _():
        for copy in copies(acts_ref, grads_ref):
            copy.start()

    @pl.when(side != 0)
    def _():
        for copy in copies(grads_ref, acts_ref):
            copy.start()

    for copy in copies(acts_ref, grads_ref):
        copy.wait()


def deal(after, acts, grads):
    tokens, features = acts.shape
    larger = features * 3 // 4
    widths = [larger, features - larger] if larger % LANES == 0 else [features]
    out = pl.pallas_call(
        deal_kernel,
        out_shape=[bf16(tokens, features)] + [bf16(tokens, width) for width in widths],
        in_specs=[HBM, HBM, ANY],
        out_specs=[VMEM] * (1 + len(widths)),
        scratch_shapes=[pltpu.SemaphoreType.DMA((1 + len(widths),))],
        compiler_params=pltpu.CompilerParams(vmem_limit_bytes=8 * MIB),
    )(*in_hbm(acts, grads), after)
    return out[0], out[1:]


def write_send(later_ref, value_ref, send_ref):
    @pl.when(at_depth(0))
    def _():
        send_ref[...] = later_ref[...]

    @pl.when(jnp.logical_not(at_depth(0)))
    def _():
        send_ref[...] = value_ref[...]


def pair_kernel(mine_ref, came_ref, early_ref, after_ref, out_ref):
    @pl.when(at_depth(0))
    def _():
        out_ref[...] = (mine_ref[...].astype(jnp.float32) + early_ref[...].astype(jnp.float32)).astype(jnp.bfloat16)

    @pl.when(jnp.logical_not(at_depth(0)))
    def _():
        out_ref[...] = (mine_ref[...].astype(jnp.float32) + came_ref[...].astype(jnp.float32)).astype(jnp.bfloat16)


def pair(after, mine, came, early):
    return pl.pallas_call(
        pair_kernel,
        out_shape=bf16(*mine.shape),
        in_specs=[VMEM, VMEM, VMEM, ANY],
        out_specs=VMEM,
        compiler_params=pltpu.CompilerParams(vmem_limit_bytes=8 * MIB),
    )(mine, came, early, after)


def total_kernel(shared, mine_ref, came_ref, after_ref, *rest):
    mine = mine_ref[...].astype(jnp.float32) + came_ref[...].astype(jnp.float32)
    rest[-1][...] = mine.astype(jnp.bfloat16)
    if shared:
        write_send(rest[0], rest[2], rest[1])
    elif len(rest) == 3:
        rest[1][...] = rest[0][...]


def total(after, mine, came, later=None, shared=False):
    extra = [] if later is None else [later]
    out = pl.pallas_call(
        functools.partial(total_kernel, shared),
        out_shape=[bf16(*a.shape) for a in extra + [mine]],
        in_specs=[VMEM, VMEM, ANY] + [VMEM] * len(extra),
        out_specs=[VMEM] * (1 + len(extra)),
        compiler_params=pltpu.CompilerParams(vmem_limit_bytes=8 * MIB),
    )(mine, came, after, *extra)
    return out[-1], (out[0] if extra else None)


def take_kernel(hop, shared, mine_ref, came_ref, after_ref, *rest):
    @pl.when(at_depth(hop))
    def _():
        rest[-1][...] = came_ref[...]

    @pl.when(jnp.logical_not(at_depth(hop)))
    def _():
        rest[-1][...] = mine_ref[...]

    if shared:
        write_send(rest[0], rest[2], rest[1])


def take(after, hop, mine, came, later=None):
    extra = [] if later is None else [later]
    out = pl.pallas_call(
        functools.partial(take_kernel, hop, later is not None),
        out_shape=[bf16(*a.shape) for a in extra + [mine]],
        in_specs=[VMEM, VMEM, ANY] + [VMEM] * len(extra),
        out_specs=[VMEM] * (1 + len(extra)),
        compiler_params=pltpu.CompilerParams(vmem_limit_bytes=8 * MIB),
    )(mine, came, after, *extra)
    return out[-1], (out[0] if extra else None)


def project_kernel(parts, after_ref, *rest):
    factors = jnp.concatenate([ref[...] for ref in rest[parts:-1]], axis=0)
    projected, first = 0.0, 0
    for ref in rest[:parts]:
        width = ref.shape[1]
        projected += lax.dot_general(
            factors[:, first : first + width], ref[...], NT, preferred_element_type=jnp.float32
        )
        first += width
    rest[-1][...] = projected.astype(rest[-1].dtype)


def project(after, factors, tokens, dtype):
    rows = sum(chunk.shape[0] for chunk in factors)
    return pl.pallas_call(
        functools.partial(project_kernel, len(tokens)),
        out_shape=jax.ShapeDtypeStruct((rows, tokens[0].shape[0]), dtype),
        in_specs=[ANY] + [VMEM] * (len(tokens) + len(factors)),
        out_specs=VMEM,
        compiler_params=pltpu.CompilerParams(vmem_limit_bytes=16 * MIB),
    )(after, *tokens, *factors)


def score_kernel(count, counts_ref, *refs):
    out_ref = refs[-1]
    own = jnp.concatenate([ref[...] for ref in refs[:count]], axis=0)
    other = jnp.concatenate([ref[...] for ref in refs[count : 2 * count]], axis=0)
    product = own * other.astype(jnp.float32)
    queries, tokens = product.shape[0] // RANK, product.shape[1]
    scores = jnp.sum(product.reshape(queries, RANK, tokens), axis=1) * RANK ** (-0.5)
    out_ref[...] = jnp.zeros(out_ref.shape, jnp.float32)
    out_ref[:, :tokens] = scores
    docs = counts_ref.shape[1]
    row = lax.broadcasted_iota(jnp.int32, (docs, 1), 0)
    column = lax.broadcasted_iota(jnp.int32, (1, docs), 1)
    starts, ends = jnp.zeros((docs, 1), jnp.int32), jnp.zeros((docs, 1), jnp.int32)
    counts = jnp.ones((1, docs), jnp.int32)
    end = jnp.int32(0)
    for k in range(docs):
        start, end = end, end + counts_ref[0, k]
        starts, ends = jnp.where(row == k, start, starts), jnp.where(row == k, end, ends)
        counts = jnp.where(column == k, end - start, counts)
    position = lax.broadcasted_iota(jnp.int32, (docs, tokens), 1)
    member = ((position >= starts) & (position < ends)).astype(jnp.float32)
    pooled = lax.dot_general(
        scores, member, NT, precision=lax.Precision.HIGHEST, preferred_element_type=jnp.float32
    )
    pooled = pooled / jnp.sqrt(counts.astype(jnp.float32))
    out_ref[:, tokens : tokens + pooled.shape[1]] = pooled


def score(counts, own, other):
    rows = sum(piece.shape[0] for piece in own)
    width = (own[0].shape[1] + counts.shape[1] + LANES - 1) // LANES * LANES
    return pl.pallas_call(
        functools.partial(score_kernel, len(own)),
        out_shape=jax.ShapeDtypeStruct((rows // RANK, width), jnp.float32),
        in_specs=[pl.BlockSpec(memory_space=pltpu.SMEM)] + [VMEM] * (2 * len(own)),
        out_specs=VMEM,
        compiler_params=pltpu.CompilerParams(vmem_limit_bytes=16 * MIB),
    )(counts, *own, *other)


def chunk_rows(spread):
    return spread // 8 if spread % 128 == 0 else RANK


def is_power(number):
    return number & (number - 1) == 0


def per_device(
    acts,
    grads,
    basis_in,
    output_eigen_basis,
    query_in,
    query_out,
    doc_counts,
    pair_query,
    pair_device,
    pair_doc,
):
    n = lax.axis_size("dp")
    layers = lax.axis_size("layer")
    z = lax.axis_index("dp")
    spread = query_in.shape[2]
    queries = spread // RANK
    half = n // 2
    rows = chunk_rows(spread)
    chunks = spread // rows

    first, send, basis, turned = first_pull(
        basis_in[0], output_eigen_basis[0], query_in[0], query_out[0], rows
    )
    own = [first] + list(pull(first, turned, basis, rows))
    tokens, theirs = deal(own[-1], acts[0], grads[0])
    swap = [(0, 1), (1, 0)]

    stages = [("in", hop) for hop in range(half - 1)] + [("mid", 0)]
    stages += [("out", hop) for hop in range(half - 2, -1, -1)]
    last = len(stages) - 1

    def transfer(kinds, hop, value):
        pairs = []
        if "in" in kinds:
            pairs += [(hop, hop + 1), (n - 1 - hop, n - 2 - hop)]
        if "mid" in kinds:
            pairs += [(half - 1, half), (half, half - 1)]
        if "out" in kinds:
            pairs += [(hop + 1, hop), (n - 2 - hop, n - 1 - hop)]
        return lax.ppermute(value, "dp", pairs)

    short = n == 4
    part, came = list(own), [None] * chunks
    ahead = min(2, chunks)
    early = came[0] = transfer(("in", "out") if short else ("in",), 0, send)
    for c in range(1, ahead):
        came[c] = transfer(("in",), 0, part[c])
    others = [lax.ppermute(piece, "parts", swap) for piece in theirs]
    after = own[0]
    waiting, mine, back = [], [], []

    def project_waiting(after):
        factors = [factor for _, factor in sorted(waiting, key=lambda entry: entry[0])]
        away = project(after, factors, others, jnp.bfloat16)
        back.append(lax.ppermute(away, "parts", swap))
        mine.append(project(away, factors, [tokens], jnp.float32))
        waiting.clear()
        return mine[-1]

    swapped = set()
    turns = chunks + last - short
    for turn in range(turns):
        steps = [(s, turn - s) for s in range(last) if 0 <= turn - s < chunks]
        due = [c for c in range(chunks) if c + last + (c in swapped) == turn]
        for s, c in steps + [(last, c) for c in due]:
            kind, hop = stages[s]
            if short and c == chunks - 1:
                if s == 0:
                    after = part[c] = pair(after, own[c], came[c], early)
                    came[c] = lax.ppermute(part[c], "dp", [(i, i ^ 2) for i in range(n)])
                elif s == 1:
                    part[c], _ = total(after, part[c], came[c])
                    after = part[c]
                    waiting.append((c, part[c]))
                continue
            later = turn + ahead if turn + ahead < chunks else None
            if turn >= last - 1:
                use = later if s == last - 1 else None
            else:
                use = later if s == 0 else None
            shared = use is not None and turn >= last - 1
            chunk = None if use is None else own[use]
            if kind == "out":
                part[c], send = take(after, hop, part[c], came[c], chunk)
            else:
                part[c], send = total(after, part[c], came[c], chunk, shared)
            after = part[c]
            if shared:
                came[c] = came[use] = transfer(("in", "out"), 0, send)
                swapped.add(c)
                continue
            if use is not None:
                came[use] = transfer(stages[0][:1], stages[0][1], send)
            if s < last:
                came[c] = transfer(stages[s + 1][:1], stages[s + 1][1], part[c])
            else:
                waiting.append((c, part[c]))
        if turn >= turns - 2 and waiting:
            after = project_waiting(after)

    scores = score(doc_counts, mine, back)
    if not is_power(layers):
        scores = lax.psum(scores, "layer")
    else:
        for step in [1 << k for k in range(layers.bit_length() - 1)]:
            scores = scores + lax.ppermute(scores, "layer", [(i, i ^ step) for i in range(layers)])
    tokens_here, docs = acts.shape[1], doc_counts.shape[1]
    token_scores, pooled = scores[:, :tokens_here], scores[:, tokens_here : tokens_here + docs]

    cells = queries * docs
    flat = pooled.reshape(1, cells)
    target = pair_device[:, 0]
    cell = pair_query * docs + pair_doc
    if n <= 8 and is_power(n):
        table = jnp.concatenate(
            [flat] + [lax.ppermute(flat, "dp", [(i, i ^ k ^ (k >> 1)) for i in range(n)]) for k in range(1, n)], axis=1
        )
        away = z ^ target
        column = (away ^ (away >> 1) ^ (away >> 2)) * cells + cell
    else:
        table = lax.all_gather(flat, "dp", axis=1, tiled=True)
        column = target * cells + cell
    hit = column[:, None] == jnp.arange(n * cells, dtype=jnp.int32)[None, :]
    pair_scores = jnp.sum(jnp.where(hit, table, 0.0), axis=1)
    return (token_scores, pair_scores)


def solution(mesh):
    in_specs = (
        P("layer", ("parts", "dp"), None),
        P("layer", ("parts", "dp"), None),
        P("layer", None, "dp"),
        P("layer", None, "dp"),
        P("layer", "dp", None),
        P("layer", "dp", None),
        P(("parts", "dp"), None),
        P(("parts", "dp")),
        P(("parts", "dp"), None),
        P(("parts", "dp")),
    )
    out_specs = (P(None, ("parts", "dp")), P(("parts", "dp")))
    return jax.shard_map(
        per_device, mesh=mesh, in_specs=in_specs, out_specs=out_specs, check_vma=False
    )
```

```python
import functools

import jax
import jax.numpy as jnp
from jax import lax
from jax.experimental import pallas as pl
from jax.experimental.pallas import tpu as pltpu
from jax.sharding import PartitionSpec as P

RANK = 32
NT = (((1,), (1,)), ((), ()))


VMEM = pl.BlockSpec(memory_space=pltpu.VMEM)
HBM = pl.BlockSpec(memory_space=pltpu.HBM)
ANY = pl.BlockSpec(memory_space=pl.ANY)
MIB = 1024 * 1024
LANES = 128


def in_hbm(*arrays):
    return [pltpu.with_memory_space_constraint(array, pltpu.HBM) for array in arrays]


def bf16(*shape):
    return jax.ShapeDtypeStruct(shape, jnp.bfloat16)


def at_depth(hop):
    z = lax.axis_index("dp")
    return jnp.minimum(z, lax.axis_size("dp") - 1 - z) == hop


def first_pull_kernel(
    basis_in_ref, basis_out_ref, query_in_ref, query_out_ref, out_ref, send_ref, basis_ref, query_ref, turned_ref, sems
):
    rows = out_ref.shape[0]
    features = basis_ref.shape[0]
    block = 512 if features % 512 == 0 else features
    spans = [pl.ds(first, block) for first in range(0, features, block)]

    def copies(from_basis, from_query):
        return [pltpu.make_async_copy(from_query, query_ref, sems.at[0])] + [
            pltpu.make_async_copy(from_basis.at[span], basis_ref.at[span], sems.at[1 + i])
            for i, span in enumerate(spans)
        ]

    side = lax.axis_index("parts")

    @pl.when(side == 0)
    def _():
        for copy in copies(basis_in_ref, query_in_ref):
            copy.start()

    @pl.when(side != 0)
    def _():
        for copy in copies(basis_out_ref, query_out_ref):
            copy.start()

    landed = copies(basis_in_ref, query_in_ref)
    landed[0].wait()
    turned_ref[...] = query_ref[...].T
    first = pl.multiple_of(jnp.where(at_depth(0), 0, turned_ref.shape[0] - rows), rows)
    factors = jnp.concatenate([turned_ref[:rows], turned_ref[pl.ds(first, rows)]], axis=0)
    for copy, span in zip(landed[1:], spans):
        copy.wait()
        pulled = lax.dot_general(factors, basis_ref[span], NT, preferred_element_type=jnp.float32)
        pulled = pulled.astype(jnp.bfloat16)
        out_ref[:, span] = pulled[:rows]
        send_ref[:, span] = pulled[rows:]


def first_pull(basis_in, basis_out, query_in, query_out, rows):
    features, depth = basis_in.shape
    spread = query_in.shape[1]
    blocks = features // 512 if features % 512 == 0 else 1
    out, send, basis, _, turned = pl.pallas_call(
        first_pull_kernel,
        out_shape=[bf16(rows, features)] * 2 + [bf16(features, depth), bf16(depth, spread), bf16(spread, depth)],
        in_specs=[HBM] * 4,
        out_specs=[VMEM] * 5,
        scratch_shapes=[pltpu.SemaphoreType.DMA((1 + blocks,))],
        compiler_params=pltpu.CompilerParams(vmem_limit_bytes=16 * MIB),
    )(*in_hbm(basis_in, basis_out, query_in, query_out))
    return out, send, basis, turned


def pull_kernel(turned_ref, basis_ref, after_ref, *outs):
    rows, features = outs[0].shape
    block = 512 if features % 512 == 0 else features
    for i in range(features // block):
        pulled = lax.dot_general(
            turned_ref[rows:], basis_ref[i * block : (i + 1) * block], NT, preferred_element_type=jnp.float32
        ).astype(jnp.bfloat16)
        for c, out in enumerate(outs):
            out[:, i * block : (i + 1) * block] = pulled[c * rows : (c + 1) * rows]


def pull(after, turned, basis, rows):
    chunks = turned.shape[0] // rows - 1
    return pl.pallas_call(
        pull_kernel,
        out_shape=[bf16(rows, basis.shape[0])] * chunks,
        in_specs=[VMEM, VMEM, ANY],
        out_specs=[VMEM] * chunks,
        compiler_params=pltpu.CompilerParams(vmem_limit_bytes=16 * MIB),
    )(turned, basis, after)


def deal_kernel(acts_ref, grads_ref, after_ref, *rest):
    outs, sems = rest[:-1], rest[-1]

    def copies(mine, theirs):
        pairs, first = [(mine, outs[0])], 0
        for out in outs[1:]:
            pairs.append((theirs.at[:, pl.ds(first, out.shape[1])], out))
            first += out.shape[1]
        return [pltpu.make_async_copy(source, target, sems.at[i]) for i, (source, target) in enumerate(pairs)]

    side = lax.axis_index("parts")

    @pl.when(side == 0)
    def _():
        for copy in copies(acts_ref, grads_ref):
            copy.start()

    @pl.when(side != 0)
    def _():
        for copy in copies(grads_ref, acts_ref):
            copy.start()

    for copy in copies(acts_ref, grads_ref):
        copy.wait()


def deal(after, acts, grads):
    tokens, features = acts.shape
    larger = features * 3 // 4
    widths = [larger, features - larger] if larger % LANES == 0 else [features]
    out = pl.pallas_call(
        deal_kernel,
        out_shape=[bf16(tokens, features)] + [bf16(tokens, width) for width in widths],
        in_specs=[HBM, HBM, ANY],
        out_specs=[VMEM] * (1 + len(widths)),
        scratch_shapes=[pltpu.SemaphoreType.DMA((1 + len(widths),))],
        compiler_params=pltpu.CompilerParams(vmem_limit_bytes=8 * MIB),
    )(*in_hbm(acts, grads), after)
    return out[0], out[1:]


def write_send(later_ref, value_ref, send_ref):
    @pl.when(at_depth(0))
    def _():
        send_ref[...] = later_ref[...]

    @pl.when(jnp.logical_not(at_depth(0)))
    def _():
        send_ref[...] = value_ref[...]


def pair_kernel(mine_ref, came_ref, early_ref, after_ref, out_ref):
    @pl.when(at_depth(0))
    def _():
        out_ref[...] = (mine_ref[...].astype(jnp.float32) + early_ref[...].astype(jnp.float32)).astype(jnp.bfloat16)

    @pl.when(jnp.logical_not(at_depth(0)))
    def _():
        out_ref[...] = (mine_ref[...].astype(jnp.float32) + came_ref[...].astype(jnp.float32)).astype(jnp.bfloat16)


def pair(after, mine, came, early):
    return pl.pallas_call(
        pair_kernel,
        out_shape=bf16(*mine.shape),
        in_specs=[VMEM, VMEM, VMEM, ANY],
        out_specs=VMEM,
        compiler_params=pltpu.CompilerParams(vmem_limit_bytes=8 * MIB),
    )(mine, came, early, after)


def total_kernel(shared, paced, mine_ref, came_ref, after_ref, *rest):
    rest = rest[paced:]
    mine = mine_ref[...].astype(jnp.float32) + came_ref[...].astype(jnp.float32)
    rest[-1][...] = mine.astype(jnp.bfloat16)
    if shared:
        write_send(rest[0], rest[2], rest[1])
    elif len(rest) == 3:
        rest[1][...] = rest[0][...]


def total(after, mine, came, later=None, shared=False, pace=None):
    extra = [] if later is None else [later]
    paced = [] if pace is None else [pace]
    out = pl.pallas_call(
        functools.partial(total_kernel, shared, len(paced)),
        out_shape=[bf16(*a.shape) for a in extra + [mine]],
        in_specs=[VMEM, VMEM, ANY] + [ANY] * len(paced) + [VMEM] * len(extra),
        out_specs=[VMEM] * (1 + len(extra)),
        compiler_params=pltpu.CompilerParams(vmem_limit_bytes=8 * MIB),
    )(mine, came, after, *paced, *extra)
    return out[-1], (out[0] if extra else None)


def take_kernel(hop, shared, mine_ref, came_ref, after_ref, *rest):
    @pl.when(at_depth(hop))
    def _():
        rest[-1][...] = came_ref[...]

    @pl.when(jnp.logical_not(at_depth(hop)))
    def _():
        rest[-1][...] = mine_ref[...]

    if shared:
        write_send(rest[0], rest[2], rest[1])


def take(after, hop, mine, came, later=None):
    extra = [] if later is None else [later]
    out = pl.pallas_call(
        functools.partial(take_kernel, hop, later is not None),
        out_shape=[bf16(*a.shape) for a in extra + [mine]],
        in_specs=[VMEM, VMEM, ANY] + [VMEM] * len(extra),
        out_specs=[VMEM] * (1 + len(extra)),
        compiler_params=pltpu.CompilerParams(vmem_limit_bytes=8 * MIB),
    )(mine, came, after, *extra)
    return out[-1], (out[0] if extra else None)


def project_kernel(parts, after_ref, *rest):
    factors = jnp.concatenate([ref[...] for ref in rest[parts:-1]], axis=0)
    projected, first = 0.0, 0
    for ref in rest[:parts]:
        width = ref.shape[1]
        projected += lax.dot_general(
            factors[:, first : first + width], ref[...], NT, preferred_element_type=jnp.float32
        )
        first += width
    rest[-1][...] = projected.astype(rest[-1].dtype)


def project(after, factors, tokens, dtype):
    rows = sum(chunk.shape[0] for chunk in factors)
    return pl.pallas_call(
        functools.partial(project_kernel, len(tokens)),
        out_shape=jax.ShapeDtypeStruct((rows, tokens[0].shape[0]), dtype),
        in_specs=[ANY] + [VMEM] * (len(tokens) + len(factors)),
        out_specs=VMEM,
        compiler_params=pltpu.CompilerParams(vmem_limit_bytes=16 * MIB),
    )(after, *tokens, *factors)


def score_kernel(count, counts_ref, *refs):
    out_ref = refs[-1]
    own = jnp.concatenate([ref[...] for ref in refs[:count]], axis=0)
    other = jnp.concatenate([ref[...] for ref in refs[count : 2 * count]], axis=0)
    product = own * other.astype(jnp.float32)
    queries, tokens = product.shape[0] // RANK, product.shape[1]
    scores = jnp.sum(product.reshape(queries, RANK, tokens), axis=1) * RANK ** (-0.5)
    out_ref[...] = jnp.zeros(out_ref.shape, jnp.float32)
    out_ref[:, :tokens] = scores
    docs = counts_ref.shape[1]
    row = lax.broadcasted_iota(jnp.int32, (docs, 1), 0)
    column = lax.broadcasted_iota(jnp.int32, (1, docs), 1)
    starts, ends = jnp.zeros((docs, 1), jnp.int32), jnp.zeros((docs, 1), jnp.int32)
    counts = jnp.ones((1, docs), jnp.int32)
    end = jnp.int32(0)
    for k in range(docs):
        start, end = end, end + counts_ref[0, k]
        starts, ends = jnp.where(row == k, start, starts), jnp.where(row == k, end, ends)
        counts = jnp.where(column == k, end - start, counts)
    position = lax.broadcasted_iota(jnp.int32, (docs, tokens), 1)
    member = ((position >= starts) & (position < ends)).astype(jnp.float32)
    pooled = lax.dot_general(
        scores, member, NT, precision=lax.Precision.HIGHEST, preferred_element_type=jnp.float32
    )
    pooled = pooled / jnp.sqrt(counts.astype(jnp.float32))
    out_ref[:, tokens : tokens + pooled.shape[1]] = pooled


def score(counts, own, other):
    rows = sum(piece.shape[0] for piece in own)
    width = (own[0].shape[1] + counts.shape[1] + LANES - 1) // LANES * LANES
    return pl.pallas_call(
        functools.partial(score_kernel, len(own)),
        out_shape=jax.ShapeDtypeStruct((rows // RANK, width), jnp.float32),
        in_specs=[pl.BlockSpec(memory_space=pltpu.SMEM)] + [VMEM] * (2 * len(own)),
        out_specs=VMEM,
        compiler_params=pltpu.CompilerParams(vmem_limit_bytes=16 * MIB),
    )(counts, *own, *other)


def chunk_rows(spread):
    return spread // 8 if spread % 128 == 0 else RANK


def is_power(number):
    return number & (number - 1) == 0


def per_device(
    acts,
    grads,
    basis_in,
    output_eigen_basis,
    query_in,
    query_out,
    doc_counts,
    pair_query,
    pair_device,
    pair_doc,
):
    n = lax.axis_size("dp")
    layers = lax.axis_size("layer")
    z = lax.axis_index("dp")
    spread = query_in.shape[2]
    queries = spread // RANK
    half = n // 2
    rows = chunk_rows(spread)
    chunks = spread // rows

    first, send, basis, turned = first_pull(
        basis_in[0], output_eigen_basis[0], query_in[0], query_out[0], rows
    )
    own = [first] + list(pull(first, turned, basis, rows))
    tokens, theirs = deal(own[-1], acts[0], grads[0])
    swap = [(0, 1), (1, 0)]

    stages = [("in", hop) for hop in range(half - 1)] + [("mid", 0)]
    stages += [("out", hop) for hop in range(half - 2, -1, -1)]
    last = len(stages) - 1

    def transfer(kinds, hop, value):
        pairs = []
        if "in" in kinds:
            pairs += [(hop, hop + 1), (n - 1 - hop, n - 2 - hop)]
        if "mid" in kinds:
            pairs += [(half - 1, half), (half, half - 1)]
        if "out" in kinds:
            pairs += [(hop + 1, hop), (n - 2 - hop, n - 1 - hop)]
        return lax.ppermute(value, "dp", pairs)

    short = n == 4
    part, came = list(own), [None] * chunks
    ahead = min(2, chunks)
    early = came[0] = transfer(("in", "out") if short else ("in",), 0, send)
    for c in range(1, ahead):
        came[c] = transfer(("in",), 0, part[c])
    others = [lax.ppermute(piece, "parts", swap) for piece in theirs]
    after = own[0]
    waiting, mine, back = [], [], []

    def project_waiting(after):
        factors = [factor for _, factor in sorted(waiting, key=lambda entry: entry[0])]
        away = project(after, factors, others, jnp.bfloat16)
        back.append(lax.ppermute(away, "parts", swap))
        mine.append(project(away, factors, [tokens], jnp.float32))
        waiting.clear()
        return mine[-1]

    pace = None
    swapped = set()
    turns = chunks + last - short
    for turn in range(turns):
        steps = [(s, turn - s) for s in range(last) if 0 <= turn - s < chunks]
        due = [c for c in range(chunks) if c + last + (c in swapped) == turn]
        for s, c in steps + [(last, c) for c in due]:
            kind, hop = stages[s]
            if short and c == chunks - 1:
                if s == 0:
                    after = part[c] = pair(after, own[c], came[c], early)
                    came[c] = lax.ppermute(part[c], "dp", [(i, i ^ 2) for i in range(n)])
                elif s == 1:
                    part[c], _ = total(after, part[c], came[c])
                    after = part[c]
                    waiting.append((c, part[c]))
                continue
            later = turn + ahead if turn + ahead < chunks else None
            if turn >= last - 1:
                use = later if s == last - 1 else None
            else:
                use = later if s == 0 else None
            shared = use is not None and turn >= last - 1
            chunk = None if use is None else own[use]
            if kind == "out":
                part[c], send = take(after, hop, part[c], came[c], chunk)
            else:
                part[c], send = total(after, part[c], came[c], chunk, shared, pace if s == 0 else None)
            if s == 0 and kind == "in" and layers % 2 == 0:
                pace = lax.ppermute(part[c], "layer", [(i, i ^ 1) for i in range(layers)])
            after = part[c]
            if shared:
                came[c] = came[use] = transfer(("in", "out"), 0, send)
                swapped.add(c)
                continue
            if use is not None:
                came[use] = transfer(stages[0][:1], stages[0][1], send)
            if s < last:
                came[c] = transfer(stages[s + 1][:1], stages[s + 1][1], part[c])
            else:
                waiting.append((c, part[c]))
        if turn >= turns - 2 and waiting:
            after = project_waiting(after)

    scores = score(doc_counts, mine, back)
    if not is_power(layers):
        scores = lax.psum(scores, "layer")
    else:
        for step in [1 << k for k in range(layers.bit_length() - 1)]:
            scores = scores + lax.ppermute(scores, "layer", [(i, i ^ step) for i in range(layers)])
    tokens_here, docs = acts.shape[1], doc_counts.shape[1]
    token_scores, pooled = scores[:, :tokens_here], scores[:, tokens_here : tokens_here + docs]

    cells = queries * docs
    flat = pooled.reshape(1, cells)
    target = pair_device[:, 0]
    cell = pair_query * docs + pair_doc
    if n <= 8 and is_power(n):
        table = jnp.concatenate(
            [flat] + [lax.ppermute(flat, "dp", [(i, i ^ k ^ (k >> 1)) for i in range(n)]) for k in range(1, n)], axis=1
        )
        away = z ^ target
        column = (away ^ (away >> 1) ^ (away >> 2)) * cells + cell
    else:
        table = lax.all_gather(flat, "dp", axis=1, tiled=True)
        column = target * cells + cell
    hit = column[:, None] == jnp.arange(n * cells, dtype=jnp.int32)[None, :]
    pair_scores = jnp.sum(jnp.where(hit, table, 0.0), axis=1)
    return (token_scores, pair_scores)


def solution(mesh):
    in_specs = (
        P("layer", ("parts", "dp"), None),
        P("layer", ("parts", "dp"), None),
        P("layer", None, "dp"),
        P("layer", None, "dp"),
        P("layer", "dp", None),
        P("layer", "dp", None),
        P(("parts", "dp"), None),
        P(("parts", "dp")),
        P(("parts", "dp"), None),
        P(("parts", "dp")),
    )
    out_specs = (P(None, ("parts", "dp")), P(("parts", "dp")))
    return jax.shard_map(
        per_device, mesh=mesh, in_specs=in_specs, out_specs=out_specs, check_vma=False
    )
```

```python
import functools

import jax
import jax.numpy as jnp
from jax import lax
from jax.experimental import pallas as pl
from jax.experimental.pallas import tpu as pltpu
from jax.sharding import PartitionSpec as P

RANK = 32
NT = (((1,), (1,)), ((), ()))


VMEM = pl.BlockSpec(memory_space=pltpu.VMEM)
HBM = pl.BlockSpec(memory_space=pltpu.HBM)
ANY = pl.BlockSpec(memory_space=pl.ANY)
MIB = 1024 * 1024
LANES = 128


def in_hbm(*arrays):
    return [pltpu.with_memory_space_constraint(array, pltpu.HBM) for array in arrays]


def bf16(*shape):
    return jax.ShapeDtypeStruct(shape, jnp.bfloat16)


def at_depth(hop):
    z = lax.axis_index("dp")
    return jnp.minimum(z, lax.axis_size("dp") - 1 - z) == hop


def first_pull_kernel(
    basis_in_ref, basis_out_ref, query_in_ref, query_out_ref, out_ref, send_ref, basis_ref, query_ref, turned_ref, sems
):
    rows = out_ref.shape[0]
    features = basis_ref.shape[0]
    block = 512 if features % 512 == 0 else features
    spans = [pl.ds(first, block) for first in range(0, features, block)]

    def copies(from_basis, from_query):
        return [pltpu.make_async_copy(from_query, query_ref, sems.at[0])] + [
            pltpu.make_async_copy(from_basis.at[span], basis_ref.at[span], sems.at[1 + i])
            for i, span in enumerate(spans)
        ]

    side = lax.axis_index("parts")

    @pl.when(side == 0)
    def _():
        for copy in copies(basis_in_ref, query_in_ref):
            copy.start()

    @pl.when(side != 0)
    def _():
        for copy in copies(basis_out_ref, query_out_ref):
            copy.start()

    landed = copies(basis_in_ref, query_in_ref)
    landed[0].wait()
    turned_ref[...] = query_ref[...].T
    first = pl.multiple_of(jnp.where(at_depth(0), 0, turned_ref.shape[0] - rows), rows)
    factors = jnp.concatenate([turned_ref[:rows], turned_ref[pl.ds(first, rows)]], axis=0)
    for copy, span in zip(landed[1:], spans):
        copy.wait()
        pulled = lax.dot_general(factors, basis_ref[span], NT, preferred_element_type=jnp.float32)
        pulled = pulled.astype(jnp.bfloat16)
        out_ref[:, span] = pulled[:rows]
        send_ref[:, span] = pulled[rows:]


def first_pull(basis_in, basis_out, query_in, query_out, rows):
    features, depth = basis_in.shape
    spread = query_in.shape[1]
    blocks = features // 512 if features % 512 == 0 else 1
    out, send, basis, _, turned = pl.pallas_call(
        first_pull_kernel,
        out_shape=[bf16(rows, features)] * 2 + [bf16(features, depth), bf16(depth, spread), bf16(spread, depth)],
        in_specs=[HBM] * 4,
        out_specs=[VMEM] * 5,
        scratch_shapes=[pltpu.SemaphoreType.DMA((1 + blocks,))],
        compiler_params=pltpu.CompilerParams(vmem_limit_bytes=16 * MIB),
    )(*in_hbm(basis_in, basis_out, query_in, query_out))
    return out, send, basis, turned


def pull_kernel(turned_ref, basis_ref, after_ref, *outs):
    rows, features = outs[0].shape
    block = 512 if features % 512 == 0 else features
    for i in range(features // block):
        pulled = lax.dot_general(
            turned_ref[rows:], basis_ref[i * block : (i + 1) * block], NT, preferred_element_type=jnp.float32
        ).astype(jnp.bfloat16)
        for c, out in enumerate(outs):
            out[:, i * block : (i + 1) * block] = pulled[c * rows : (c + 1) * rows]


def pull(after, turned, basis, rows):
    chunks = turned.shape[0] // rows - 1
    return pl.pallas_call(
        pull_kernel,
        out_shape=[bf16(rows, basis.shape[0])] * chunks,
        in_specs=[VMEM, VMEM, ANY],
        out_specs=[VMEM] * chunks,
        compiler_params=pltpu.CompilerParams(vmem_limit_bytes=16 * MIB),
    )(turned, basis, after)


def deal_kernel(acts_ref, grads_ref, after_ref, *rest):
    outs, sems = rest[:-1], rest[-1]

    def copies(mine, theirs):
        pairs, first = [(mine, outs[0])], 0
        for out in outs[1:]:
            pairs.append((theirs.at[:, pl.ds(first, out.shape[1])], out))
            first += out.shape[1]
        return [pltpu.make_async_copy(source, target, sems.at[i]) for i, (source, target) in enumerate(pairs)]

    side = lax.axis_index("parts")

    @pl.when(side == 0)
    def _():
        for copy in copies(acts_ref, grads_ref):
            copy.start()

    @pl.when(side != 0)
    def _():
        for copy in copies(grads_ref, acts_ref):
            copy.start()

    for copy in copies(acts_ref, grads_ref):
        copy.wait()


def deal(after, acts, grads):
    tokens, features = acts.shape
    larger = features * 3 // 4
    widths = [larger, features - larger] if larger % LANES == 0 else [features]
    out = pl.pallas_call(
        deal_kernel,
        out_shape=[bf16(tokens, features)] + [bf16(tokens, width) for width in widths],
        in_specs=[HBM, HBM, ANY],
        out_specs=[VMEM] * (1 + len(widths)),
        scratch_shapes=[pltpu.SemaphoreType.DMA((1 + len(widths),))],
        compiler_params=pltpu.CompilerParams(vmem_limit_bytes=8 * MIB),
    )(*in_hbm(acts, grads), after)
    return out[0], out[1:]


def write_send(later_ref, value_ref, send_ref):
    @pl.when(at_depth(0))
    def _():
        send_ref[...] = later_ref[...]

    @pl.when(jnp.logical_not(at_depth(0)))
    def _():
        send_ref[...] = value_ref[...]


def pair_kernel(mine_ref, came_ref, early_ref, after_ref, out_ref):
    @pl.when(at_depth(0))
    def _():
        out_ref[...] = (mine_ref[...].astype(jnp.float32) + early_ref[...].astype(jnp.float32)).astype(jnp.bfloat16)

    @pl.when(jnp.logical_not(at_depth(0)))
    def _():
        out_ref[...] = (mine_ref[...].astype(jnp.float32) + came_ref[...].astype(jnp.float32)).astype(jnp.bfloat16)


def pair(after, mine, came, early):
    return pl.pallas_call(
        pair_kernel,
        out_shape=bf16(*mine.shape),
        in_specs=[VMEM, VMEM, VMEM, ANY],
        out_specs=VMEM,
        compiler_params=pltpu.CompilerParams(vmem_limit_bytes=8 * MIB),
    )(mine, came, early, after)


def total_kernel(shared, mine_ref, came_ref, after_ref, *rest):
    mine = mine_ref[...].astype(jnp.float32) + came_ref[...].astype(jnp.float32)
    rest[-1][...] = mine.astype(jnp.bfloat16)
    if shared:
        write_send(rest[0], rest[2], rest[1])
    elif len(rest) == 3:
        rest[1][...] = rest[0][...]


def total(after, mine, came, later=None, shared=False):
    extra = [] if later is None else [later]
    out = pl.pallas_call(
        functools.partial(total_kernel, shared),
        out_shape=[bf16(*a.shape) for a in extra + [mine]],
        in_specs=[VMEM, VMEM, ANY] + [VMEM] * len(extra),
        out_specs=[VMEM] * (1 + len(extra)),
        compiler_params=pltpu.CompilerParams(vmem_limit_bytes=8 * MIB),
    )(mine, came, after, *extra)
    return out[-1], (out[0] if extra else None)


def take_kernel(hop, shared, mine_ref, came_ref, after_ref, *rest):
    @pl.when(at_depth(hop))
    def _():
        rest[-1][...] = came_ref[...]

    @pl.when(jnp.logical_not(at_depth(hop)))
    def _():
        rest[-1][...] = mine_ref[...]

    if shared:
        write_send(rest[0], rest[2], rest[1])


def take(after, hop, mine, came, later=None):
    extra = [] if later is None else [later]
    out = pl.pallas_call(
        functools.partial(take_kernel, hop, later is not None),
        out_shape=[bf16(*a.shape) for a in extra + [mine]],
        in_specs=[VMEM, VMEM, ANY] + [VMEM] * len(extra),
        out_specs=[VMEM] * (1 + len(extra)),
        compiler_params=pltpu.CompilerParams(vmem_limit_bytes=8 * MIB),
    )(mine, came, after, *extra)
    return out[-1], (out[0] if extra else None)


def project_kernel(parts, after_ref, *rest):
    factors = jnp.concatenate([ref[...] for ref in rest[parts:-1]], axis=0)
    projected, first = 0.0, 0
    for ref in rest[:parts]:
        width = ref.shape[1]
        projected += lax.dot_general(
            factors[:, first : first + width], ref[...], NT, preferred_element_type=jnp.float32
        )
        first += width
    rest[-1][...] = projected.astype(rest[-1].dtype)


def project(after, factors, tokens, dtype):
    rows = sum(chunk.shape[0] for chunk in factors)
    return pl.pallas_call(
        functools.partial(project_kernel, len(tokens)),
        out_shape=jax.ShapeDtypeStruct((rows, tokens[0].shape[0]), dtype),
        in_specs=[ANY] + [VMEM] * (len(tokens) + len(factors)),
        out_specs=VMEM,
        compiler_params=pltpu.CompilerParams(vmem_limit_bytes=16 * MIB),
    )(after, *tokens, *factors)


def score_kernel(count, counts_ref, *refs):
    out_ref = refs[-1]
    own = jnp.concatenate([ref[...] for ref in refs[:count]], axis=0)
    other = jnp.concatenate([ref[...] for ref in refs[count : 2 * count]], axis=0)
    product = own * other.astype(jnp.float32)
    queries, tokens = product.shape[0] // RANK, product.shape[1]
    scores = jnp.sum(product.reshape(queries, RANK, tokens), axis=1) * RANK ** (-0.5)
    out_ref[...] = jnp.zeros(out_ref.shape, jnp.float32)
    out_ref[:, :tokens] = scores
    docs = counts_ref.shape[1]
    row = lax.broadcasted_iota(jnp.int32, (docs, 1), 0)
    column = lax.broadcasted_iota(jnp.int32, (1, docs), 1)
    starts, ends = jnp.zeros((docs, 1), jnp.int32), jnp.zeros((docs, 1), jnp.int32)
    counts = jnp.ones((1, docs), jnp.int32)
    end = jnp.int32(0)
    for k in range(docs):
        start, end = end, end + counts_ref[0, k]
        starts, ends = jnp.where(row == k, start, starts), jnp.where(row == k, end, ends)
        counts = jnp.where(column == k, end - start, counts)
    position = lax.broadcasted_iota(jnp.int32, (docs, tokens), 1)
    member = ((position >= starts) & (position < ends)).astype(jnp.float32)
    pooled = lax.dot_general(
        scores, member, NT, precision=lax.Precision.HIGHEST, preferred_element_type=jnp.float32
    )
    pooled = pooled / jnp.sqrt(counts.astype(jnp.float32))
    out_ref[:, tokens : tokens + pooled.shape[1]] = pooled


def score(counts, own, other):
    rows = sum(piece.shape[0] for piece in own)
    width = (own[0].shape[1] + counts.shape[1] + LANES - 1) // LANES * LANES
    return pl.pallas_call(
        functools.partial(score_kernel, len(own)),
        out_shape=jax.ShapeDtypeStruct((rows // RANK, width), jnp.float32),
        in_specs=[pl.BlockSpec(memory_space=pltpu.SMEM)] + [VMEM] * (2 * len(own)),
        out_specs=VMEM,
        compiler_params=pltpu.CompilerParams(vmem_limit_bytes=16 * MIB),
    )(counts, *own, *other)


def chunk_rows(spread):
    return spread // 8 if spread % 128 == 0 else RANK


def is_power(number):
    return number & (number - 1) == 0


def per_device(
    acts,
    grads,
    basis_in,
    output_eigen_basis,
    query_in,
    query_out,
    doc_counts,
    pair_query,
    pair_device,
    pair_doc,
):
    n = lax.axis_size("dp")
    layers = lax.axis_size("layer")
    z = lax.axis_index("dp")
    spread = query_in.shape[2]
    queries = spread // RANK
    half = n // 2
    rows = chunk_rows(spread)
    chunks = spread // rows

    first, send, basis, turned = first_pull(
        basis_in[0], output_eigen_basis[0], query_in[0], query_out[0], rows
    )
    own = [first] + list(pull(first, turned, basis, rows))
    tokens, theirs = deal(own[-1], acts[0], grads[0])
    swap = [(0, 1), (1, 0)]

    stages = [("in", hop) for hop in range(half - 1)] + [("mid", 0)]
    stages += [("out", hop) for hop in range(half - 2, -1, -1)]
    last = len(stages) - 1

    def transfer(kinds, hop, value):
        pairs = []
        if "in" in kinds:
            pairs += [(hop, hop + 1), (n - 1 - hop, n - 2 - hop)]
        if "mid" in kinds:
            pairs += [(half - 1, half), (half, half - 1)]
        if "out" in kinds:
            pairs += [(hop + 1, hop), (n - 2 - hop, n - 1 - hop)]
        return lax.ppermute(value, "dp", pairs)

    short = n == 4
    part, came = list(own), [None] * chunks
    ahead = min(2, chunks)
    early = came[0] = transfer(("in", "out") if short else ("in",), 0, send)
    for c in range(1, ahead):
        came[c] = transfer(("in",), 0, part[c])
    others = [lax.ppermute(piece, "parts", swap) for piece in theirs]
    after = own[0]
    waiting, mine, back = [], [], []

    def project_waiting(after):
        factors = [factor for _, factor in sorted(waiting, key=lambda entry: entry[0])]
        away = project(after, factors, others, jnp.bfloat16)
        back.append(lax.ppermute(away, "parts", swap))
        mine.append(project(away, factors, [tokens], jnp.float32))
        waiting.clear()
        return mine[-1]

    swapped = set()
    turns = chunks + last - short
    for turn in range(turns):
        steps = [(s, turn - s) for s in range(last) if 0 <= turn - s < chunks]
        due = [c for c in range(chunks) if c + last + (c in swapped) == turn]
        order = steps + [(last, c) for c in due]
        if short and turn == chunks - 1:
            order = [(last, c) for c in due if c in swapped] + steps[::-1] + [(last, c) for c in due if c not in swapped]
        for s, c in order:
            kind, hop = stages[s]
            if short and c == chunks - 1:
                if s == 0:
                    after = part[c] = pair(after, own[c], came[c], early)
                    came[c] = lax.ppermute(part[c], "dp", [(i, i ^ 2) for i in range(n)])
                elif s == 1:
                    part[c], _ = total(after, part[c], came[c])
                    after = part[c]
                    waiting.append((c, part[c]))
                continue
            later = turn + ahead if turn + ahead < chunks else None
            if turn >= last - 1:
                use = later if s == last - 1 else None
            else:
                use = later if s == 0 else None
            shared = use is not None and turn >= last - 1
            chunk = None if use is None else own[use]
            if kind == "out":
                part[c], send = take(after, hop, part[c], came[c], chunk)
            else:
                part[c], send = total(after, part[c], came[c], chunk, shared)
            after = part[c]
            if shared:
                came[c] = came[use] = transfer(("in", "out"), 0, send)
                swapped.add(c)
                continue
            if use is not None:
                came[use] = transfer(stages[0][:1], stages[0][1], send)
            if s < last:
                came[c] = transfer(stages[s + 1][:1], stages[s + 1][1], part[c])
            else:
                waiting.append((c, part[c]))
        if turn >= turns - 2 and waiting:
            after = project_waiting(after)

    scores = score(doc_counts, mine, back)
    if not is_power(layers):
        scores = lax.psum(scores, "layer")
    else:
        for step in [1 << k for k in range(layers.bit_length() - 1)]:
            scores = scores + lax.ppermute(scores, "layer", [(i, i ^ step) for i in range(layers)])
    tokens_here, docs = acts.shape[1], doc_counts.shape[1]
    token_scores, pooled = scores[:, :tokens_here], scores[:, tokens_here : tokens_here + docs]

    cells = queries * docs
    flat = pooled.reshape(1, cells)
    target = pair_device[:, 0]
    cell = pair_query * docs + pair_doc
    if n <= 8 and is_power(n):
        table = jnp.concatenate(
            [flat] + [lax.ppermute(flat, "dp", [(i, i ^ k ^ (k >> 1)) for i in range(n)]) for k in range(1, n)], axis=1
        )
        away = z ^ target
        column = (away ^ (away >> 1) ^ (away >> 2)) * cells + cell
    else:
        table = lax.all_gather(flat, "dp", axis=1, tiled=True)
        column = target * cells + cell
    hit = column[:, None] == jnp.arange(n * cells, dtype=jnp.int32)[None, :]
    pair_scores = jnp.sum(jnp.where(hit, table, 0.0), axis=1)
    return (token_scores, pair_scores)


def solution(mesh):
    in_specs = (
        P("layer", ("parts", "dp"), None),
        P("layer", ("parts", "dp"), None),
        P("layer", None, "dp"),
        P("layer", None, "dp"),
        P("layer", "dp", None),
        P("layer", "dp", None),
        P(("parts", "dp"), None),
        P(("parts", "dp")),
        P(("parts", "dp"), None),
        P(("parts", "dp")),
    )
    out_specs = (P(None, ("parts", "dp")), P(("parts", "dp")))
    return jax.shard_map(
        per_device, mesh=mesh, in_specs=in_specs, out_specs=out_specs, check_vma=False
    )
```

```python
import functools

import jax
import jax.numpy as jnp
from jax import lax
from jax.experimental import pallas as pl
from jax.experimental.pallas import tpu as pltpu
from jax.sharding import PartitionSpec as P

RANK = 32
NT = (((1,), (1,)), ((), ()))


VMEM = pl.BlockSpec(memory_space=pltpu.VMEM)
HBM = pl.BlockSpec(memory_space=pltpu.HBM)
ANY = pl.BlockSpec(memory_space=pl.ANY)
MIB = 1024 * 1024
LANES = 128


def in_hbm(*arrays):
    return [pltpu.with_memory_space_constraint(array, pltpu.HBM) for array in arrays]


def bf16(*shape):
    return jax.ShapeDtypeStruct(shape, jnp.bfloat16)


def at_depth(hop):
    z = lax.axis_index("dp")
    return jnp.minimum(z, lax.axis_size("dp") - 1 - z) == hop


def first_pull_kernel(
    basis_in_ref, basis_out_ref, query_in_ref, query_out_ref, out_ref, send_ref, basis_ref, query_ref, turned_ref, sems
):
    rows = out_ref.shape[0]
    features = basis_ref.shape[0]
    block = 512 if features % 512 == 0 else features
    spans = [pl.ds(first, block) for first in range(0, features, block)]

    def copies(from_basis, from_query):
        return [pltpu.make_async_copy(from_query, query_ref, sems.at[0])] + [
            pltpu.make_async_copy(from_basis.at[span], basis_ref.at[span], sems.at[1 + i])
            for i, span in enumerate(spans)
        ]

    side = lax.axis_index("parts")

    @pl.when(side == 0)
    def _():
        for copy in copies(basis_in_ref, query_in_ref):
            copy.start()

    @pl.when(side != 0)
    def _():
        for copy in copies(basis_out_ref, query_out_ref):
            copy.start()

    landed = copies(basis_in_ref, query_in_ref)
    landed[0].wait()
    turned_ref[...] = query_ref[...].T
    first = pl.multiple_of(jnp.where(at_depth(0), 0, turned_ref.shape[0] - rows), rows)
    factors = jnp.concatenate([turned_ref[:rows], turned_ref[pl.ds(first, rows)]], axis=0)
    for copy, span in zip(landed[1:], spans):
        copy.wait()
        pulled = lax.dot_general(factors, basis_ref[span], NT, preferred_element_type=jnp.float32)
        pulled = pulled.astype(jnp.bfloat16)
        out_ref[:, span] = pulled[:rows]
        send_ref[:, span] = pulled[rows:]


def first_pull(basis_in, basis_out, query_in, query_out, rows):
    features, depth = basis_in.shape
    spread = query_in.shape[1]
    blocks = features // 512 if features % 512 == 0 else 1
    out, send, basis, _, turned = pl.pallas_call(
        first_pull_kernel,
        out_shape=[bf16(rows, features)] * 2 + [bf16(features, depth), bf16(depth, spread), bf16(spread, depth)],
        in_specs=[HBM] * 4,
        out_specs=[VMEM] * 5,
        scratch_shapes=[pltpu.SemaphoreType.DMA((1 + blocks,))],
        compiler_params=pltpu.CompilerParams(vmem_limit_bytes=16 * MIB),
    )(*in_hbm(basis_in, basis_out, query_in, query_out))
    return out, send, basis, turned


def pull_kernel(turned_ref, basis_ref, after_ref, *outs):
    rows, features = outs[0].shape
    block = 512 if features % 512 == 0 else features
    for i in range(features // block):
        pulled = lax.dot_general(
            turned_ref[rows:], basis_ref[i * block : (i + 1) * block], NT, preferred_element_type=jnp.float32
        ).astype(jnp.bfloat16)
        for c, out in enumerate(outs):
            out[:, i * block : (i + 1) * block] = pulled[c * rows : (c + 1) * rows]


def pull(after, turned, basis, rows):
    chunks = turned.shape[0] // rows - 1
    return pl.pallas_call(
        pull_kernel,
        out_shape=[bf16(rows, basis.shape[0])] * chunks,
        in_specs=[VMEM, VMEM, ANY],
        out_specs=[VMEM] * chunks,
        compiler_params=pltpu.CompilerParams(vmem_limit_bytes=16 * MIB),
    )(turned, basis, after)


def deal_kernel(acts_ref, grads_ref, after_ref, *rest):
    outs, sems = rest[:-1], rest[-1]

    def copies(mine, theirs):
        pairs, first = [(mine, outs[0])], 0
        for out in outs[1:]:
            pairs.append((theirs.at[:, pl.ds(first, out.shape[1])], out))
            first += out.shape[1]
        return [pltpu.make_async_copy(source, target, sems.at[i]) for i, (source, target) in enumerate(pairs)]

    side = lax.axis_index("parts")

    @pl.when(side == 0)
    def _():
        for copy in copies(acts_ref, grads_ref):
            copy.start()

    @pl.when(side != 0)
    def _():
        for copy in copies(grads_ref, acts_ref):
            copy.start()

    for copy in copies(acts_ref, grads_ref):
        copy.wait()


def deal(after, acts, grads):
    tokens, features = acts.shape
    larger = features * 13 // 20
    widths = [larger, features - larger] if larger % LANES == 0 else [features]
    out = pl.pallas_call(
        deal_kernel,
        out_shape=[bf16(tokens, features)] + [bf16(tokens, width) for width in widths],
        in_specs=[HBM, HBM, ANY],
        out_specs=[VMEM] * (1 + len(widths)),
        scratch_shapes=[pltpu.SemaphoreType.DMA((1 + len(widths),))],
        compiler_params=pltpu.CompilerParams(vmem_limit_bytes=8 * MIB),
    )(*in_hbm(acts, grads), after)
    return out[0], out[1:]


def write_send(later_ref, value_ref, send_ref):
    @pl.when(at_depth(0))
    def _():
        send_ref[...] = later_ref[...]

    @pl.when(jnp.logical_not(at_depth(0)))
    def _():
        send_ref[...] = value_ref[...]


def pair_kernel(mine_ref, came_ref, early_ref, after_ref, out_ref):
    @pl.when(at_depth(0))
    def _():
        out_ref[...] = (mine_ref[...].astype(jnp.float32) + early_ref[...].astype(jnp.float32)).astype(jnp.bfloat16)

    @pl.when(jnp.logical_not(at_depth(0)))
    def _():
        out_ref[...] = (mine_ref[...].astype(jnp.float32) + came_ref[...].astype(jnp.float32)).astype(jnp.bfloat16)


def pair(after, mine, came, early):
    return pl.pallas_call(
        pair_kernel,
        out_shape=bf16(*mine.shape),
        in_specs=[VMEM, VMEM, VMEM, ANY],
        out_specs=VMEM,
        compiler_params=pltpu.CompilerParams(vmem_limit_bytes=8 * MIB),
    )(mine, came, early, after)


def total_kernel(shared, mine_ref, came_ref, after_ref, *rest):
    mine = mine_ref[...].astype(jnp.float32) + came_ref[...].astype(jnp.float32)
    rest[-1][...] = mine.astype(jnp.bfloat16)
    if shared:
        write_send(rest[0], rest[2], rest[1])
    elif len(rest) == 3:
        rest[1][...] = rest[0][...]


def total(after, mine, came, later=None, shared=False):
    extra = [] if later is None else [later]
    out = pl.pallas_call(
        functools.partial(total_kernel, shared),
        out_shape=[bf16(*a.shape) for a in extra + [mine]],
        in_specs=[VMEM, VMEM, ANY] + [VMEM] * len(extra),
        out_specs=[VMEM] * (1 + len(extra)),
        compiler_params=pltpu.CompilerParams(vmem_limit_bytes=8 * MIB),
    )(mine, came, after, *extra)
    return out[-1], (out[0] if extra else None)


def take_kernel(hop, shared, mine_ref, came_ref, after_ref, *rest):
    @pl.when(at_depth(hop))
    def _():
        rest[-1][...] = came_ref[...]

    @pl.when(jnp.logical_not(at_depth(hop)))
    def _():
        rest[-1][...] = mine_ref[...]

    if shared:
        write_send(rest[0], rest[2], rest[1])


def take(after, hop, mine, came, later=None):
    extra = [] if later is None else [later]
    out = pl.pallas_call(
        functools.partial(take_kernel, hop, later is not None),
        out_shape=[bf16(*a.shape) for a in extra + [mine]],
        in_specs=[VMEM, VMEM, ANY] + [VMEM] * len(extra),
        out_specs=[VMEM] * (1 + len(extra)),
        compiler_params=pltpu.CompilerParams(vmem_limit_bytes=8 * MIB),
    )(mine, came, after, *extra)
    return out[-1], (out[0] if extra else None)


def project_kernel(parts, after_ref, *rest):
    factors = jnp.concatenate([ref[...] for ref in rest[parts:-1]], axis=0)
    projected, first = 0.0, 0
    for ref in rest[:parts]:
        width = ref.shape[1]
        projected += lax.dot_general(
            factors[:, first : first + width], ref[...], NT, preferred_element_type=jnp.float32
        )
        first += width
    rest[-1][...] = projected.astype(rest[-1].dtype)


def project(after, factors, tokens, dtype):
    rows = sum(chunk.shape[0] for chunk in factors)
    return pl.pallas_call(
        functools.partial(project_kernel, len(tokens)),
        out_shape=jax.ShapeDtypeStruct((rows, tokens[0].shape[0]), dtype),
        in_specs=[ANY] + [VMEM] * (len(tokens) + len(factors)),
        out_specs=VMEM,
        compiler_params=pltpu.CompilerParams(vmem_limit_bytes=16 * MIB),
    )(after, *tokens, *factors)


def score_kernel(count, counts_ref, *refs):
    out_ref = refs[-1]
    own = jnp.concatenate([ref[...] for ref in refs[:count]], axis=0)
    other = jnp.concatenate([ref[...] for ref in refs[count : 2 * count]], axis=0)
    product = own * other.astype(jnp.float32)
    queries, tokens = product.shape[0] // RANK, product.shape[1]
    scores = jnp.sum(product.reshape(queries, RANK, tokens), axis=1) * RANK ** (-0.5)
    out_ref[...] = jnp.zeros(out_ref.shape, jnp.float32)
    out_ref[:, :tokens] = scores
    docs = counts_ref.shape[1]
    row = lax.broadcasted_iota(jnp.int32, (docs, 1), 0)
    column = lax.broadcasted_iota(jnp.int32, (1, docs), 1)
    starts, ends = jnp.zeros((docs, 1), jnp.int32), jnp.zeros((docs, 1), jnp.int32)
    counts = jnp.ones((1, docs), jnp.int32)
    end = jnp.int32(0)
    for k in range(docs):
        start, end = end, end + counts_ref[0, k]
        starts, ends = jnp.where(row == k, start, starts), jnp.where(row == k, end, ends)
        counts = jnp.where(column == k, end - start, counts)
    position = lax.broadcasted_iota(jnp.int32, (docs, tokens), 1)
    member = ((position >= starts) & (position < ends)).astype(jnp.float32)
    pooled = lax.dot_general(
        scores, member, NT, precision=lax.Precision.HIGHEST, preferred_element_type=jnp.float32
    )
    pooled = pooled / jnp.sqrt(counts.astype(jnp.float32))
    out_ref[:, tokens : tokens + pooled.shape[1]] = pooled


def score(counts, own, other):
    rows = sum(piece.shape[0] for piece in own)
    width = (own[0].shape[1] + counts.shape[1] + LANES - 1) // LANES * LANES
    return pl.pallas_call(
        functools.partial(score_kernel, len(own)),
        out_shape=jax.ShapeDtypeStruct((rows // RANK, width), jnp.float32),
        in_specs=[pl.BlockSpec(memory_space=pltpu.SMEM)] + [VMEM] * (2 * len(own)),
        out_specs=VMEM,
        compiler_params=pltpu.CompilerParams(vmem_limit_bytes=16 * MIB),
    )(counts, *own, *other)


def chunk_rows(spread):
    return spread // 8 if spread % 128 == 0 else RANK


def is_power(number):
    return number & (number - 1) == 0


def per_device(
    acts,
    grads,
    basis_in,
    output_eigen_basis,
    query_in,
    query_out,
    doc_counts,
    pair_query,
    pair_device,
    pair_doc,
):
    n = lax.axis_size("dp")
    layers = lax.axis_size("layer")
    z = lax.axis_index("dp")
    spread = query_in.shape[2]
    queries = spread // RANK
    half = n // 2
    rows = chunk_rows(spread)
    chunks = spread // rows

    first, send, basis, turned = first_pull(
        basis_in[0], output_eigen_basis[0], query_in[0], query_out[0], rows
    )
    own = [first] + list(pull(first, turned, basis, rows))
    tokens, theirs = deal(own[-1], acts[0], grads[0])
    swap = [(0, 1), (1, 0)]

    stages = [("in", hop) for hop in range(half - 1)] + [("mid", 0)]
    stages += [("out", hop) for hop in range(half - 2, -1, -1)]
    last = len(stages) - 1

    def transfer(kinds, hop, value):
        pairs = []
        if "in" in kinds:
            pairs += [(hop, hop + 1), (n - 1 - hop, n - 2 - hop)]
        if "mid" in kinds:
            pairs += [(half - 1, half), (half, half - 1)]
        if "out" in kinds:
            pairs += [(hop + 1, hop), (n - 2 - hop, n - 1 - hop)]
        return lax.ppermute(value, "dp", pairs)

    short = n == 4
    part, came = list(own), [None] * chunks
    ahead = min(2, chunks)
    early = came[0] = transfer(("in", "out") if short else ("in",), 0, send)
    for c in range(1, ahead):
        came[c] = transfer(("in",), 0, part[c])
    others = [lax.ppermute(piece, "parts", swap) for piece in theirs]
    after = own[0]
    waiting, mine, back = [], [], []

    def project_waiting(after):
        factors = [factor for _, factor in sorted(waiting, key=lambda entry: entry[0])]
        away = project(after, factors, others, jnp.bfloat16)
        back.append(lax.ppermute(away, "parts", swap))
        mine.append(project(away, factors, [tokens], jnp.float32))
        waiting.clear()
        return mine[-1]

    swapped = set()
    turns = chunks + last - short
    for turn in range(turns):
        steps = [(s, turn - s) for s in range(last) if 0 <= turn - s < chunks]
        due = [c for c in range(chunks) if c + last + (c in swapped) == turn]
        for s, c in steps + [(last, c) for c in due]:
            kind, hop = stages[s]
            if short and c == chunks - 1:
                if s == 0:
                    after = part[c] = pair(after, own[c], came[c], early)
                    came[c] = lax.ppermute(part[c], "dp", [(i, i ^ 2) for i in range(n)])
                elif s == 1:
                    part[c], _ = total(after, part[c], came[c])
                    after = part[c]
                    waiting.append((c, part[c]))
                continue
            later = turn + ahead if turn + ahead < chunks else None
            if turn >= last - 1:
                use = later if s == last - 1 else None
            else:
                use = later if s == 0 else None
            shared = use is not None and turn >= last - 1
            chunk = None if use is None else own[use]
            if kind == "out":
                part[c], send = take(after, hop, part[c], came[c], chunk)
            else:
                part[c], send = total(after, part[c], came[c], chunk, shared)
            after = part[c]
            if shared:
                came[c] = came[use] = transfer(("in", "out"), 0, send)
                swapped.add(c)
                continue
            if use is not None:
                came[use] = transfer(stages[0][:1], stages[0][1], send)
            if s < last:
                came[c] = transfer(stages[s + 1][:1], stages[s + 1][1], part[c])
            else:
                waiting.append((c, part[c]))
        if turn >= turns - 2 and waiting:
            after = project_waiting(after)

    scores = score(doc_counts, mine, back)
    if not is_power(layers):
        scores = lax.psum(scores, "layer")
    else:
        for step in [1 << k for k in range(layers.bit_length() - 1)]:
            scores = scores + lax.ppermute(scores, "layer", [(i, i ^ step) for i in range(layers)])
    tokens_here, docs = acts.shape[1], doc_counts.shape[1]
    token_scores, pooled = scores[:, :tokens_here], scores[:, tokens_here : tokens_here + docs]

    cells = queries * docs
    flat = pooled.reshape(1, cells)
    target = pair_device[:, 0]
    cell = pair_query * docs + pair_doc
    if n <= 8 and is_power(n):
        table = jnp.concatenate(
            [flat] + [lax.ppermute(flat, "dp", [(i, i ^ k ^ (k >> 1)) for i in range(n)]) for k in range(1, n)], axis=1
        )
        away = z ^ target
        column = (away ^ (away >> 1) ^ (away >> 2)) * cells + cell
    else:
        table = lax.all_gather(flat, "dp", axis=1, tiled=True)
        column = target * cells + cell
    hit = column[:, None] == jnp.arange(n * cells, dtype=jnp.int32)[None, :]
    pair_scores = jnp.sum(jnp.where(hit, table, 0.0), axis=1)
    return (token_scores, pair_scores)


def solution(mesh):
    in_specs = (
        P("layer", ("parts", "dp"), None),
        P("layer", ("parts", "dp"), None),
        P("layer", None, "dp"),
        P("layer", None, "dp"),
        P("layer", "dp", None),
        P("layer", "dp", None),
        P(("parts", "dp"), None),
        P(("parts", "dp")),
        P(("parts", "dp"), None),
        P(("parts", "dp")),
    )
    out_specs = (P(None, ("parts", "dp")), P(("parts", "dp")))
    return jax.shard_map(
        per_device, mesh=mesh, in_specs=in_specs, out_specs=out_specs, check_vma=False
    )
```

```python
import functools

import jax
import jax.numpy as jnp
from jax import lax
from jax.experimental import pallas as pl
from jax.experimental.pallas import tpu as pltpu
from jax.sharding import PartitionSpec as P

RANK = 32
NT = (((1,), (1,)), ((), ()))


VMEM = pl.BlockSpec(memory_space=pltpu.VMEM)
HBM = pl.BlockSpec(memory_space=pltpu.HBM)
ANY = pl.BlockSpec(memory_space=pl.ANY)
MIB = 1024 * 1024
LANES = 128


def in_hbm(*arrays):
    return [pltpu.with_memory_space_constraint(array, pltpu.HBM) for array in arrays]


def bf16(*shape):
    return jax.ShapeDtypeStruct(shape, jnp.bfloat16)


def at_depth(hop):
    z = lax.axis_index("dp")
    return jnp.minimum(z, lax.axis_size("dp") - 1 - z) == hop


def first_pull_kernel(
    basis_in_ref, basis_out_ref, query_in_ref, query_out_ref, out_ref, send_ref, basis_ref, query_ref, turned_ref, sems
):
    rows = out_ref.shape[0]
    features = basis_ref.shape[0]
    block = 512 if features % 512 == 0 else features
    spans = [pl.ds(first, block) for first in range(0, features, block)]

    def copies(from_basis, from_query):
        return [pltpu.make_async_copy(from_query, query_ref, sems.at[0])] + [
            pltpu.make_async_copy(from_basis.at[span], basis_ref.at[span], sems.at[1 + i])
            for i, span in enumerate(spans)
        ]

    side = lax.axis_index("parts")

    @pl.when(side == 0)
    def _():
        for copy in copies(basis_in_ref, query_in_ref):
            copy.start()

    @pl.when(side != 0)
    def _():
        for copy in copies(basis_out_ref, query_out_ref):
            copy.start()

    landed = copies(basis_in_ref, query_in_ref)
    landed[0].wait()
    turned_ref[...] = query_ref[...].T
    first = pl.multiple_of(jnp.where(at_depth(0), 0, turned_ref.shape[0] - rows), rows)
    factors = jnp.concatenate([turned_ref[:rows], turned_ref[pl.ds(first, rows)]], axis=0)
    for copy, span in zip(landed[1:], spans):
        copy.wait()
        pulled = lax.dot_general(factors, basis_ref[span], NT, preferred_element_type=jnp.float32)
        pulled = pulled.astype(jnp.bfloat16)
        out_ref[:, span] = pulled[:rows]
        send_ref[:, span] = pulled[rows:]


def first_pull(basis_in, basis_out, query_in, query_out, rows):
    features, depth = basis_in.shape
    spread = query_in.shape[1]
    blocks = features // 512 if features % 512 == 0 else 1
    out, send, basis, _, turned = pl.pallas_call(
        first_pull_kernel,
        out_shape=[bf16(rows, features)] * 2 + [bf16(features, depth), bf16(depth, spread), bf16(spread, depth)],
        in_specs=[HBM] * 4,
        out_specs=[VMEM] * 5,
        scratch_shapes=[pltpu.SemaphoreType.DMA((1 + blocks,))],
        compiler_params=pltpu.CompilerParams(vmem_limit_bytes=16 * MIB),
    )(*in_hbm(basis_in, basis_out, query_in, query_out))
    return out, send, basis, turned


def pull_kernel(turned_ref, basis_ref, after_ref, *outs):
    rows, features = outs[0].shape
    block = 512 if features % 512 == 0 else features
    for i in range(features // block):
        pulled = lax.dot_general(
            turned_ref[rows:], basis_ref[i * block : (i + 1) * block], NT, preferred_element_type=jnp.float32
        ).astype(jnp.bfloat16)
        for c, out in enumerate(outs):
            out[:, i * block : (i + 1) * block] = pulled[c * rows : (c + 1) * rows]


def pull(after, turned, basis, rows):
    chunks = turned.shape[0] // rows - 1
    return pl.pallas_call(
        pull_kernel,
        out_shape=[bf16(rows, basis.shape[0])] * chunks,
        in_specs=[VMEM, VMEM, ANY],
        out_specs=[VMEM] * chunks,
        compiler_params=pltpu.CompilerParams(vmem_limit_bytes=16 * MIB),
    )(turned, basis, after)


def deal_kernel(acts_ref, grads_ref, after_ref, *rest):
    outs, sems = rest[:-1], rest[-1]

    def copies(mine, theirs):
        pairs, first = [(mine, outs[0])], 0
        for out in outs[1:]:
            pairs.append((theirs.at[:, pl.ds(first, out.shape[1])], out))
            first += out.shape[1]
        return [pltpu.make_async_copy(source, target, sems.at[i]) for i, (source, target) in enumerate(pairs)]

    side = lax.axis_index("parts")

    @pl.when(side == 0)
    def _():
        for copy in copies(acts_ref, grads_ref):
            copy.start()

    @pl.when(side != 0)
    def _():
        for copy in copies(grads_ref, acts_ref):
            copy.start()

    for copy in copies(acts_ref, grads_ref):
        copy.wait()


def deal(after, acts, grads):
    tokens, features = acts.shape
    larger = features * 13 // 20
    widths = [larger, features - larger] if larger % LANES == 0 else [features]
    out = pl.pallas_call(
        deal_kernel,
        out_shape=[bf16(tokens, features)] + [bf16(tokens, width) for width in widths],
        in_specs=[HBM, HBM, ANY],
        out_specs=[VMEM] * (1 + len(widths)),
        scratch_shapes=[pltpu.SemaphoreType.DMA((1 + len(widths),))],
        compiler_params=pltpu.CompilerParams(vmem_limit_bytes=8 * MIB),
    )(*in_hbm(acts, grads), after)
    return out[0], out[1:]


def write_send(later_ref, value_ref, send_ref):
    @pl.when(at_depth(0))
    def _():
        send_ref[...] = later_ref[...]

    @pl.when(jnp.logical_not(at_depth(0)))
    def _():
        send_ref[...] = value_ref[...]


def pair_kernel(mine_ref, came_ref, early_ref, after_ref, out_ref):
    @pl.when(at_depth(0))
    def _():
        out_ref[...] = (mine_ref[...].astype(jnp.float32) + early_ref[...].astype(jnp.float32)).astype(jnp.bfloat16)

    @pl.when(jnp.logical_not(at_depth(0)))
    def _():
        out_ref[...] = (mine_ref[...].astype(jnp.float32) + came_ref[...].astype(jnp.float32)).astype(jnp.bfloat16)


def pair(after, mine, came, early):
    return pl.pallas_call(
        pair_kernel,
        out_shape=bf16(*mine.shape),
        in_specs=[VMEM, VMEM, VMEM, ANY],
        out_specs=VMEM,
        compiler_params=pltpu.CompilerParams(vmem_limit_bytes=8 * MIB),
    )(mine, came, early, after)


def join_kernel(mine_ref, one_ref, two_ref, after_ref, out_ref):
    came = one_ref[...].astype(jnp.float32) + two_ref[...].astype(jnp.float32)
    out_ref[...] = (mine_ref[...].astype(jnp.float32) + came).astype(jnp.bfloat16)


def join(after, mine, one, two):
    return pl.pallas_call(
        join_kernel,
        out_shape=bf16(*mine.shape),
        in_specs=[VMEM, VMEM, VMEM, ANY],
        out_specs=VMEM,
        compiler_params=pltpu.CompilerParams(vmem_limit_bytes=8 * MIB),
    )(mine, one, two, after)


def late_kernel(mine_ref, came_ref, after_ref, out_ref):
    here = at_depth(0) & (lax.rem(lax.axis_index("layer"), 2) == 1)

    @pl.when(here)
    def _():
        out_ref[...] = came_ref[...]

    @pl.when(jnp.logical_not(here))
    def _():
        out_ref[...] = mine_ref[...]


def late(after, mine, came):
    return pl.pallas_call(
        late_kernel,
        out_shape=bf16(*mine.shape),
        in_specs=[VMEM, VMEM, ANY],
        out_specs=VMEM,
        compiler_params=pltpu.CompilerParams(vmem_limit_bytes=8 * MIB),
    )(mine, came, after)


def total_kernel(shared, mine_ref, came_ref, after_ref, *rest):
    mine = mine_ref[...].astype(jnp.float32) + came_ref[...].astype(jnp.float32)
    rest[-1][...] = mine.astype(jnp.bfloat16)
    if shared:
        write_send(rest[0], rest[2], rest[1])
    elif len(rest) == 3:
        rest[1][...] = rest[0][...]


def total(after, mine, came, later=None, shared=False):
    extra = [] if later is None else [later]
    out = pl.pallas_call(
        functools.partial(total_kernel, shared),
        out_shape=[bf16(*a.shape) for a in extra + [mine]],
        in_specs=[VMEM, VMEM, ANY] + [VMEM] * len(extra),
        out_specs=[VMEM] * (1 + len(extra)),
        compiler_params=pltpu.CompilerParams(vmem_limit_bytes=8 * MIB),
    )(mine, came, after, *extra)
    return out[-1], (out[0] if extra else None)


def take_kernel(hop, shared, mine_ref, came_ref, after_ref, *rest):
    @pl.when(at_depth(hop))
    def _():
        rest[-1][...] = came_ref[...]

    @pl.when(jnp.logical_not(at_depth(hop)))
    def _():
        rest[-1][...] = mine_ref[...]

    if shared:
        write_send(rest[0], rest[2], rest[1])


def take(after, hop, mine, came, later=None):
    extra = [] if later is None else [later]
    out = pl.pallas_call(
        functools.partial(take_kernel, hop, later is not None),
        out_shape=[bf16(*a.shape) for a in extra + [mine]],
        in_specs=[VMEM, VMEM, ANY] + [VMEM] * len(extra),
        out_specs=[VMEM] * (1 + len(extra)),
        compiler_params=pltpu.CompilerParams(vmem_limit_bytes=8 * MIB),
    )(mine, came, after, *extra)
    return out[-1], (out[0] if extra else None)


def project_kernel(parts, after_ref, *rest):
    factors = jnp.concatenate([ref[...] for ref in rest[parts:-1]], axis=0)
    projected, first = 0.0, 0
    for ref in rest[:parts]:
        width = ref.shape[1]
        projected += lax.dot_general(
            factors[:, first : first + width], ref[...], NT, preferred_element_type=jnp.float32
        )
        first += width
    rest[-1][...] = projected.astype(rest[-1].dtype)


def project(after, factors, tokens, dtype):
    rows = sum(chunk.shape[0] for chunk in factors)
    return pl.pallas_call(
        functools.partial(project_kernel, len(tokens)),
        out_shape=jax.ShapeDtypeStruct((rows, tokens[0].shape[0]), dtype),
        in_specs=[ANY] + [VMEM] * (len(tokens) + len(factors)),
        out_specs=VMEM,
        compiler_params=pltpu.CompilerParams(vmem_limit_bytes=16 * MIB),
    )(after, *tokens, *factors)


def score_kernel(count, counts_ref, *refs):
    out_ref = refs[-1]
    own = jnp.concatenate([ref[...] for ref in refs[:count]], axis=0)
    other = jnp.concatenate([ref[...] for ref in refs[count : 2 * count]], axis=0)
    product = own * other.astype(jnp.float32)
    queries, tokens = product.shape[0] // RANK, product.shape[1]
    scores = jnp.sum(product.reshape(queries, RANK, tokens), axis=1) * RANK ** (-0.5)
    out_ref[...] = jnp.zeros(out_ref.shape, jnp.float32)
    out_ref[:, :tokens] = scores
    docs = counts_ref.shape[1]
    row = lax.broadcasted_iota(jnp.int32, (docs, 1), 0)
    column = lax.broadcasted_iota(jnp.int32, (1, docs), 1)
    starts, ends = jnp.zeros((docs, 1), jnp.int32), jnp.zeros((docs, 1), jnp.int32)
    counts = jnp.ones((1, docs), jnp.int32)
    end = jnp.int32(0)
    for k in range(docs):
        start, end = end, end + counts_ref[0, k]
        starts, ends = jnp.where(row == k, start, starts), jnp.where(row == k, end, ends)
        counts = jnp.where(column == k, end - start, counts)
    position = lax.broadcasted_iota(jnp.int32, (docs, tokens), 1)
    member = ((position >= starts) & (position < ends)).astype(jnp.float32)
    pooled = lax.dot_general(
        scores, member, NT, precision=lax.Precision.HIGHEST, preferred_element_type=jnp.float32
    )
    pooled = pooled / jnp.sqrt(counts.astype(jnp.float32))
    out_ref[:, tokens : tokens + pooled.shape[1]] = pooled


def score(counts, own, other):
    rows = sum(piece.shape[0] for piece in own)
    width = (own[0].shape[1] + counts.shape[1] + LANES - 1) // LANES * LANES
    return pl.pallas_call(
        functools.partial(score_kernel, len(own)),
        out_shape=jax.ShapeDtypeStruct((rows // RANK, width), jnp.float32),
        in_specs=[pl.BlockSpec(memory_space=pltpu.SMEM)] + [VMEM] * (2 * len(own)),
        out_specs=VMEM,
        compiler_params=pltpu.CompilerParams(vmem_limit_bytes=16 * MIB),
    )(counts, *own, *other)


def chunk_rows(spread):
    return spread // 8 if spread % 128 == 0 else RANK


def is_power(number):
    return number & (number - 1) == 0


def per_device(
    acts,
    grads,
    basis_in,
    output_eigen_basis,
    query_in,
    query_out,
    doc_counts,
    pair_query,
    pair_device,
    pair_doc,
):
    n = lax.axis_size("dp")
    layers = lax.axis_size("layer")
    z = lax.axis_index("dp")
    spread = query_in.shape[2]
    queries = spread // RANK
    half = n // 2
    rows = chunk_rows(spread)
    chunks = spread // rows

    first, send, basis, turned = first_pull(
        basis_in[0], output_eigen_basis[0], query_in[0], query_out[0], rows
    )
    own = [first] + list(pull(first, turned, basis, rows))
    tokens, theirs = deal(own[-1], acts[0], grads[0])
    swap = [(0, 1), (1, 0)]

    stages = [("in", hop) for hop in range(half - 1)] + [("mid", 0)]
    stages += [("out", hop) for hop in range(half - 2, -1, -1)]
    last = len(stages) - 1

    def transfer(kinds, hop, value):
        pairs = []
        if "in" in kinds:
            pairs += [(hop, hop + 1), (n - 1 - hop, n - 2 - hop)]
        if "mid" in kinds:
            pairs += [(half - 1, half), (half, half - 1)]
        if "out" in kinds:
            pairs += [(hop + 1, hop), (n - 2 - hop, n - 1 - hop)]
        return lax.ppermute(value, "dp", pairs)

    short = n == 4
    def on_cores(core, value, pairs):
        pairs = [(a * layers + i, b * layers + i) for a, b in pairs for i in range(core, layers, 2)]
        return lax.ppermute(value, ("dp", "layer"), pairs)

    part, came = list(own), [None] * chunks
    ahead = min(2, chunks)
    early = came[0] = transfer(("in", "out") if short else ("in",), 0, send)
    for c in range(1, ahead):
        came[c] = transfer(("in",), 0, part[c])
    others = [lax.ppermute(piece, "parts", swap) for piece in theirs]
    after = own[0]
    waiting, mine, back = [], [], []

    def project_waiting(after):
        factors = [factor for _, factor in sorted(waiting, key=lambda entry: entry[0])]
        away = project(after, factors, others, jnp.bfloat16)
        back.append(lax.ppermute(away, "parts", swap))
        mine.append(project(away, factors, [tokens], jnp.float32))
        waiting.clear()
        return mine[-1]

    swapped = set()
    turns = chunks + last - short
    for turn in range(turns):
        steps = [(s, turn - s) for s in range(last) if 0 <= turn - s < chunks]
        due = [c for c in range(chunks) if c + last + (c in swapped) == turn]
        for s, c in steps + [(last, c) for c in due]:
            kind, hop = stages[s]
            if short and c == chunks - 1:
                if s == 0:
                    after = part[c] = pair(after, own[c], came[c], early)
                    came[c] = [
                        on_cores(0, part[c], [(i, i ^ 2) for i in range(n)]),
                        on_cores(1, part[c], [(1, 2), (2, 1)]),
                    ]
                elif s == 1:
                    after = part[c] = join(after, part[c], *came[c])
                    came[c] = on_cores(1, part[c], [(1, 0), (2, 3)])
                continue
            later = turn + ahead if turn + ahead < chunks else None
            if turn >= last - 1:
                use = later if s == last - 1 else None
            else:
                use = later if s == 0 else None
            shared = use is not None and turn >= last - 1
            chunk = None if use is None else own[use]
            if kind == "out":
                part[c], send = take(after, hop, part[c], came[c], chunk)
            else:
                part[c], send = total(after, part[c], came[c], chunk, shared)
            after = part[c]
            if shared:
                came[c] = came[use] = transfer(("in", "out"), 0, send)
                swapped.add(c)
                continue
            if use is not None:
                came[use] = transfer(stages[0][:1], stages[0][1], send)
            if s < last:
                came[c] = transfer(stages[s + 1][:1], stages[s + 1][1], part[c])
            else:
                waiting.append((c, part[c]))
        if short and turn == turns - 1:
            c = chunks - 1
            after = part[c] = late(after, part[c], came[c])
            waiting.append((c, part[c]))
        if turn >= turns - 2 and waiting:
            after = project_waiting(after)

    scores = score(doc_counts, mine, back)
    if not is_power(layers):
        scores = lax.psum(scores, "layer")
    else:
        for step in [1 << k for k in range(layers.bit_length() - 1)]:
            scores = scores + lax.ppermute(scores, "layer", [(i, i ^ step) for i in range(layers)])
    tokens_here, docs = acts.shape[1], doc_counts.shape[1]
    token_scores, pooled = scores[:, :tokens_here], scores[:, tokens_here : tokens_here + docs]

    cells = queries * docs
    flat = pooled.reshape(1, cells)
    target = pair_device[:, 0]
    cell = pair_query * docs + pair_doc
    if n <= 8 and is_power(n):
        table = jnp.concatenate(
            [flat] + [lax.ppermute(flat, "dp", [(i, i ^ k ^ (k >> 1)) for i in range(n)]) for k in range(1, n)], axis=1
        )
        away = z ^ target
        column = (away ^ (away >> 1) ^ (away >> 2)) * cells + cell
    else:
        table = lax.all_gather(flat, "dp", axis=1, tiled=True)
        column = target * cells + cell
    hit = column[:, None] == jnp.arange(n * cells, dtype=jnp.int32)[None, :]
    pair_scores = jnp.sum(jnp.where(hit, table, 0.0), axis=1)
    return (token_scores, pair_scores)


def solution(mesh):
    in_specs = (
        P("layer", ("parts", "dp"), None),
        P("layer", ("parts", "dp"), None),
        P("layer", None, "dp"),
        P("layer", None, "dp"),
        P("layer", "dp", None),
        P("layer", "dp", None),
        P(("parts", "dp"), None),
        P(("parts", "dp")),
        P(("parts", "dp"), None),
        P(("parts", "dp")),
    )
    out_specs = (P(None, ("parts", "dp")), P(("parts", "dp")))
    return jax.shard_map(
        per_device, mesh=mesh, in_specs=in_specs, out_specs=out_specs, check_vma=False
    )
```

```python
import functools

import jax
import jax.numpy as jnp
from jax import lax
from jax.experimental import pallas as pl
from jax.experimental.pallas import tpu as pltpu
from jax.sharding import PartitionSpec as P

RANK = 32
NT = (((1,), (1,)), ((), ()))


VMEM = pl.BlockSpec(memory_space=pltpu.VMEM)
HBM = pl.BlockSpec(memory_space=pltpu.HBM)
ANY = pl.BlockSpec(memory_space=pl.ANY)
MIB = 1024 * 1024
LANES = 128


def in_hbm(*arrays):
    return [pltpu.with_memory_space_constraint(array, pltpu.HBM) for array in arrays]


def bf16(*shape):
    return jax.ShapeDtypeStruct(shape, jnp.bfloat16)


def at_depth(hop):
    z = lax.axis_index("dp")
    return jnp.minimum(z, lax.axis_size("dp") - 1 - z) == hop


def first_pull_kernel(
    basis_in_ref, basis_out_ref, query_in_ref, query_out_ref, out_ref, send_ref, basis_ref, query_ref, turned_ref, sems
):
    rows = out_ref.shape[0]
    features = basis_ref.shape[0]
    block = 512 if features % 512 == 0 else features
    spans = [pl.ds(first, block) for first in range(0, features, block)]

    def copies(from_basis, from_query):
        return [pltpu.make_async_copy(from_query, query_ref, sems.at[0])] + [
            pltpu.make_async_copy(from_basis.at[span], basis_ref.at[span], sems.at[1 + i])
            for i, span in enumerate(spans)
        ]

    side = lax.axis_index("parts")

    @pl.when(side == 0)
    def _():
        for copy in copies(basis_in_ref, query_in_ref):
            copy.start()

    @pl.when(side != 0)
    def _():
        for copy in copies(basis_out_ref, query_out_ref):
            copy.start()

    landed = copies(basis_in_ref, query_in_ref)
    landed[0].wait()
    turned_ref[...] = query_ref[...].T
    first = pl.multiple_of(jnp.where(at_depth(0), 0, turned_ref.shape[0] - rows), rows)
    factors = jnp.concatenate([turned_ref[:rows], turned_ref[pl.ds(first, rows)]], axis=0)
    for copy, span in zip(landed[1:], spans):
        copy.wait()
        pulled = lax.dot_general(factors, basis_ref[span], NT, preferred_element_type=jnp.float32)
        pulled = pulled.astype(jnp.bfloat16)
        out_ref[:, span] = pulled[:rows]
        send_ref[:, span] = pulled[rows:]


def first_pull(basis_in, basis_out, query_in, query_out, rows):
    features, depth = basis_in.shape
    spread = query_in.shape[1]
    blocks = features // 512 if features % 512 == 0 else 1
    out, send, basis, _, turned = pl.pallas_call(
        first_pull_kernel,
        out_shape=[bf16(rows, features)] * 2 + [bf16(features, depth), bf16(depth, spread), bf16(spread, depth)],
        in_specs=[HBM] * 4,
        out_specs=[VMEM] * 5,
        scratch_shapes=[pltpu.SemaphoreType.DMA((1 + blocks,))],
        compiler_params=pltpu.CompilerParams(vmem_limit_bytes=16 * MIB),
    )(*in_hbm(basis_in, basis_out, query_in, query_out))
    return out, send, basis, turned


def pull_kernel(turned_ref, basis_ref, after_ref, *outs):
    rows, features = outs[0].shape
    block = 512 if features % 512 == 0 else features
    for i in range(features // block):
        pulled = lax.dot_general(
            turned_ref[rows:], basis_ref[i * block : (i + 1) * block], NT, preferred_element_type=jnp.float32
        ).astype(jnp.bfloat16)
        for c, out in enumerate(outs):
            out[:, i * block : (i + 1) * block] = pulled[c * rows : (c + 1) * rows]


def pull(after, turned, basis, rows):
    chunks = turned.shape[0] // rows - 1
    return pl.pallas_call(
        pull_kernel,
        out_shape=[bf16(rows, basis.shape[0])] * chunks,
        in_specs=[VMEM, VMEM, ANY],
        out_specs=[VMEM] * chunks,
        compiler_params=pltpu.CompilerParams(vmem_limit_bytes=16 * MIB),
    )(turned, basis, after)


def deal_kernel(acts_ref, grads_ref, after_ref, *rest):
    outs, sems = rest[:-1], rest[-1]

    def copies(mine, theirs):
        pairs, first = [(mine, outs[0])], 0
        for out in outs[1:]:
            pairs.append((theirs.at[:, pl.ds(first, out.shape[1])], out))
            first += out.shape[1]
        return [pltpu.make_async_copy(source, target, sems.at[i]) for i, (source, target) in enumerate(pairs)]

    side = lax.axis_index("parts")

    @pl.when(side == 0)
    def _():
        for copy in copies(acts_ref, grads_ref):
            copy.start()

    @pl.when(side != 0)
    def _():
        for copy in copies(grads_ref, acts_ref):
            copy.start()

    for copy in copies(acts_ref, grads_ref):
        copy.wait()


def deal(after, acts, grads):
    tokens, features = acts.shape
    larger = features * 13 // 20
    widths = [larger, features - larger] if larger % LANES == 0 else [features]
    out = pl.pallas_call(
        deal_kernel,
        out_shape=[bf16(tokens, features)] + [bf16(tokens, width) for width in widths],
        in_specs=[HBM, HBM, ANY],
        out_specs=[VMEM] * (1 + len(widths)),
        scratch_shapes=[pltpu.SemaphoreType.DMA((1 + len(widths),))],
        compiler_params=pltpu.CompilerParams(vmem_limit_bytes=8 * MIB),
    )(*in_hbm(acts, grads), after)
    return out[0], out[1:]


def write_send(later_ref, value_ref, send_ref):
    @pl.when(at_depth(0))
    def _():
        send_ref[...] = later_ref[...]

    @pl.when(jnp.logical_not(at_depth(0)))
    def _():
        send_ref[...] = value_ref[...]


def pair_kernel(mine_ref, came_ref, early_ref, after_ref, out_ref):
    @pl.when(at_depth(0))
    def _():
        out_ref[...] = (mine_ref[...].astype(jnp.float32) + early_ref[...].astype(jnp.float32)).astype(jnp.bfloat16)

    @pl.when(jnp.logical_not(at_depth(0)))
    def _():
        out_ref[...] = (mine_ref[...].astype(jnp.float32) + came_ref[...].astype(jnp.float32)).astype(jnp.bfloat16)


def pair(after, mine, came, early):
    return pl.pallas_call(
        pair_kernel,
        out_shape=bf16(*mine.shape),
        in_specs=[VMEM, VMEM, VMEM, ANY],
        out_specs=VMEM,
        compiler_params=pltpu.CompilerParams(vmem_limit_bytes=8 * MIB),
    )(mine, came, early, after)


def late_kernel(mine_ref, came_ref, after_ref, out_ref):
    here = at_depth(0) & (lax.rem(lax.axis_index("layer"), 2) == 1)

    @pl.when(here)
    def _():
        out_ref[...] = came_ref[...]

    @pl.when(jnp.logical_not(here))
    def _():
        out_ref[...] = mine_ref[...]


def late(after, mine, came):
    return pl.pallas_call(
        late_kernel,
        out_shape=bf16(*mine.shape),
        in_specs=[VMEM, VMEM, ANY],
        out_specs=VMEM,
        compiler_params=pltpu.CompilerParams(vmem_limit_bytes=8 * MIB),
    )(mine, came, after)


def total_kernel(shared, mine_ref, came_ref, after_ref, *rest):
    mine = mine_ref[...].astype(jnp.float32) + came_ref[...].astype(jnp.float32)
    rest[-1][...] = mine.astype(jnp.bfloat16)
    if shared:
        write_send(rest[0], rest[2], rest[1])
    elif len(rest) == 3:
        rest[1][...] = rest[0][...]


def total(after, mine, came, later=None, shared=False):
    extra = [] if later is None else [later]
    out = pl.pallas_call(
        functools.partial(total_kernel, shared),
        out_shape=[bf16(*a.shape) for a in extra + [mine]],
        in_specs=[VMEM, VMEM, ANY] + [VMEM] * len(extra),
        out_specs=[VMEM] * (1 + len(extra)),
        compiler_params=pltpu.CompilerParams(vmem_limit_bytes=8 * MIB),
    )(mine, came, after, *extra)
    return out[-1], (out[0] if extra else None)


def take_kernel(hop, shared, mine_ref, came_ref, after_ref, *rest):
    @pl.when(at_depth(hop))
    def _():
        rest[-1][...] = came_ref[...]

    @pl.when(jnp.logical_not(at_depth(hop)))
    def _():
        rest[-1][...] = mine_ref[...]

    if shared:
        write_send(rest[0], rest[2], rest[1])


def take(after, hop, mine, came, later=None):
    extra = [] if later is None else [later]
    out = pl.pallas_call(
        functools.partial(take_kernel, hop, later is not None),
        out_shape=[bf16(*a.shape) for a in extra + [mine]],
        in_specs=[VMEM, VMEM, ANY] + [VMEM] * len(extra),
        out_specs=[VMEM] * (1 + len(extra)),
        compiler_params=pltpu.CompilerParams(vmem_limit_bytes=8 * MIB),
    )(mine, came, after, *extra)
    return out[-1], (out[0] if extra else None)


def project_kernel(parts, after_ref, *rest):
    factors = jnp.concatenate([ref[...] for ref in rest[parts:-1]], axis=0)
    projected, first = 0.0, 0
    for ref in rest[:parts]:
        width = ref.shape[1]
        projected += lax.dot_general(
            factors[:, first : first + width], ref[...], NT, preferred_element_type=jnp.float32
        )
        first += width
    rest[-1][...] = projected.astype(rest[-1].dtype)


def project(after, factors, tokens, dtype):
    rows = sum(chunk.shape[0] for chunk in factors)
    return pl.pallas_call(
        functools.partial(project_kernel, len(tokens)),
        out_shape=jax.ShapeDtypeStruct((rows, tokens[0].shape[0]), dtype),
        in_specs=[ANY] + [VMEM] * (len(tokens) + len(factors)),
        out_specs=VMEM,
        compiler_params=pltpu.CompilerParams(vmem_limit_bytes=16 * MIB),
    )(after, *tokens, *factors)


def score_kernel(count, counts_ref, *refs):
    out_ref = refs[-1]
    own = jnp.concatenate([ref[...] for ref in refs[:count]], axis=0)
    other = jnp.concatenate([ref[...] for ref in refs[count : 2 * count]], axis=0)
    product = own * other.astype(jnp.float32)
    queries, tokens = product.shape[0] // RANK, product.shape[1]
    scores = jnp.sum(product.reshape(queries, RANK, tokens), axis=1) * RANK ** (-0.5)
    out_ref[...] = jnp.zeros(out_ref.shape, jnp.float32)
    out_ref[:, :tokens] = scores
    docs = counts_ref.shape[1]
    row = lax.broadcasted_iota(jnp.int32, (docs, 1), 0)
    column = lax.broadcasted_iota(jnp.int32, (1, docs), 1)
    starts, ends = jnp.zeros((docs, 1), jnp.int32), jnp.zeros((docs, 1), jnp.int32)
    counts = jnp.ones((1, docs), jnp.int32)
    end = jnp.int32(0)
    for k in range(docs):
        start, end = end, end + counts_ref[0, k]
        starts, ends = jnp.where(row == k, start, starts), jnp.where(row == k, end, ends)
        counts = jnp.where(column == k, end - start, counts)
    position = lax.broadcasted_iota(jnp.int32, (docs, tokens), 1)
    member = ((position >= starts) & (position < ends)).astype(jnp.float32)
    pooled = lax.dot_general(
        scores, member, NT, precision=lax.Precision.HIGHEST, preferred_element_type=jnp.float32
    )
    pooled = pooled / jnp.sqrt(counts.astype(jnp.float32))
    out_ref[:, tokens : tokens + pooled.shape[1]] = pooled


def score(counts, own, other):
    rows = sum(piece.shape[0] for piece in own)
    width = (own[0].shape[1] + counts.shape[1] + LANES - 1) // LANES * LANES
    return pl.pallas_call(
        functools.partial(score_kernel, len(own)),
        out_shape=jax.ShapeDtypeStruct((rows // RANK, width), jnp.float32),
        in_specs=[pl.BlockSpec(memory_space=pltpu.SMEM)] + [VMEM] * (2 * len(own)),
        out_specs=VMEM,
        compiler_params=pltpu.CompilerParams(vmem_limit_bytes=16 * MIB),
    )(counts, *own, *other)


def chunk_rows(spread):
    return spread // 8 if spread % 128 == 0 else RANK


def is_power(number):
    return number & (number - 1) == 0


def per_device(
    acts,
    grads,
    basis_in,
    output_eigen_basis,
    query_in,
    query_out,
    doc_counts,
    pair_query,
    pair_device,
    pair_doc,
):
    n = lax.axis_size("dp")
    layers = lax.axis_size("layer")
    z = lax.axis_index("dp")
    spread = query_in.shape[2]
    queries = spread // RANK
    half = n // 2
    rows = chunk_rows(spread)
    chunks = spread // rows

    first, send, basis, turned = first_pull(
        basis_in[0], output_eigen_basis[0], query_in[0], query_out[0], rows
    )
    own = [first] + list(pull(first, turned, basis, rows))
    tokens, theirs = deal(own[-1], acts[0], grads[0])
    swap = [(0, 1), (1, 0)]

    stages = [("in", hop) for hop in range(half - 1)] + [("mid", 0)]
    stages += [("out", hop) for hop in range(half - 2, -1, -1)]
    last = len(stages) - 1

    def transfer(kinds, hop, value):
        pairs = []
        if "in" in kinds:
            pairs += [(hop, hop + 1), (n - 1 - hop, n - 2 - hop)]
        if "mid" in kinds:
            pairs += [(half - 1, half), (half, half - 1)]
        if "out" in kinds:
            pairs += [(hop + 1, hop), (n - 2 - hop, n - 1 - hop)]
        return lax.ppermute(value, "dp", pairs)

    short = n == 4
    def on_cores(value, *pairs):
        pairs = [(a * layers + i, b * layers + i) for i in range(layers) for a, b in pairs[i % 2]]
        return lax.ppermute(value, ("dp", "layer"), pairs)

    part, came = list(own), [None] * chunks
    ahead = min(2, chunks)
    early = came[0] = transfer(("in", "out") if short else ("in",), 0, send)
    for c in range(1, ahead):
        came[c] = transfer(("in",), 0, part[c])
    others = [lax.ppermute(piece, "parts", swap) for piece in theirs]
    after = own[0]
    waiting, mine, back = [], [], []

    def project_waiting(after):
        factors = [factor for _, factor in sorted(waiting, key=lambda entry: entry[0])]
        away = project(after, factors, others, jnp.bfloat16)
        back.append(lax.ppermute(away, "parts", swap))
        mine.append(project(away, factors, [tokens], jnp.float32))
        waiting.clear()
        return mine[-1]

    swapped = set()
    turns = chunks + last - short
    for turn in range(turns):
        steps = [(s, turn - s) for s in range(last) if 0 <= turn - s < chunks]
        due = [c for c in range(chunks) if c + last + (c in swapped) == turn]
        for s, c in steps + [(last, c) for c in due]:
            kind, hop = stages[s]
            if short and c == chunks - 1:
                if s == 0:
                    after = part[c] = pair(after, own[c], came[c], early)
                    came[c] = on_cores(part[c], [(i, i ^ 2) for i in range(n)], [(1, 2), (2, 1)])
                elif s == 1:
                    part[c], _ = total(after, part[c], came[c])
                    after = part[c]
                    came[c] = on_cores(part[c], [], [(1, 0), (2, 3)])
                continue
            later = turn + ahead if turn + ahead < chunks else None
            if turn >= last - 1:
                use = later if s == last - 1 else None
            else:
                use = later if s == 0 else None
            shared = use is not None and turn >= last - 1
            chunk = None if use is None else own[use]
            if kind == "out":
                part[c], send = take(after, hop, part[c], came[c], chunk)
            else:
                part[c], send = total(after, part[c], came[c], chunk, shared)
            after = part[c]
            if shared:
                came[c] = came[use] = transfer(("in", "out"), 0, send)
                swapped.add(c)
                continue
            if use is not None:
                came[use] = transfer(stages[0][:1], stages[0][1], send)
            if s < last:
                came[c] = transfer(stages[s + 1][:1], stages[s + 1][1], part[c])
            else:
                waiting.append((c, part[c]))
        if short and turn == turns - 1:
            c = chunks - 1
            after = part[c] = late(after, part[c], came[c])
            waiting.append((c, part[c]))
        if turn >= turns - 2 and waiting:
            after = project_waiting(after)

    scores = score(doc_counts, mine, back)
    if not is_power(layers):
        scores = lax.psum(scores, "layer")
    else:
        for step in [1 << k for k in range(layers.bit_length() - 1)]:
            scores = scores + lax.ppermute(scores, "layer", [(i, i ^ step) for i in range(layers)])
    tokens_here, docs = acts.shape[1], doc_counts.shape[1]
    token_scores, pooled = scores[:, :tokens_here], scores[:, tokens_here : tokens_here + docs]

    cells = queries * docs
    flat = pooled.reshape(1, cells)
    target = pair_device[:, 0]
    cell = pair_query * docs + pair_doc
    if n <= 8 and is_power(n):
        table = jnp.concatenate(
            [flat] + [lax.ppermute(flat, "dp", [(i, i ^ k ^ (k >> 1)) for i in range(n)]) for k in range(1, n)], axis=1
        )
        away = z ^ target
        column = (away ^ (away >> 1) ^ (away >> 2)) * cells + cell
    else:
        table = lax.all_gather(flat, "dp", axis=1, tiled=True)
        column = target * cells + cell
    hit = column[:, None] == jnp.arange(n * cells, dtype=jnp.int32)[None, :]
    pair_scores = jnp.sum(jnp.where(hit, table, 0.0), axis=1)
    return (token_scores, pair_scores)


def solution(mesh):
    in_specs = (
        P("layer", ("parts", "dp"), None),
        P("layer", ("parts", "dp"), None),
        P("layer", None, "dp"),
        P("layer", None, "dp"),
        P("layer", "dp", None),
        P("layer", "dp", None),
        P(("parts", "dp"), None),
        P(("parts", "dp")),
        P(("parts", "dp"), None),
        P(("parts", "dp")),
    )
    out_specs = (P(None, ("parts", "dp")), P(("parts", "dp")))
    return jax.shard_map(
        per_device, mesh=mesh, in_specs=in_specs, out_specs=out_specs, check_vma=False
    )
```

```python
import functools

import jax
import jax.numpy as jnp
from jax import lax
from jax.experimental import pallas as pl
from jax.experimental.pallas import tpu as pltpu
from jax.sharding import PartitionSpec as P

RANK = 32
NT = (((1,), (1,)), ((), ()))


VMEM = pl.BlockSpec(memory_space=pltpu.VMEM)
HBM = pl.BlockSpec(memory_space=pltpu.HBM)
ANY = pl.BlockSpec(memory_space=pl.ANY)
MIB = 1024 * 1024
LANES = 128


def in_hbm(*arrays):
    return [pltpu.with_memory_space_constraint(array, pltpu.HBM) for array in arrays]


def bf16(*shape):
    return jax.ShapeDtypeStruct(shape, jnp.bfloat16)


def at_depth(hop):
    z = lax.axis_index("dp")
    return jnp.minimum(z, lax.axis_size("dp") - 1 - z) == hop


def first_pull_kernel(
    basis_in_ref, basis_out_ref, query_in_ref, query_out_ref, out_ref, send_ref, basis_ref, query_ref, turned_ref, sems
):
    rows = out_ref.shape[0]
    features = basis_ref.shape[0]
    block = 512 if features % 512 == 0 else features
    spans = [pl.ds(first, block) for first in range(0, features, block)]

    def copies(from_basis, from_query):
        return [pltpu.make_async_copy(from_query, query_ref, sems.at[0])] + [
            pltpu.make_async_copy(from_basis.at[span], basis_ref.at[span], sems.at[1 + i])
            for i, span in enumerate(spans)
        ]

    side = lax.axis_index("parts")

    @pl.when(side == 0)
    def _():
        for copy in copies(basis_in_ref, query_in_ref):
            copy.start()

    @pl.when(side != 0)
    def _():
        for copy in copies(basis_out_ref, query_out_ref):
            copy.start()

    landed = copies(basis_in_ref, query_in_ref)
    landed[0].wait()
    turned_ref[...] = query_ref[...].T
    first = pl.multiple_of(jnp.where(at_depth(0), 0, turned_ref.shape[0] - rows), rows)
    factors = jnp.concatenate([turned_ref[:rows], turned_ref[pl.ds(first, rows)]], axis=0)
    for copy, span in zip(landed[1:], spans):
        copy.wait()
        pulled = lax.dot_general(factors, basis_ref[span], NT, preferred_element_type=jnp.float32)
        pulled = pulled.astype(jnp.bfloat16)
        out_ref[:, span] = pulled[:rows]
        send_ref[:, span] = pulled[rows:]


def first_pull(basis_in, basis_out, query_in, query_out, rows):
    features, depth = basis_in.shape
    spread = query_in.shape[1]
    blocks = features // 512 if features % 512 == 0 else 1
    out, send, basis, _, turned = pl.pallas_call(
        first_pull_kernel,
        out_shape=[bf16(rows, features)] * 2 + [bf16(features, depth), bf16(depth, spread), bf16(spread, depth)],
        in_specs=[HBM] * 4,
        out_specs=[VMEM] * 5,
        scratch_shapes=[pltpu.SemaphoreType.DMA((1 + blocks,))],
        compiler_params=pltpu.CompilerParams(vmem_limit_bytes=16 * MIB),
    )(*in_hbm(basis_in, basis_out, query_in, query_out))
    return out, send, basis, turned


def pull_kernel(turned_ref, basis_ref, after_ref, *outs):
    rows, features = outs[0].shape
    block = 512 if features % 512 == 0 else features
    for i in range(features // block):
        pulled = lax.dot_general(
            turned_ref[rows:], basis_ref[i * block : (i + 1) * block], NT, preferred_element_type=jnp.float32
        ).astype(jnp.bfloat16)
        for c, out in enumerate(outs):
            out[:, i * block : (i + 1) * block] = pulled[c * rows : (c + 1) * rows]


def pull(after, turned, basis, rows):
    chunks = turned.shape[0] // rows - 1
    return pl.pallas_call(
        pull_kernel,
        out_shape=[bf16(rows, basis.shape[0])] * chunks,
        in_specs=[VMEM, VMEM, ANY],
        out_specs=[VMEM] * chunks,
        compiler_params=pltpu.CompilerParams(vmem_limit_bytes=16 * MIB),
    )(turned, basis, after)


def deal_kernel(acts_ref, grads_ref, after_ref, *rest):
    outs, sems = rest[:-1], rest[-1]

    def copies(mine, theirs):
        pairs, first = [(mine, outs[0])], 0
        for out in outs[1:]:
            pairs.append((theirs.at[:, pl.ds(first, out.shape[1])], out))
            first += out.shape[1]
        return [pltpu.make_async_copy(source, target, sems.at[i]) for i, (source, target) in enumerate(pairs)]

    side = lax.axis_index("parts")

    @pl.when(side == 0)
    def _():
        for copy in copies(acts_ref, grads_ref):
            copy.start()

    @pl.when(side != 0)
    def _():
        for copy in copies(grads_ref, acts_ref):
            copy.start()

    for copy in copies(acts_ref, grads_ref):
        copy.wait()


def deal(after, acts, grads):
    tokens, features = acts.shape
    larger = features * 13 // 20
    widths = [larger, features - larger] if larger % LANES == 0 else [features]
    out = pl.pallas_call(
        deal_kernel,
        out_shape=[bf16(tokens, features)] + [bf16(tokens, width) for width in widths],
        in_specs=[HBM, HBM, ANY],
        out_specs=[VMEM] * (1 + len(widths)),
        scratch_shapes=[pltpu.SemaphoreType.DMA((1 + len(widths),))],
        compiler_params=pltpu.CompilerParams(vmem_limit_bytes=8 * MIB),
    )(*in_hbm(acts, grads), after)
    return out[0], out[1:]


def write_send(later_ref, value_ref, send_ref):
    @pl.when(at_depth(0))
    def _():
        send_ref[...] = later_ref[...]

    @pl.when(jnp.logical_not(at_depth(0)))
    def _():
        send_ref[...] = value_ref[...]


def pair_kernel(mine_ref, came_ref, early_ref, after_ref, out_ref):
    @pl.when(at_depth(0))
    def _():
        out_ref[...] = (mine_ref[...].astype(jnp.float32) + early_ref[...].astype(jnp.float32)).astype(jnp.bfloat16)

    @pl.when(jnp.logical_not(at_depth(0)))
    def _():
        out_ref[...] = (mine_ref[...].astype(jnp.float32) + came_ref[...].astype(jnp.float32)).astype(jnp.bfloat16)


def pair(after, mine, came, early):
    return pl.pallas_call(
        pair_kernel,
        out_shape=bf16(*mine.shape),
        in_specs=[VMEM, VMEM, VMEM, ANY],
        out_specs=VMEM,
        compiler_params=pltpu.CompilerParams(vmem_limit_bytes=8 * MIB),
    )(mine, came, early, after)


def total_kernel(shared, mine_ref, came_ref, after_ref, *rest):
    mine = mine_ref[...].astype(jnp.float32) + came_ref[...].astype(jnp.float32)
    rest[-1][...] = mine.astype(jnp.bfloat16)
    if shared:
        write_send(rest[0], rest[2], rest[1])
    elif len(rest) == 3:
        rest[1][...] = rest[0][...]


def total(after, mine, came, later=None, shared=False):
    extra = [] if later is None else [later]
    out = pl.pallas_call(
        functools.partial(total_kernel, shared),
        out_shape=[bf16(*a.shape) for a in extra + [mine]],
        in_specs=[VMEM, VMEM, ANY] + [VMEM] * len(extra),
        out_specs=[VMEM] * (1 + len(extra)),
        compiler_params=pltpu.CompilerParams(vmem_limit_bytes=8 * MIB),
    )(mine, came, after, *extra)
    return out[-1], (out[0] if extra else None)


def take_kernel(hop, shared, mine_ref, came_ref, after_ref, *rest):
    @pl.when(at_depth(hop))
    def _():
        rest[-1][...] = came_ref[...]

    @pl.when(jnp.logical_not(at_depth(hop)))
    def _():
        rest[-1][...] = mine_ref[...]

    if shared:
        write_send(rest[0], rest[2], rest[1])


def take(after, hop, mine, came, later=None):
    extra = [] if later is None else [later]
    out = pl.pallas_call(
        functools.partial(take_kernel, hop, later is not None),
        out_shape=[bf16(*a.shape) for a in extra + [mine]],
        in_specs=[VMEM, VMEM, ANY] + [VMEM] * len(extra),
        out_specs=[VMEM] * (1 + len(extra)),
        compiler_params=pltpu.CompilerParams(vmem_limit_bytes=8 * MIB),
    )(mine, came, after, *extra)
    return out[-1], (out[0] if extra else None)


def project_kernel(parts, after_ref, *rest):
    factors = jnp.concatenate([ref[...] for ref in rest[parts:-1]], axis=0)
    projected, first = 0.0, 0
    for ref in rest[:parts]:
        width = ref.shape[1]
        projected += lax.dot_general(
            factors[:, first : first + width], ref[...], NT, preferred_element_type=jnp.float32
        )
        first += width
    rest[-1][...] = projected.astype(rest[-1].dtype)


def project(after, factors, tokens, dtype):
    rows = sum(chunk.shape[0] for chunk in factors)
    return pl.pallas_call(
        functools.partial(project_kernel, len(tokens)),
        out_shape=jax.ShapeDtypeStruct((rows, tokens[0].shape[0]), dtype),
        in_specs=[ANY] + [VMEM] * (len(tokens) + len(factors)),
        out_specs=VMEM,
        compiler_params=pltpu.CompilerParams(vmem_limit_bytes=16 * MIB),
    )(after, *tokens, *factors)


def score_kernel(count, counts_ref, *refs):
    out_ref = refs[-1]
    own = jnp.concatenate([ref[...] for ref in refs[:count]], axis=0)
    other = jnp.concatenate([ref[...] for ref in refs[count : 2 * count]], axis=0)
    product = own * other.astype(jnp.float32)
    queries, tokens = product.shape[0] // RANK, product.shape[1]
    scores = jnp.sum(product.reshape(queries, RANK, tokens), axis=1) * RANK ** (-0.5)
    out_ref[...] = jnp.zeros(out_ref.shape, jnp.float32)
    out_ref[:, :tokens] = scores
    docs = counts_ref.shape[1]
    row = lax.broadcasted_iota(jnp.int32, (docs, 1), 0)
    column = lax.broadcasted_iota(jnp.int32, (1, docs), 1)
    starts, ends = jnp.zeros((docs, 1), jnp.int32), jnp.zeros((docs, 1), jnp.int32)
    counts = jnp.ones((1, docs), jnp.int32)
    end = jnp.int32(0)
    for k in range(docs):
        start, end = end, end + counts_ref[0, k]
        starts, ends = jnp.where(row == k, start, starts), jnp.where(row == k, end, ends)
        counts = jnp.where(column == k, end - start, counts)
    position = lax.broadcasted_iota(jnp.int32, (docs, tokens), 1)
    member = ((position >= starts) & (position < ends)).astype(jnp.float32)
    pooled = lax.dot_general(
        scores, member, NT, precision=lax.Precision.HIGHEST, preferred_element_type=jnp.float32
    )
    pooled = pooled / jnp.sqrt(counts.astype(jnp.float32))
    out_ref[:, tokens : tokens + pooled.shape[1]] = pooled


def score(counts, own, other):
    rows = sum(piece.shape[0] for piece in own)
    width = (own[0].shape[1] + counts.shape[1] + LANES - 1) // LANES * LANES
    return pl.pallas_call(
        functools.partial(score_kernel, len(own)),
        out_shape=jax.ShapeDtypeStruct((rows // RANK, width), jnp.float32),
        in_specs=[pl.BlockSpec(memory_space=pltpu.SMEM)] + [VMEM] * (2 * len(own)),
        out_specs=VMEM,
        compiler_params=pltpu.CompilerParams(vmem_limit_bytes=16 * MIB),
    )(counts, *own, *other)


def chunk_rows(spread):
    return spread // 8 if spread % 128 == 0 else RANK


def is_power(number):
    return number & (number - 1) == 0


def per_device(
    acts,
    grads,
    basis_in,
    output_eigen_basis,
    query_in,
    query_out,
    doc_counts,
    pair_query,
    pair_device,
    pair_doc,
):
    n = lax.axis_size("dp")
    layers = lax.axis_size("layer")
    z = lax.axis_index("dp")
    spread = query_in.shape[2]
    queries = spread // RANK
    half = n // 2
    rows = chunk_rows(spread)
    chunks = spread // rows

    first, send, basis, turned = first_pull(
        basis_in[0], output_eigen_basis[0], query_in[0], query_out[0], rows
    )
    own = [first] + list(pull(first, turned, basis, rows))
    tokens, theirs = deal(own[-1], acts[0], grads[0])
    swap = [(0, 1), (1, 0)]

    stages = [("in", hop) for hop in range(half - 1)] + [("mid", 0)]
    stages += [("out", hop) for hop in range(half - 2, -1, -1)]
    last = len(stages) - 1

    def transfer(kinds, hop, value):
        pairs = []
        if "in" in kinds:
            pairs += [(hop, hop + 1), (n - 1 - hop, n - 2 - hop)]
        if "mid" in kinds:
            pairs += [(half - 1, half), (half, half - 1)]
        if "out" in kinds:
            pairs += [(hop + 1, hop), (n - 2 - hop, n - 1 - hop)]
        return lax.ppermute(value, "dp", pairs)

    short = n == 4
    part, came = list(own), [None] * chunks
    ahead = min(2, chunks)
    early = came[0] = transfer(("in", "out") if short else ("in",), 0, send)
    for c in range(1, ahead):
        came[c] = transfer(("in",), 0, part[c])
    others = [lax.ppermute(piece, "parts", swap) for piece in theirs]
    after = own[0]
    waiting, mine, back = [], [], []

    def project_waiting(after):
        factors = [factor for _, factor in sorted(waiting, key=lambda entry: entry[0])]
        away = project(after, factors, others, jnp.bfloat16)
        back.append(lax.ppermute(away, "parts", swap))
        mine.append(project(away, factors, [tokens], jnp.float32))
        waiting.clear()
        return mine[-1]

    swapped = set()
    turns = chunks + last - short
    for turn in range(turns):
        steps = [(s, turn - s) for s in range(last) if 0 <= turn - s < chunks]
        due = [c for c in range(chunks) if c + last + (c in swapped) == turn]
        for s, c in steps + [(last, c) for c in due]:
            kind, hop = stages[s]
            if short and c == chunks - 1:
                if s == 0:
                    after = part[c] = pair(after, own[c], came[c], early)
                    came[c] = lax.ppermute(part[c], "dp", [(i, i ^ 2) for i in range(n)])
                elif s == 1:
                    part[c], _ = total(after, part[c], came[c])
                    after = part[c]
                    waiting.append((c, part[c]))
                continue
            later = turn + ahead if turn + ahead < chunks else None
            if turn >= last - 1:
                use = later if s == last - 1 else None
            else:
                use = later if s == 0 else None
            shared = use is not None and turn >= last - 1
            chunk = None if use is None else own[use]
            if kind == "out":
                part[c], send = take(after, hop, part[c], came[c], chunk)
            else:
                part[c], send = total(after, part[c], came[c], chunk, shared)
            after = part[c]
            if shared:
                came[c] = came[use] = transfer(("in", "out"), 0, send)
                swapped.add(c)
                continue
            if use is not None:
                came[use] = transfer(stages[0][:1], stages[0][1], send)
            if s < last:
                came[c] = transfer(stages[s + 1][:1], stages[s + 1][1], part[c])
            else:
                waiting.append((c, part[c]))
        if turn >= turns - 2 and waiting:
            after = project_waiting(after)

    scores = score(doc_counts, mine, back)
    if not is_power(layers):
        scores = lax.psum(scores, "layer")
    else:
        for step in [1 << k for k in range(layers.bit_length() - 1)]:
            pairs = [(i, i ^ step) for i in range(layers)]
            if step == 1:
                scores = scores + lax.ppermute(scores, "layer", pairs)
                continue
            scores = lax.reduce_precision(scores, 8, 7)
            scores = scores + lax.ppermute(scores.astype(jnp.bfloat16), "layer", pairs).astype(jnp.float32)
    tokens_here, docs = acts.shape[1], doc_counts.shape[1]
    token_scores, pooled = scores[:, :tokens_here], scores[:, tokens_here : tokens_here + docs]

    cells = queries * docs
    flat = pooled.reshape(1, cells)
    target = pair_device[:, 0]
    cell = pair_query * docs + pair_doc
    if n <= 8 and is_power(n):
        table = jnp.concatenate(
            [flat] + [lax.ppermute(flat, "dp", [(i, i ^ k ^ (k >> 1)) for i in range(n)]) for k in range(1, n)], axis=1
        )
        away = z ^ target
        column = (away ^ (away >> 1) ^ (away >> 2)) * cells + cell
    else:
        table = lax.all_gather(flat, "dp", axis=1, tiled=True)
        column = target * cells + cell
    hit = column[:, None] == jnp.arange(n * cells, dtype=jnp.int32)[None, :]
    pair_scores = jnp.sum(jnp.where(hit, table, 0.0), axis=1)
    return (token_scores, pair_scores)


def solution(mesh):
    in_specs = (
        P("layer", ("parts", "dp"), None),
        P("layer", ("parts", "dp"), None),
        P("layer", None, "dp"),
        P("layer", None, "dp"),
        P("layer", "dp", None),
        P("layer", "dp", None),
        P(("parts", "dp"), None),
        P(("parts", "dp")),
        P(("parts", "dp"), None),
        P(("parts", "dp")),
    )
    out_specs = (P(None, ("parts", "dp")), P(("parts", "dp")))
    return jax.shard_map(
        per_device, mesh=mesh, in_specs=in_specs, out_specs=out_specs, check_vma=False
    )
```
